32 devices in a mesh: batch: 4 (over z), own: 8 (over y, x, core).
Axes of the slice: x: 2, y: 2, z: 4, core: 2. Of those that a mesh axis runs over, the one named last changes fastest.
Arguments:
- memory: float32 [8192, 172], P('own'), may hold values from -1.5 to 1.5
- last_update: int32 [8192], P('own'), may hold values from 0 to 999
- src_local: int32 [32768], P(('batch', 'own')), may hold values from 0 to 1023
- edge_feat: bfloat16 [32768, 172], P(('batch', 'own')), may hold values from -6 to 6
- event_time: int32 [32768], P(('batch', 'own')), may hold values from 1000 to 1999
- nbr_owner: int32 [32768, 4], P(('batch', 'own')), may hold values from 0 to 7, all different within a row; in each aligned block of 1024 rows (0 to 1023, 1024 to 2047, ...) at most 1024 rows name the same one
- nbr_ids: int32 [32768, 4, 5], P(('batch', 'own')), may hold values from 0 to 1023
- nbr_mask: int32 [32768, 4, 5], P(('batch', 'own')), may hold values from 0 to 1, as said below
- event_mask: int32 [32768], P(('batch', 'own')), may hold values from 0 to 1
- dest_local: int32 [16384], P(('batch', 'own')), may hold values from 0 to 1023
- target: int32 [32768], P(('batch', 'own')), may hold values from 0 to 4095
- w_msg: float32 [444, 172], replicated, may hold values from -0.25 to 0.25
- w_gru: float32 [2, 172, 516], replicated, may hold values from -0.4375 to 0.4375
- w_square: float32 [4, 172, 172], replicated, may hold values from -0.4375 to 0.4375
- w_key_value: float32 [272, 344], replicated, may hold values from -1.75 to 1.75
- w_output: float32 [344, 172], replicated, may hold values from -0.3125 to 0.3125
- mom_msg: float32 [444, 172], replicated, may hold values from -0.75 to 0.75
- mom_gru: float32 [2, 172, 516], replicated, may hold values from -0.75 to 0.75
- mom_square: float32 [4, 172, 172], replicated, may hold values from -0.75 to 0.75
- mom_key_value: float32 [272, 344], replicated, may hold values from -0.75 to 0.75
- mom_output: float32 [344, 172], replicated, may hold values from -0.75 to 0.75
- avg_msg: float32 [444, 172], replicated, may hold values from -0.25 to 0.25
- avg_gru: float32 [2, 172, 516], replicated, may hold values from -0.4375 to 0.4375
- avg_square: float32 [4, 172, 172], replicated, may hold values from -0.4375 to 0.4375
- avg_key_value: float32 [272, 344], replicated, may hold values from -1.75 to 1.75
- avg_output: float32 [344, 172], replicated, may hold values from -0.3125 to 0.3125
Outputs:
- loss_sum: float32 [], replicated
- positives: float32 [], replicated
- new_last: int32 [8192], P('own')
- new_mom_msg: float32 [444, 172], replicated
- new_mom_gru: float32 [2, 172, 516], replicated
- new_mom_square: float32 [4, 172, 172], replicated
- new_mom_key_value: float32 [272, 344], replicated
- new_mom_output: float32 [344, 172], replicated
- new_w_msg: float32 [444, 172], replicated
- new_w_gru: float32 [2, 172, 516], replicated
- new_w_square: float32 [4, 172, 172], replicated
- new_w_key_value: float32 [272, 344], replicated
- new_w_output: float32 [344, 172], replicated
- new_avg_msg: float32 [444, 172], replicated
- new_avg_gru: float32 [2, 172, 516], replicated
- new_avg_square: float32 [4, 172, 172], replicated
- new_avg_key_value: float32 [272, 344], replicated
- new_avg_output: float32 [344, 172], replicated
The draws below stay inside these ranges and needn't reach their ends.
Inputs may be any that keep to these rules, and one draw needn't show every extreme that they name: `nbr_owner`: each row names 4 different owners; the rows of one device name one owner 1024 times at the most, and exactly 1024 times in some devices. `nbr_mask`: the first slot of the first owner of every event is live.
All inputs are finite; a program needn't handle non-finite values.
Results may differ from the reference program's by a relative error of at most 0.0018.
The reference program's roundings to bfloat16 on the way count: a program that leaves them out, or rounds other values in their place, can miss the bound.
Values may be sent and summed in bfloat16 or wider, within the bound.
A program may use at most 192 MiB of HBM per device.

```python
import math
from functools import partial
import jax
import jax.numpy as jnp
import numpy as np
from jax import lax

D = 172
EDGE = 172
TIME_DIM = 100
HEADS = 2
HEAD_DIM = 86
OWN_PICK = 4
SLOTS = 5
ROUTE_SLOTS = 20
EV_DEV = 1024
CAND_DEV = 512
NODES_DEV = 1024
OWNERS = 8
CAP = 1024
EVENTS = 32768
NODES = 8192
CANDS = 16384
N_BATCH = 4


def draw_event_mask(key, part):
    key = jax.random.fold_in(key, 11)
    device_row = jnp.arange(EVENTS, dtype=jnp.int32) // EV_DEV
    own_idx = device_row % OWNERS
    batch_idx = device_row // OWNERS
    own_span = max(OWNERS - 1, 1)
    batch_span = max(N_BATCH - 1, 1)
    threshold = 150 * (own_span + 2 * own_idx) * (batch_span + batch_idx) // (own_span * batch_span)
    return (jax.random.randint(key, (EVENTS,), 0, 1000) < threshold).astype(jnp.int32)


def draw_nbr_mask(key, part):
    key = jax.random.fold_in(key, 23)
    keep_bits = jax.random.randint(key, (EVENTS, OWN_PICK, SLOTS), 0, 4) > 0
    first_slot = (jnp.arange(OWN_PICK)[:, None] == 0) & (jnp.arange(SLOTS)[None, :] == 0)
    return (keep_bits | first_slot[None]).astype(jnp.int32)


def place_ends(entries, stream_key, smallest, largest):
    dims = entries.shape
    index_at = [jax.random.randint(jax.random.fold_in(stream_key, axis), (), 0, dims[axis]) for axis in range(len(dims))]
    entries = entries.at[tuple(index_at)].set(smallest)
    longest = dims.index(max(dims))
    index_at[longest] = (index_at[longest] + 1) % dims[longest]
    return entries.at[tuple(index_at)].set(largest)


def block_scale(stream_key, shape, split, least, top_value):
    factor_of = 1.0
    for dim, parts in split:
        draws = jax.random.uniform(jax.random.fold_in(jax.random.fold_in(stream_key, 6), dim), (parts,), jnp.float32, least / len(split), top_value / len(split))
        factor_of = factor_of * jnp.repeat(jnp.exp(draws), shape[dim] // parts).reshape((-1,) + (1,) * (len(shape) - 1 - dim))
    return factor_of


def assign_block(rng, own, number, rows, number_of, top, bound, skew):
    ranking = jax.random.permutation(rng, number_of)
    crowded, ordinary = shares(number_of, rows * top, bound, skew, True), shares(number_of, rows * top, bound, skew, False)
    places = jnp.arange(number_of)

    def named(lengths, rotation):
        used = int((lengths > 0).sum())
        fixed = max(1, used // 4)
        passed = fixed + (places - fixed + rotation * (used - fixed)) % max(1, number_of - fixed)
        return jnp.zeros((number_of,), jnp.int32).at[ranking[jnp.where(places < fixed, places, passed)]].set(jnp.asarray(lengths, jnp.int32))

    lengths = jnp.where(number % 4 == 0, named(crowded, number // 4), named(ordinary, number - number // 4 - 1))
    mixed = jax.random.permutation(jax.random.fold_in(own, 3), number_of)
    source_of, taker = mixed[0:number_of // 2 * 2:2], mixed[1:number_of // 2 * 2:2]
    room = jnp.minimum(lengths[source_of] - 1, bound - lengths[taker]) // 2
    room = jnp.where((source_of == ranking[0]) | (taker == ranking[0]) | (lengths[taker] == 0), 0, jnp.maximum(room, 0))
    passed = jax.random.randint(jax.random.fold_in(own, 4), (number_of // 2,), 0, 1 << 20) % (room + 1)
    lengths = lengths.at[source_of].add(-passed).at[taker].add(passed)
    labels = jnp.searchsorted(jnp.cumsum(lengths), jnp.arange(rows * top), side="right").astype(jnp.int32)
    grid = labels.reshape(top, rows).T
    grid = grid[jax.random.permutation(jax.random.fold_in(own, 1), rows)]
    rotation = jax.random.randint(jax.random.fold_in(own, 2), (rows, 1), 0, top)
    return jnp.take_along_axis(grid, (jnp.arange(top)[None, :] + rotation) % top, axis=1)


def shares(number_of, total, reach, slope, full):
    portions = [(1 << 20) // math.isqrt(rank ** slope) + 1 for rank in range(1, number_of + 1)]
    largest = reach if full else min(reach, max(-(-total // number_of), total * portions[0] // sum(portions)))
    least = 1 if total - largest >= number_of - 1 else 0
    counts, spare = [largest] + [least] * (number_of - 1), total - largest - least * (number_of - 1)
    while spare > 0:
        free = [i for i in range(1, number_of) if counts[i] < largest] or [i for i in range(1, number_of) if counts[i] < reach]
        mass, remaining = sum([portions[i] for i in free]), spare
        for i in free:
            extra = min(reach - counts[i], max(1, remaining * portions[i] // mass), spare)
            counts[i] = counts[i] + extra
            spare = spare - extra
    return np.array(counts)


def gaussian(stream_key, shape, deviation, limit, pieces=(), kind=jnp.bfloat16):
    drawn = jax.random.normal(stream_key, shape, jnp.float32) * deviation
    if len(pieces) > 0:
        drawn = block_scale(stream_key, shape, pieces, -0.22, 0.18) * drawn
    return jnp.clip(drawn, min=-limit, max=limit).astype(kind)


def setup_inputs(seed: int = 0) -> dict:
    key_of = jax.random.split(jax.random.key(seed), 27)
    memory = gaussian(key_of[0], (NODES, D), 0.25, 1.5, ((0, 8),), jnp.float32)
    last_update = place_ends(jax.random.randint(key_of[1], (NODES,), 0, 1000), jax.random.fold_in(key_of[1], 1), 0, 999).astype(jnp.int32)
    src_local = place_ends(jax.random.randint(key_of[2], (EVENTS,), 0, NODES_DEV), jax.random.fold_in(key_of[2], 1), 0, NODES_DEV - 1).astype(jnp.int32)
    edge_feat = gaussian(key_of[3], (EVENTS, EDGE), 1.0, 6.0, ((0, 32),))
    event_time = place_ends(jax.random.randint(key_of[4], (EVENTS,), 1000, 2000), jax.random.fold_in(key_of[4], 1), 1000, 1999).astype(jnp.int32)
    nbr_owner_keys = jax.random.split(jax.random.fold_in(key_of[5], 1), EVENTS // EV_DEV)
    nbr_owner_turns = jax.random.permutation(jax.random.fold_in(key_of[5], 3), EVENTS // EV_DEV)
    nbr_owner = jax.vmap(lambda own, number: assign_block(jax.random.fold_in(key_of[5], 2), own, number, EV_DEV, OWNERS, OWN_PICK, CAP, 2))(nbr_owner_keys, nbr_owner_turns).reshape((EVENTS, OWN_PICK))
    nbr_ids = place_ends(jax.random.randint(key_of[6], (EVENTS, OWN_PICK, SLOTS), 0, NODES_DEV), jax.random.fold_in(key_of[6], 1), 0, NODES_DEV - 1).astype(jnp.int32)
    nbr_mask = draw_nbr_mask(jax.random.fold_in(key_of[26], 71), 0)
    event_mask = draw_event_mask(jax.random.fold_in(key_of[26], 71), 0)
    dest_local = place_ends(jax.random.randint(key_of[9], (CANDS,), 0, NODES_DEV), jax.random.fold_in(key_of[9], 1), 0, NODES_DEV - 1).astype(jnp.int32)
    target = place_ends(jax.random.randint(key_of[10], (EVENTS,), 0, CAND_DEV * OWNERS), jax.random.fold_in(key_of[10], 1), 0, (CAND_DEV * OWNERS) - 1).astype(jnp.int32)
    w_msg = gaussian(key_of[11], (D + EDGE + TIME_DIM, D), (D + EDGE + TIME_DIM) ** -0.5, 0.25, (), jnp.float32)
    w_gru = gaussian(key_of[12], (2, D, 3 * D), D ** -0.5, 0.4375, (), jnp.float32)
    w_square = gaussian(key_of[13], (4, D, D), D ** -0.5, 0.4375, (), jnp.float32)
    w_key_value = gaussian(key_of[14], (D + TIME_DIM, 2 * D), ((D + TIME_DIM) // 20) ** -0.5, 1.75, (), jnp.float32)
    w_output = gaussian(key_of[15], (2 * D, D), (2 * D) ** -0.5, 0.3125, (), jnp.float32)
    mom_msg = gaussian(key_of[16], (D + EDGE + TIME_DIM, D), (9.0 * EVENTS ** -0.5), 0.75, (), jnp.float32)
    mom_gru = gaussian(key_of[17], (2, D, 3 * D), (9.0 * EVENTS ** -0.5), 0.75, (), jnp.float32)
    mom_square = gaussian(key_of[18], (4, D, D), (9.0 * EVENTS ** -0.5), 0.75, (), jnp.float32)
    mom_key_value = gaussian(key_of[19], (D + TIME_DIM, 2 * D), (9.0 * EVENTS ** -0.5), 0.75, (), jnp.float32)
    mom_output = gaussian(key_of[20], (2 * D, D), (9.0 * EVENTS ** -0.5), 0.75, (), jnp.float32)
    avg_msg = gaussian(key_of[21], (D + EDGE + TIME_DIM, D), (D + EDGE + TIME_DIM) ** -0.5, 0.25, (), jnp.float32)
    avg_gru = gaussian(key_of[22], (2, D, 3 * D), D ** -0.5, 0.4375, (), jnp.float32)
    avg_square = gaussian(key_of[23], (4, D, D), D ** -0.5, 0.4375, (), jnp.float32)
    avg_key_value = gaussian(key_of[24], (D + TIME_DIM, 2 * D), ((D + TIME_DIM) // 20) ** -0.5, 1.75, (), jnp.float32)
    avg_output = gaussian(key_of[25], (2 * D, D), (2 * D) ** -0.5, 0.3125, (), jnp.float32)
    return dict(memory=memory, last_update=last_update, src_local=src_local, edge_feat=edge_feat, event_time=event_time, nbr_owner=nbr_owner, nbr_ids=nbr_ids, nbr_mask=nbr_mask, event_mask=event_mask, dest_local=dest_local, target=target, w_msg=w_msg, w_gru=w_gru, w_square=w_square, w_key_value=w_key_value, w_output=w_output, mom_msg=mom_msg, mom_gru=mom_gru, mom_square=mom_square, mom_key_value=mom_key_value, mom_output=mom_output, avg_msg=avg_msg, avg_gru=avg_gru, avg_square=avg_square, avg_key_value=avg_key_value, avg_output=avg_output)


@jax.custom_vjp
def low(v):
    return lax.optimization_barrier(v.astype(jnp.bfloat16)).astype(jnp.float32)

@jax.custom_vjp
def low_back(v):
    return v

def low_keep(v):
    return (low(v), None)

def low_pass(kept, grad):
    return (grad,)

def back_keep(v):
    return (v, None)

def back_low(kept, grad):
    return (low(grad),)
low.defvjp(low_keep, low_pass)
low_back.defvjp(back_keep, back_low)
mu_coef = 0.9
avg_coef = 0.1
rate_coef = 0.008
mask_fill = -1e+30
highest = lax.Precision.HIGHEST

def time_code(delta, time_width):
    frequency = 1.0 / 10.0 ** jnp.linspace(0.0, 9.0, time_width, dtype=jnp.float32)
    return jnp.cos(delta[..., None] * frequency)

def product(left_side, right_side):
    return jnp.dot(left_side, right_side, precision=highest)

def nesterov(weight, gradient, moment, average, step_rate):
    new_moment = mu_coef * moment + gradient
    new_weight = weight - step_rate * (gradient + mu_coef * new_moment)
    return (new_moment, new_weight, (1.0 - avg_coef) * average + avg_coef * new_weight)

def reference(memory, last_update, src_local, edge_feat, event_time, nbr_owner, nbr_ids, nbr_mask, event_mask, dest_local, target, w_msg, w_gru, w_square, w_key_value, w_output, mom_msg, mom_gru, mom_square, mom_key_value, mom_output, avg_msg, avg_gru, avg_square, avg_key_value, avg_output):
    device = jnp.arange(EVENTS, dtype=jnp.int32) // EV_DEV
    src_node = device % OWNERS * NODES_DEV + src_local
    mem_src = memory[src_node]
    delta_src = (event_time - last_update[src_node]).astype(jnp.float32)
    edge_rows = edge_feat.astype(jnp.float32)
    nbr_node = (nbr_owner[:, :, None] * NODES_DEV + nbr_ids).reshape(EVENTS, ROUTE_SLOTS)
    live_slots = (nbr_mask > 0).reshape(EVENTS, ROUTE_SLOTS)
    cand_owner = jnp.arange(CANDS, dtype=jnp.int32) // CAND_DEV % OWNERS
    dest_mem = memory[cand_owner * NODES_DEV + dest_local]
    mask_float = event_mask.astype(jnp.float32)
    positives = jnp.maximum(jnp.sum(mask_float), 1.0)
    device_count = EVENTS // EV_DEV

    def attend(w_kv, block_data):
        block_query, block_time, node_ids, is_valid = block_data
        delta_key = (block_time[:, None] - last_update[node_ids]).astype(jnp.float32)
        inputs = low(jnp.concatenate([memory[node_ids], time_code(delta_key, TIME_DIM)], -1))
        pair_kv = low_back(jnp.einsum('rse,ef->rsf', inputs, w_kv, precision=highest))
        key_rows = low(pair_kv[..., :D]).reshape(EV_DEV, ROUTE_SLOTS, HEADS, HEAD_DIM)
        value_rows = low(pair_kv[..., D:]).reshape(EV_DEV, ROUTE_SLOTS, HEADS, HEAD_DIM)
        query_heads = block_query.reshape(EV_DEV, HEADS, HEAD_DIM)
        scores = jnp.einsum('rhd,rshd->rsh', query_heads, key_rows, precision=highest) * HEAD_DIM ** (-0.5)
        scores = jnp.where(is_valid[..., None], scores, mask_fill)
        row_max = lax.optimization_barrier(jnp.max(scores, 1, keepdims=True))
        expo_rows = jnp.exp(scores - row_max)
        probs = expo_rows / lax.optimization_barrier(jnp.sum(expo_rows, 1, keepdims=True))
        return jnp.einsum('rsh,rshd->rhd', probs, value_rows, precision=highest).reshape(EV_DEV, D)

    def forward(params):
        low_msg, low_gru, low_square, low_kv, low_output = [low(weight) for weight in params]
        x_msg = low(jnp.concatenate([mem_src, edge_rows, time_code(delta_src, TIME_DIM)], 1))
        pre_msg = low_back(product(x_msg, low_msg))
        hidden = low(jax.nn.silu(pre_msg))
        gate_in = low_back(product(hidden, low_gru[0]))
        gate_hid = low_back(product(low(mem_src), low_gru[1]))
        reset_gate = jax.nn.sigmoid(gate_in[:, :D] + gate_hid[:, :D])
        update = jax.nn.sigmoid(gate_in[:, D:2 * D] + gate_hid[:, D:2 * D])
        candidate = jnp.tanh(gate_in[:, 2 * D:] + reset_gate * gate_hid[:, 2 * D:])
        fresh_mem = (1.0 - update) * candidate + update * mem_src
        fresh_low = low(fresh_mem)
        queries = low(low_back(product(fresh_low, low_square[0])))
        blocks = (queries.reshape(device_count, EV_DEV, D), event_time.reshape(device_count, EV_DEV), nbr_node.reshape(device_count, EV_DEV, ROUTE_SLOTS), live_slots.reshape(device_count, EV_DEV, ROUTE_SLOTS))
        attended = lax.map(jax.checkpoint(partial(attend, low_kv)), blocks).reshape(EVENTS, D)
        attended_low = low(low_back(attended))
        mixed_out = low_back(product(attended_low, low_square[1]))
        x_out = low(jnp.concatenate([mixed_out, fresh_mem], 1))
        pre_out = low_back(product(x_out, low_output))
        hidden_out = low(jax.nn.silu(pre_out))
        embedding = low(low_back(product(hidden_out, low_square[2])))
        dest_emb = low(product(low(dest_mem), low_square[3])).reshape(N_BATCH, OWNERS * CAND_DEV, D)

        def device_loss(block_data):
            row_data, tgt_ids, mask_rows, group_idx = block_data
            cand_rows = low_back(lax.dynamic_index_in_dim(dest_emb, group_idx, 0, keepdims=False))
            logits = low_back(jnp.dot(row_data, cand_rows.T, precision=highest))
            row_max = lax.optimization_barrier(jnp.max(logits, 1, keepdims=True))
            log_sum = row_max[:, 0] + jnp.log(lax.optimization_barrier(jnp.sum(jnp.exp(logits - row_max), 1)))
            picked = jnp.take_along_axis(logits, tgt_ids[:, None], 1)[:, 0]
            return jnp.sum(mask_rows * (log_sum - picked))
        groups = jnp.arange(device_count, dtype=jnp.int32) // OWNERS
        losses = lax.map(jax.checkpoint(device_loss), (embedding.reshape(device_count, EV_DEV, D), target.reshape(device_count, EV_DEV), mask_float.reshape(device_count, EV_DEV), groups))
        loss_sum = jnp.sum(losses)
        return (loss_sum / positives, loss_sum)
    params = (w_msg, w_gru, w_square, w_key_value, w_output)
    loss_mean, grad_fn, loss_sum = jax.vjp(forward, params, has_aux=True)
    grads = grad_fn(jnp.ones_like(loss_mean))[0]
    step_rate = rate_coef * math.sqrt(EVENTS)
    moments = (mom_msg, mom_gru, mom_square, mom_key_value, mom_output)
    averages = (avg_msg, avg_gru, avg_square, avg_key_value, avg_output)
    states = [nesterov(params[index], grads[index], moments[index], averages[index], step_rate) for index in range(5)]
    new_last = last_update.at[src_node].max(event_time)
    return (loss_sum, positives, new_last, states[0][0], states[1][0], states[2][0], states[3][0], states[4][0], states[0][1], states[1][1], states[2][1], states[3][1], states[4][1], states[0][2], states[1][2], states[2][2], states[3][2], states[4][2])
```

```python
from functools import partial
import math

import jax
import jax.numpy as jnp
import numpy as np
from jax import lax
from jax.experimental import pallas as pl
from jax.experimental.pallas import tpu as pltpu
from jax.sharding import PartitionSpec as P

HEADS = 2
LANES = 256
MESH = pl.DeviceIdType.MESH
f32 = jnp.float32
bf16 = jnp.bfloat16

mu_coef = 0.9
avg_coef = 0.1
rate_coef = 0.008
mask_fill = -1e30

COS_TERMS = (
    1.0,
    -19.73920440673828,
    64.93911743164062,
    -85.45011901855469,
    60.16745376586914,
    -25.966907501220703,
    6.527653217315674,
)


def pad_to(size, step):
    return -(-size // step) * step


def nn(a, b):
    return lax.dot_general(a, b, (((1,), (0,)), ((), ())), preferred_element_type=f32)


def nt(a, b):
    return lax.dot_general(a, b, (((1,), (1,)), ((), ())), preferred_element_type=f32)


def flip_bit(index, bit):
    size = 1 << bit
    return index + size * (1 - 2 * (lax.div(index, size) % 2))


def nesterov(weight, gradient, moment, average, step_rate):
    new_moment = mu_coef * moment + gradient
    new_weight = weight - step_rate * (gradient + mu_coef * new_moment)
    return (new_moment, new_weight, (1.0 - avg_coef) * average + avg_coef * new_weight)


def time_columns(time_width, rows):
    turns = 10.0 ** (-np.linspace(0.0, 9.0, time_width)) / (2.0 * np.pi)
    mant, expo = np.frexp(turns)
    high = np.ldexp(np.round(mant * 4096.0) / 4096.0, expo)
    out = np.zeros((rows, 128), np.float32)
    out[:time_width, 0] = high
    out[:time_width, 1] = turns - high
    return out


def cos_rows(delta, high, low):
    turns = delta * high
    rest = turns - jnp.floor(turns + 0.5) + delta * low
    square = rest * rest
    value = square * COS_TERMS[-1] + COS_TERMS[-2]
    for term in COS_TERMS[-3::-1]:
        value = value * square + term
    return value


class Heads:
    def __init__(self, head_dim, rows):
        self.low = head_dim // 8 * 8
        self.high = pad_to(head_dim, 8)
        self.cut = head_dim - self.low
        self.rows = rows

    def split(self, lanes):
        return lax.broadcasted_iota(jnp.int32, (8, lanes), 0) < self.cut

    def sums(self, x):
        lanes = x.shape[1]
        mid = x[self.low : self.high]
        first = self.split(lanes)
        a = jnp.sum(x[: self.low].reshape(self.low // 8, 8, lanes), 0)
        b = jnp.sum(x[self.high :].reshape((self.rows - self.high) // 8, 8, lanes), 0)
        a = a + jnp.where(first, mid, 0.0)
        b = b + jnp.where(first, 0.0, mid)
        return jnp.sum(a, 0, keepdims=True), jnp.sum(b, 0, keepdims=True)

    def scale(self, x, p0, p1):
        lanes = x.shape[1]
        mid = jnp.where(self.split(lanes), p0, p1)
        return jnp.concatenate(
            [x[: self.low] * p0, x[self.low : self.high] * mid, x[self.high :] * p1], 0
        )


def exchange_kernel(
    own, batch, shard_ref, cand_ref, event_ref, last_ref,
    table_ref, ids_ref, pos_ref, newest_ref,
    batch_buf, own_buf, local_sem, table_send, table_recv, batch_send, batch_recv, own_send, own_recv,
):
    me = lax.axis_index("own")
    group = lax.axis_index("batch")
    barrier = pltpu.get_barrier_semaphore()
    for step in range(1, own):
        pl.semaphore_signal(barrier, inc=1, device_id=(group, lax.rem(me + step, own)), device_id_type=MESH)
    for step in range(1, batch):
        pl.semaphore_signal(barrier, inc=1, device_id=(lax.rem(group + step, batch), me), device_id_type=MESH)
    pl.semaphore_wait(barrier, own + batch - 2)

    nodes = shard_ref.shape[0]
    half = nodes // 2
    bits = own.bit_length() - 1
    rest = list(range(1, bits))
    cut = len(rest) // 2
    orders = (rest + [0], rest[cut:] + rest[:cut] + [0])

    def shard_copy(stream, pattern, bit):
        peer = flip_bit(me, bit)
        source = me
        for b in range(bits):
            if pattern >> b & 1:
                source = flip_bit(source, b)
        rows = pl.ds(pl.multiple_of(source * nodes + stream * half, half), half)
        slot = pattern | 1 << bit
        src = shard_ref.at[pl.ds(stream * half, half)] if pattern == 0 else table_ref.at[rows]
        return pltpu.make_async_remote_copy(
            src_ref=src, dst_ref=table_ref.at[rows],
            send_sem=table_send.at[stream, slot], recv_sem=table_recv.at[stream, slot],
            device_id=(group, peer), device_id_type=MESH,
        )

    copies = [{}, {}]
    for step in range(bits):
        for stream in range(2):
            bit = orders[stream][step]
            copy = shard_copy(stream, 0, bit)
            copy.start()
            copies[stream][1 << bit] = copy
    mine = pltpu.make_async_copy(
        shard_ref, table_ref.at[pl.ds(pl.multiple_of(me * nodes, nodes), nodes)], local_sem
    )
    mine.start()

    events = event_ref.shape[1]
    time_row = event_ref[0:1, :].astype(f32)
    src_row = event_ref[2:3, :]
    best = []
    tile = 256
    for start in range(0, nodes, tile):
        node = lax.broadcasted_iota(jnp.int32, (tile, 128), 0) + start
        top = jnp.full((tile, 128), -1.0, f32)
        for lane in range(0, events, 128):
            hit = src_row[:, lane : lane + 128] == node
            top = jnp.maximum(top, jnp.where(hit, time_row[:, lane : lane + 128], -1.0))
        best.append(jnp.max(top.T, 0, keepdims=True))
    newest = jnp.concatenate(best, 1).astype(jnp.int32)
    newest = jnp.maximum(newest, last_ref[0:1, :])
    count = jnp.sum(event_ref[1:2, :].astype(f32), 1, keepdims=True).astype(jnp.int32)
    batch_buf[0, 0:1, :] = newest
    batch_buf[0, 1:2, :] = jnp.broadcast_to(count, (1, nodes))

    def peer_copy(step):
        return pltpu.make_async_remote_copy(
            src_ref=batch_buf.at[0], dst_ref=batch_buf.at[step],
            send_sem=batch_send.at[step], recv_sem=batch_recv.at[step],
            device_id=(lax.rem(group + step, batch), me), device_id_type=MESH,
        )

    peers = [peer_copy(step) for step in range(1, batch)]
    for copy in peers:
        copy.start()
    total = count
    for step, copy in enumerate(peers, 1):
        copy.wait_recv()
        newest = jnp.maximum(newest, batch_buf[step, 0:1, :])
        total = total + batch_buf[step, 1:2, 0:1]
    newest_ref[...] = newest

    width = cand_ref.shape[1]
    own_buf[0, 0:1, :] = cand_ref[...] + me * nodes
    own_buf[0, 1:2, :] = jnp.broadcast_to(total, (1, width))

    def owner_copy(step):
        return pltpu.make_async_remote_copy(
            src_ref=own_buf.at[0], dst_ref=own_buf.at[step],
            send_sem=own_send.at[step], recv_sem=own_recv.at[step],
            device_id=(group, lax.rem(me + step, own)), device_id_type=MESH,
        )

    owners = [owner_copy(step) for step in range(1, own)]
    for copy in owners:
        copy.start()

    for step in range(bits):
        for stream in range(2):
            order = orders[stream]
            held = [0]
            for bit in order[:step]:
                held = held + [p | 1 << bit for p in held]
            for pattern in held:
                slot = pattern | 1 << order[step]
                copies[stream][slot].wait_recv() if slot in copies[stream] else None
                for bit in order[step + 1 :]:
                    copy = shard_copy(stream, slot, bit)
                    copy.start()
                    copies[stream][slot | 1 << bit] = copy

    ids_ref[pl.ds(me, 1), :] = own_buf[0, 0:1, :]
    for step, copy in enumerate(owners, 1):
        copy.wait_recv()
        source = lax.rem(me - step + own, own)
        ids_ref[pl.ds(source, 1), :] = own_buf[step, 0:1, :]
        total = total + own_buf[step, 1:2, 0:1]
    pos_ref[...] = jnp.broadcast_to(jnp.maximum(total.astype(f32), 1.0), pos_ref.shape)
    mine.wait()
    for copy in peers + owners:
        copy.wait_send()
    for stream in range(2):
        for slot in copies[stream]:
            copies[stream][slot].wait_send()


def exchange(own, batch, shard, cand, event_rows, last):
    nodes = shard.shape[0]
    width = cand.shape[1]
    vmem = pl.BlockSpec(memory_space=pltpu.VMEM)
    hbm = pl.BlockSpec(memory_space=pl.ANY)
    return pl.pallas_call(
        partial(exchange_kernel, own, batch),
        out_shape=(
            jax.ShapeDtypeStruct((own * nodes, 2, 128), bf16),
            jax.ShapeDtypeStruct((own, width), jnp.int32),
            jax.ShapeDtypeStruct((8, 128), f32),
            jax.ShapeDtypeStruct((1, nodes), jnp.int32),
        ),
        in_specs=[hbm, vmem, vmem, vmem],
        out_specs=(hbm, vmem, vmem, vmem),
        scratch_shapes=[
            pltpu.VMEM((batch, 8, nodes), jnp.int32),
            pltpu.VMEM((own, 8, width), jnp.int32),
            pltpu.SemaphoreType.DMA,
            pltpu.SemaphoreType.DMA((2, own)),
            pltpu.SemaphoreType.DMA((2, own)),
            pltpu.SemaphoreType.DMA((batch,)),
            pltpu.SemaphoreType.DMA((batch,)),
            pltpu.SemaphoreType.DMA((own,)),
            pltpu.SemaphoreType.DMA((own,)),
        ],
        compiler_params=pltpu.CompilerParams(
            collective_id=1, has_side_effects=True, vmem_limit_bytes=32 * 2**20
        ),
        name="exchange",
    )(shard, cand, event_rows, last)


class Layout:
    def __init__(self, width, edge, time_width, fold):
        rows = pad_to(width, 16)
        times = pad_to(time_width, 16)
        edges = pad_to(edge, 16)
        assert width <= 192 and edges == rows
        names = ["msg_mem", "msg_edge"]
        names += [f"gru{i}{g}" for i in range(2) for g in range(3)]
        names += [f"square{i}" for i in range(4)]
        names += ["kv_mem_k", "kv_mem_v", "out_a", "out_b"]
        sizes = [(n, rows) for n in names] + [("kv_time_k", times), ("kv_time_v", times), ("msg_time", times)]
        self.at = {}
        row = 0
        for name, size in sizes:
            self.at[name] = [row, size, None, None]
            row += size
        for index, (name, size) in enumerate(sizes):
            if index % 2 == 0:
                self.at[name][2:] = [row, 0]
                row += size
            else:
                before = self.at[sizes[index - 1][0]]
                assert before[1] == size
                self.at[name][2:] = [before[2], 64]
        self.loss = row
        row += 8
        self.total = pad_to(row, fold)
        self.unused = row

    def put(self, ref, name, value):
        first, size, second, lane = self.at[name]
        ref[first : first + size, :] = value[:, :128]
        ref[second : second + size, lane : lane + value.shape[1] - 128] = value[:, 128:]

    def take(self, packed, name, rows, width):
        first, size, second, lane = self.at[name]
        return jnp.concatenate(
            [packed[first : first + rows, :128], packed[second : second + rows, lane : lane + width - 128]], 1
        )


def main_kernel(
    dims,
    ids_ref, cand_ref, pos_ref, table_ref, event_ref, valid_ref, mem3_ref, edge_ref,
    wsq_ref, wme_ref, wtime_ref, wkv1_ref, wkv2_ref, wd_ref, wdt_ref, eye_ref, freq_ref,
    grad_ref,
    xs, x_all, t_all, kv_all, score, dest_rows, slab,
    t_src, mem_low, hidden, fresh_low, att_low, mixed_low, hid_out, emb, emb_rows,
    mem_src, pre_msg, reset_gate, update, cand_act, gate_n, queries, attended, pre_out,
    acc_a, grad_att, gkv_m, gkv_t, rows_ref,
):
    width, head_dim, slots, keep_kv, layout = dims
    events = event_ref.shape[1]
    rows = pad_to(width, 16)
    times = t_src.shape[0]
    heads = Heads(head_dim, rows)
    scale = head_dim ** (-0.5)
    high, low = freq_ref[:, 0:1], freq_ref[:, 1:2]
    chunks = events // LANES
    owners, cand_width = cand_ref.shape
    W = {}
    order = ["wm_m", "g0r", "g0z", "g0n", "g1r", "g1z", "g1n", "s0t", "s1t", "s2t", "oat", "obt",
             "g0r_", "g0z_", "g0n_", "s0", "s1", "s2", "oa", "ob"]
    for index, name in enumerate(order):
        W[name] = index

    def w(name):
        return wsq_ref[W[name]]

    def gather(read_id, count):
        unroll = 64

        def body(i, unused):
            base = i * unroll
            got = [table_ref[read_id(base + k)] for k in range(unroll)]
            for k in range(unroll):
                xs[pl.ds(pl.multiple_of(2 * base, 2 * unroll) + 2 * k, 2), :] = got[k].astype(f32)
            return unused

        lax.fori_loop(0, count // unroll, body, 0)

    def gathered(start, count):
        base = pl.multiple_of(2 * start, 2 * count)
        return jnp.concatenate(
            [xs[pl.ds(base, count, stride=2), :], xs[pl.ds(base + 1, count, stride=2), :]], 1
        ).astype(bf16)

    grad_ref[...] = jnp.zeros_like(grad_ref)

    def cand_body(o, unused):
        gather(lambda i: cand_ref[o, i], cand_width)
        at = pl.multiple_of(o * cand_width, cand_width)
        dest_rows[pl.ds(at, cand_width), :] = gathered(0, cand_width)
        return unused

    lax.fori_loop(0, owners, cand_body, 0)

    def lanes(c, size=LANES):
        return pl.ds(pl.multiple_of(c * size, size), size)

    def gru_body(c, unused):
        cs = lanes(c)
        node = lax.broadcasted_iota(jnp.int32, (mem3_ref.shape[1], LANES), 0)
        onehot = (node == event_ref[2:3, cs]).astype(f32).astype(bf16)
        parts = nn(mem3_ref[...], onehot)
        mem = parts[:rows] + parts[rows : 2 * rows] + parts[2 * rows :]
        mem_src[:, cs] = mem
        delta = event_ref[0:1, cs].astype(f32) - mem[width : width + 1]
        t_low = cos_rows(delta, high, low).astype(bf16)
        t_src[:, cs] = t_low
        m_low = mem.astype(bf16)
        mem_low[:, cs] = m_low
        pre = nn(w("wm_m"), m_low) + nt(wme_ref[...], edge_ref[cs, :]) + nn(wtime_ref[...], t_low)
        pre_msg[:, cs] = pre
        hid = (pre * jax.nn.sigmoid(pre)).astype(bf16)
        hidden[:, cs] = hid
        r = jax.nn.sigmoid(nn(w("g0r"), hid) + nn(w("g1r"), m_low))
        reset_gate[:, cs] = r
        u = jax.nn.sigmoid(nn(w("g0z"), hid) + nn(w("g1z"), m_low))
        update[:, cs] = u
        gn = nn(w("g1n"), m_low)
        gate_n[:, cs] = gn
        cand = jnp.tanh(nn(w("g0n"), hid) + r * gn)
        cand_act[:, cs] = cand
        fresh = ((1.0 - u) * cand + u * mem).astype(bf16)
        fresh_low[:, cs] = fresh
        queries[:, cs] = nn(w("s0t"), fresh).astype(bf16)
        return unused

    lax.fori_loop(0, chunks, gru_body, 0)

    def slot_body(j, unused):
        gather(lambda i: ids_ref[j * events + i], events)

        def chunk_body(c, unused):
            cs = lanes(c)
            x = gathered(c * LANES, LANES)
            x_all[j, cs, :] = x
            kv = nt(wkv1_ref[...], x)
            delta = event_ref[0:1, cs].astype(f32) - kv[width : width + 1]
            t_low = cos_rows(delta, high, low).astype(bf16)
            t_all[j, :, cs] = t_low
            kv = (kv + nn(wkv2_ref[...], t_low)).astype(bf16)
            if keep_kv:
                kv_all[j, :, cs] = kv
            s0, s1 = heads.sums(kv[:rows].astype(f32) * queries[:, cs].astype(f32))
            live = valid_ref[j, :, cs] > 0
            score[j, 0:1, cs] = jnp.where(live, s0 * scale, mask_fill)
            score[j, 1:2, cs] = jnp.where(live, s1 * scale, mask_fill)
            return unused

        lax.fori_loop(0, chunks, chunk_body, 0)
        return unused

    lax.fori_loop(0, slots, slot_body, 0)

    def soft_body(c, unused):
        cs = lanes(c, 128)
        s = score[:, 0:2, cs]
        top = jnp.max(s, 0, keepdims=True)
        p = jnp.where(s > 0.5 * mask_fill, jnp.exp(s - top), 0.0)
        score[:, 0:2, cs] = p / jnp.sum(p, 0, keepdims=True)
        return unused

    lax.fori_loop(0, events // 128, soft_body, 0)

    def kv_of(j, cs, part):
        if keep_kv:
            return kv_all[j, part, cs]
        return (nt(wkv1_ref[part, :], x_all[j, cs, :]) + nn(wkv2_ref[part, :], t_all[j, :, cs])).astype(bf16)

    def att_body(c, unused):
        cs = lanes(c, 128)

        def add(j, total):
            v = kv_of(j, cs, slice(rows, 2 * rows)).astype(f32)
            return total + heads.scale(v, score[j, 0:1, cs], score[j, 1:2, cs])

        att = lax.fori_loop(0, slots, add, jnp.zeros((rows, 128), f32))
        attended[:, cs] = att
        att_low[:, cs] = att.astype(bf16)
        return unused

    lax.fori_loop(0, events // 128, att_body, 0)

    def out_body(c, unused):
        cs = lanes(c)
        mixed = nn(w("s1t"), att_low[:, cs]).astype(bf16)
        mixed_low[:, cs] = mixed
        pre = nn(w("oat"), mixed) + nn(w("obt"), fresh_low[:, cs])
        pre_out[:, cs] = pre
        hid = (pre * jax.nn.sigmoid(pre)).astype(bf16)
        hid_out[:, cs] = hid
        e = nn(w("s2t"), hid).astype(bf16)
        emb[:, cs] = e
        emb_rows[cs, :] = nt(eye_ref[...], e).astype(bf16)
        return unused

    lax.fori_loop(0, chunks, out_body, 0)

    def row_init(c, unused):
        cs = lanes(c)
        rows_ref[0:1, cs] = jnp.full((1, LANES), mask_fill, f32)
        rows_ref[1:3, cs] = jnp.zeros((2, LANES), f32)
        acc_a[:, cs] = jnp.zeros((rows, LANES), f32)
        return unused

    lax.fori_loop(0, chunks, row_init, 0)

    def dest_of(o):
        at = pl.multiple_of(o * cand_width, cand_width)
        return dest_rows[pl.ds(at, cand_width), :]

    def lse_block(o, unused):
        dest = nn(dest_of(o), wd_ref[...]).astype(bf16)

        def chunk(c, unused):
            cs = lanes(c)
            logits = nn(dest, emb[:, cs])
            old = rows_ref[0:1, cs]
            top = jnp.maximum(old, jnp.max(logits, 0, keepdims=True))
            rows_ref[0:1, cs] = top
            rows_ref[1:2, cs] = rows_ref[1:2, cs] * jnp.exp(old - top) + jnp.sum(
                jnp.exp(logits - top), 0, keepdims=True
            )
            hit = lax.broadcasted_iota(jnp.int32, logits.shape, 0) == event_ref[3:4, cs] - o * cand_width
            rows_ref[2:3, cs] = rows_ref[2:3, cs] + jnp.sum(jnp.where(hit, logits, 0.0), 0, keepdims=True)
            return unused

        lax.fori_loop(0, chunks, chunk, 0)
        return unused

    lax.fori_loop(0, owners, lse_block, 0)

    mask_row = event_ref[1:2, :].astype(f32)
    log_sum = rows_ref[0:1, :] + jnp.log(rows_ref[1:2, :])
    rows_ref[3:4, :] = log_sum
    rows_ref[4:5, :] = mask_row / jnp.broadcast_to(pos_ref[0:1, 0:1], mask_row.shape)
    loss = jnp.sum(mask_row * (log_sum - rows_ref[2:3, :]), 1, keepdims=True)
    grad_ref[layout.loss : layout.loss + 8, :] = jnp.broadcast_to(loss, (8, 128))

    def back_block(o, grad_dest_w):
        block = dest_of(o)
        dest = nn(block, wd_ref[...]).astype(bf16)
        dest_t = nt(wdt_ref[...], block).astype(bf16)
        block_t = nt(eye_ref[...], block).astype(bf16)

        def chunk(c, unused):
            cs = lanes(c)
            logits = nn(dest, emb[:, cs])
            coeff = rows_ref[4:5, cs]
            hit = lax.broadcasted_iota(jnp.int32, logits.shape, 0) == event_ref[3:4, cs] - o * cand_width
            grad = jnp.exp(logits - rows_ref[3:4, cs]) - jnp.where(hit, 1.0, 0.0)
            grad = (grad * coeff).astype(bf16)
            slab[0:cand_width, cs] = grad
            acc_a[:, cs] += nn(dest_t, grad)
            return unused

        lax.fori_loop(0, chunks, chunk, 0)
        grad_dest = nn(slab[0:cand_width, :], emb_rows[...]).astype(bf16)
        return grad_dest_w + nn(block_t, grad_dest)[:rows]

    grad_dest_w = lax.fori_loop(0, owners, back_block, jnp.zeros((rows, rows), f32))
    layout.put(grad_ref, "square3", grad_dest_w)

    r0, r1, r2 = slice(0, rows), slice(rows, 2 * rows), slice(2 * rows, 3 * rows)

    def out_back(c, unused):
        cs = lanes(c)
        ge = acc_a[:, cs].astype(bf16)
        slab[r0, cs] = ge
        pre = pre_out[:, cs]
        sig = jax.nn.sigmoid(pre)
        gp = (nn(w("s2"), ge) * (sig * (1.0 + pre * (1.0 - sig)))).astype(bf16)
        slab[r1, cs] = gp
        gm = nn(w("oa"), gp).astype(bf16)
        slab[r2, cs] = gm
        acc_a[:, cs] = nn(w("ob"), gp)
        ga = nn(w("s1"), gm).astype(bf16)
        grad_att[:, cs] = ga
        d0, d1 = heads.sums(ga.astype(f32) * attended[:, cs])
        rows_ref[5:6, cs] = d0
        rows_ref[6:7, cs] = d1
        return unused

    lax.fori_loop(0, chunks, out_back, 0)
    layout.put(grad_ref, "square2", nt(hid_out[...], slab[r0, :]))
    layout.put(grad_ref, "out_a", nt(mixed_low[...], slab[r1, :]))
    layout.put(grad_ref, "out_b", nt(fresh_low[...], slab[r1, :]))
    layout.put(grad_ref, "square1", nt(att_low[...], slab[r2, :]))

    attended[...] = jnp.zeros_like(attended)
    gkv_m[...] = jnp.zeros_like(gkv_m)
    gkv_t[...] = jnp.zeros_like(gkv_t)

    def slot_back(j, unused):
        def chunk(c, unused):
            cs = lanes(c, 128)
            kv = kv_of(j, cs, slice(0, 2 * rows)).astype(f32)
            ga = grad_att[:, cs].astype(f32)
            p0, p1 = score[j, 0:1, cs], score[j, 1:2, cs]
            g0, g1 = heads.sums(ga * kv[rows:])
            g0 = p0 * (g0 - rows_ref[5:6, cs]) * scale
            g1 = p1 * (g1 - rows_ref[6:7, cs]) * scale
            attended[:, cs] += heads.scale(kv[:rows], g0, g1)
            slab[r0, cs] = heads.scale(queries[:, cs].astype(f32), g0, g1).astype(bf16)
            slab[r1, cs] = heads.scale(ga, p0, p1).astype(bf16)
            return unused

        lax.fori_loop(0, events // 128, chunk, 0)
        both = slab[0 : 2 * rows, :]
        gkv_m[...] += nn(both, x_all[j])
        gkv_t[...] += nt(both, t_all[j])
        return unused

    lax.fori_loop(0, slots, slot_back, 0)
    gm = gkv_m[...].T
    layout.put(grad_ref, "kv_mem_k", gm[:rows, :rows])
    layout.put(grad_ref, "kv_mem_v", gm[:rows, rows:])
    gt = gkv_t[...].T
    layout.put(grad_ref, "kv_time_k", gt[:times, :rows])
    layout.put(grad_ref, "kv_time_v", gt[:times, rows:])

    def gru_back(c, unused):
        cs = lanes(c)
        gq = attended[:, cs].astype(bf16)
        slab[r0, cs] = gq
        gf = acc_a[:, cs] + nn(w("s0"), gq)
        u, cand, r = update[:, cs], cand_act[:, cs], reset_gate[:, cs]
        act = gf * (1.0 - u) * (1.0 - cand * cand)
        gr = (act * gate_n[:, cs] * r * (1.0 - r)).astype(bf16)
        gu = (gf * (mem_src[:, cs] - cand) * u * (1.0 - u)).astype(bf16)
        gn = act.astype(bf16)
        gh = (act * r).astype(bf16)
        slab[r1, cs] = gr
        slab[r2, cs] = gu
        mixed_low[:, cs] = gn
        hid_out[:, cs] = gh
        pre = pre_msg[:, cs]
        sig = jax.nn.sigmoid(pre)
        back = nn(w("g0r_"), gr) + nn(w("g0z_"), gu) + nn(w("g0n_"), gn)
        att_low[:, cs] = (back * (sig * (1.0 + pre * (1.0 - sig)))).astype(bf16)
        return unused

    lax.fori_loop(0, chunks, gru_back, 0)
    layout.put(grad_ref, "square0", nt(fresh_low[...], slab[r0, :]))
    for index, (left, last) in enumerate(((hidden, mixed_low), (mem_low, hid_out))):
        layout.put(grad_ref, f"gru{index}0", nt(left[...], slab[r1, :]))
        layout.put(grad_ref, f"gru{index}1", nt(left[...], slab[r2, :]))
        layout.put(grad_ref, f"gru{index}2", nt(left[...], last[...]))
    layout.put(grad_ref, "msg_mem", nt(mem_low[...], att_low[...]))
    layout.put(grad_ref, "msg_time", nt(t_src[...], att_low[...]))
    edge_back = nn(att_low[...], edge_ref[...])
    edge_back = jnp.concatenate([edge_back, jnp.zeros((rows, 256 - edge_back.shape[1]), f32)], 1)
    edge_back = jnp.concatenate([edge_back, jnp.zeros((256 - rows, 256), f32)], 0).T
    layout.put(grad_ref, "msg_edge", edge_back[:rows, :rows])


def main(layout, keep_kv, width, head_dim, slots, times, args):
    events = args[4].shape[1]
    rows = pad_to(width, 16)
    cands = args[1].shape[0] * args[1].shape[1]
    smem = pl.BlockSpec(memory_space=pltpu.SMEM)
    vmem = pl.BlockSpec(memory_space=pltpu.VMEM)
    low = lambda *shape: pltpu.VMEM(shape, bf16)
    full = lambda *shape: pltpu.VMEM(shape, f32)
    return pl.pallas_call(
        partial(main_kernel, (width, head_dim, slots, keep_kv, layout)),
        out_shape=jax.ShapeDtypeStruct((layout.total, 128), f32),
        in_specs=[smem, smem] + [vmem] * (len(args) - 2),
        out_specs=vmem,
        scratch_shapes=[
            full(2 * events, 128),
            low(slots, events, 256),
            low(slots, times, events),
            low(slots if keep_kv else 1, 2 * rows if keep_kv else 16, events),
            full(slots, 8, events),
            low(cands, 256),
            low(max(3 * rows, args[1].shape[1]), events),
            low(times, events),
        ]
        + [low(rows, events)] * 7
        + [low(events, rows)]
        + [full(rows, events)] * 6
        + [low(rows, events)]
        + [full(rows, events)] * 3
        + [low(rows, events), full(2 * rows, 256), full(2 * rows, times), full(8, events)],
        compiler_params=pltpu.CompilerParams(vmem_limit_bytes=63 * 2**20),
        name="train",
    )(*args)


def reduce_kernel(own, batch, streams, grad_ref, out_ref, acc, recv, send_sem, recv_sem):
    place = {"own": lax.axis_index("own"), "batch": lax.axis_index("batch")}

    def peer(axis, bit):
        moved = dict(place)
        moved[axis] = flip_bit(place[axis], bit)
        return (moved["batch"], moved["own"])

    barrier = pltpu.get_barrier_semaphore()
    steps = streams[0][2]
    for axis, bit in steps:
        pl.semaphore_signal(barrier, inc=1, device_id=peer(axis, bit), device_id_type=MESH)
    pl.semaphore_wait(barrier, len(steps))

    base = [start for start, size, order in streams]
    sizes = [size for start, size, order in streams]
    inner = [start for start, size, order in streams]
    sent = []
    for step in range(len(steps)):
        source = grad_ref if step == 0 else acc
        copies = []
        for s, (start, size, order) in enumerate(streams):
            axis, bit = order[step]
            half = sizes[s] // 2
            mine = lax.div(place[axis], 1 << bit) % 2
            away = pl.multiple_of(base[s] + (1 - mine) * half, 8)
            copy = pltpu.make_async_remote_copy(
                src_ref=source.at[pl.ds(away, half), :],
                dst_ref=recv.at[pl.ds(inner[s], half), :],
                send_sem=send_sem.at[s, step], recv_sem=recv_sem.at[s, step],
                device_id=peer(axis, bit), device_id_type=MESH,
            )
            copy.start()
            copies.append(copy)
            base[s] = pl.multiple_of(base[s] + mine * half, 8)
            sizes[s] = half
        last = step == len(steps) - 1
        target = out_ref if last else acc
        for s, copy in enumerate(copies):
            copy.wait_recv()
            part = pl.ds(base[s], sizes[s])
            target[part, :] = source[part, :] + recv[pl.ds(inner[s], sizes[s]), :]
            inner[s] += sizes[s]
        sent += copies
    for step in reversed(range(len(steps))):
        copies = []
        for s, (start, size, order) in enumerate(streams):
            axis, bit = order[step]
            part = pl.ds(base[s], sizes[s])
            copy = pltpu.make_async_remote_copy(
                src_ref=out_ref.at[part, :], dst_ref=out_ref.at[part, :],
                send_sem=send_sem.at[s, step + len(steps)], recv_sem=recv_sem.at[s, step + len(steps)],
                device_id=peer(axis, bit), device_id_type=MESH,
            )
            copy.start()
            copies.append(copy)
            mine = lax.div(place[axis], 1 << bit) % 2
            base[s] = pl.multiple_of(base[s] - mine * sizes[s], 8)
            sizes[s] *= 2
        for copy in copies:
            copy.wait_recv()
        sent += copies
    for copy in sent:
        copy.wait_send()


def reduce_all(own, batch, packed):
    total = packed.shape[0]
    own_bits = own.bit_length() - 1
    batch_bits = batch.bit_length() - 1
    fold = 8 << (own_bits + batch_bits)
    rest = [("own", b) for b in range(1, own_bits)]
    cut = len(rest) // 2
    tail = [("batch", b) for b in range(batch_bits)]
    blocks = total // fold
    first = (blocks + 1) // 2 * fold
    streams = (
        (0, first, [("own", 0)] + rest + tail),
        (first, total - first, [("own", 0)] + rest[cut:] + rest[:cut] + tail),
    )
    count = 2 * (own_bits + batch_bits)
    return pl.pallas_call(
        partial(reduce_kernel, own, batch, streams),
        out_shape=jax.ShapeDtypeStruct(packed.shape, f32),
        in_specs=[pl.BlockSpec(memory_space=pltpu.VMEM)],
        out_specs=pl.BlockSpec(memory_space=pltpu.VMEM),
        scratch_shapes=[
            pltpu.VMEM(packed.shape, f32),
            pltpu.VMEM(packed.shape, f32),
            pltpu.SemaphoreType.DMA((2, count)),
            pltpu.SemaphoreType.DMA((2, count)),
        ],
        compiler_params=pltpu.CompilerParams(
            collective_id=2, has_side_effects=True, vmem_limit_bytes=32 * 2**20
        ),
        name="reduce",
    )(packed)


def local(
    memory, last_update, src_local, edge_feat, event_time, nbr_owner, nbr_ids, nbr_mask, event_mask,
    dest_local, target, w_msg, w_gru, w_square, w_key_value, w_output,
    mom_msg, mom_gru, mom_square, mom_key_value, mom_output,
    avg_msg, avg_gru, avg_square, avg_key_value, avg_output,
):
    own = lax.axis_size("own")
    batch = lax.axis_size("batch")
    events, edge = edge_feat.shape
    nodes, width = memory.shape
    picks, per_pick = nbr_ids.shape[1:]
    slots = picks * per_pick
    head_dim = width // HEADS
    time_width = w_key_value.shape[0] - width
    rows = pad_to(width, 16)
    times = pad_to(time_width, 16)
    layout = Layout(width, edge, time_width, (8 * own * batch))

    mem_low = memory.astype(bf16)
    time_parts = jnp.stack([last_update // 8, last_update % 8], 1).astype(bf16)
    shard = jnp.pad(jnp.concatenate([mem_low, time_parts], 1), ((0, 0), (0, 256 - width - 2)))
    shard = shard.reshape(nodes, 2, 128)
    event_rows = jnp.stack([event_time, event_mask, src_local, target])
    event_rows = jnp.pad(event_rows, ((0, 4), (0, 0)))
    table, cand_ids, positives, newest = exchange(
        own, batch, shard, dest_local[None, :], event_rows, last_update[None, :]
    )

    flat_ids = (nbr_owner[:, :, None] * nodes + nbr_ids).reshape(events, slots).T.reshape(-1)
    valid = nbr_mask.reshape(events, slots).T.reshape(slots, 1, events)
    mem_t = jnp.pad(jnp.concatenate([memory, last_update.astype(f32)[:, None]], 1).T, ((0, rows - width - 1), (0, 0)))
    part0 = mem_t.astype(bf16)
    part1 = (mem_t - part0.astype(f32)).astype(bf16)
    part2 = (mem_t - part0.astype(f32) - part1.astype(f32)).astype(bf16)
    mem3 = jnp.concatenate([part0, part1, part2], 0)

    def square(weight):
        weight = weight.astype(bf16)
        return jnp.pad(weight, ((0, rows - weight.shape[0]), (0, rows - weight.shape[1])))

    g0 = [w_gru[0, :, i * width : (i + 1) * width] for i in range(3)]
    g1 = [w_gru[1, :, i * width : (i + 1) * width] for i in range(3)]
    sq = [w_square[i] for i in range(3)]
    out = [w_output[:width], w_output[width:]]
    wsq = jnp.stack(
        [square(m.T) for m in [w_msg[:width]] + g0 + g1 + sq + out] + [square(m) for m in g0 + sq + out]
    )
    w_edge = jnp.pad(w_msg[width : width + edge].T.astype(bf16), ((0, rows - width), (0, 0)))
    w_time = jnp.pad(w_msg[width + edge :].T.astype(bf16), ((0, rows - width), (0, times - time_width)))
    kv_t = w_key_value.T.astype(bf16)
    pick_last = jnp.zeros((rows - width, 256), bf16).at[0, width].set(8.0).at[0, width + 1].set(1.0)

    def kv_rows(part, first):
        mem_part = jnp.pad(part[:, :width], ((0, 0), (0, 256 - width)))
        return jnp.concatenate([mem_part, pick_last if first else jnp.zeros_like(pick_last)], 0)

    wkv1 = jnp.concatenate([kv_rows(kv_t[:width], True), kv_rows(kv_t[width:], False)], 0)
    pad_time = lambda part: jnp.pad(part[:, width:], ((0, rows - width), (0, times - time_width)))
    wkv2 = jnp.concatenate([pad_time(kv_t[:width]), pad_time(kv_t[width:])], 0)
    wd = jnp.pad(w_square[3].astype(bf16), ((0, 256 - width), (0, rows - width)))
    eye = jnp.eye(256, dtype=bf16)
    freq = jnp.asarray(time_columns(time_width, times))

    packed = main(
        layout, own * nodes <= 16384, width, head_dim, slots, times,
        (flat_ids, cand_ids, positives, table, event_rows, valid, mem3, edge_feat,
         wsq, w_edge, w_time, wkv1, wkv2, wd, wd.T, eye, freq),
    )
    summed = reduce_all(own, batch, packed)

    take = partial(layout.take, summed)
    grads = (
        jnp.concatenate(
            [take("msg_mem", width, width), take("msg_edge", edge, width), take("msg_time", time_width, width)], 0
        ),
        jnp.stack([jnp.concatenate([take(f"gru{i}{g}", width, width) for g in range(3)], 1) for i in range(2)]),
        jnp.stack([take(f"square{i}", width, width) for i in range(4)]),
        jnp.concatenate(
            [
                jnp.concatenate([take("kv_mem_k", width, width), take("kv_time_k", time_width, width)], 0),
                jnp.concatenate([take("kv_mem_v", width, width), take("kv_time_v", time_width, width)], 0),
            ],
            1,
        ),
        jnp.concatenate([take("out_a", width, width), take("out_b", width, width)], 0),
    )
    step_rate = rate_coef * math.sqrt(events * own * batch)
    params = (w_msg, w_gru, w_square, w_key_value, w_output)
    moments = (mom_msg, mom_gru, mom_square, mom_key_value, mom_output)
    averages = (avg_msg, avg_gru, avg_square, avg_key_value, avg_output)
    states = [nesterov(params[i], grads[i], moments[i], averages[i], step_rate) for i in range(5)]
    return (
        (summed[layout.loss, 0], positives[0, 0], newest.reshape(-1))
        + tuple(s[0] for s in states)
        + tuple(s[1] for s in states)
        + tuple(s[2] for s in states)
    )


def solution(mesh):
    row = P(("batch", "own"))
    placed = (
        (P("own", None), P("own"), row, P(("batch", "own"), None), row, P(("batch", "own"), None))
        + (P(("batch", "own"), None, None),) * 2
        + (row,) * 3
        + (P(),) * 15
    )
    return jax.shard_map(
        local,
        mesh=mesh,
        in_specs=placed,
        out_specs=(P(), P(), P("own")) + (P(),) * 15,
        check_vma=False,
    )
```

```python
from functools import partial
import math

import jax
import jax.numpy as jnp
import numpy as np
from jax import lax
from jax.experimental import pallas as pl
from jax.experimental.pallas import tpu as pltpu
from jax.sharding import PartitionSpec as P

HEADS = 2
LANES = 256
MESH = pl.DeviceIdType.MESH
f32 = jnp.float32
bf16 = jnp.bfloat16

mu_coef = 0.9
avg_coef = 0.1
rate_coef = 0.008
mask_fill = -1e30

COS_TERMS = (
    1.0,
    -19.73920440673828,
    64.93911743164062,
    -85.45011901855469,
    60.16745376586914,
    -25.966907501220703,
    6.527653217315674,
)


def pad_to(size, step):
    return -(-size // step) * step


def nn(a, b):
    return lax.dot_general(a, b, (((1,), (0,)), ((), ())), preferred_element_type=f32)


def nt(a, b):
    return lax.dot_general(a, b, (((1,), (1,)), ((), ())), preferred_element_type=f32)


def flip_bit(index, bit):
    size = 1 << bit
    return index + size * (1 - 2 * (lax.div(index, size) % 2))


def time_columns(time_width, rows):
    turns = 10.0 ** (-np.linspace(0.0, 9.0, time_width)) / (2.0 * np.pi)
    mant, expo = np.frexp(turns)
    high = np.ldexp(np.round(mant * 4096.0) / 4096.0, expo)
    out = np.zeros((rows, 128), np.float32)
    out[:time_width, 0] = high
    out[:time_width, 1] = turns - high
    return out


def cos_rows(delta, high, low):
    turns = delta * high
    rest = turns - jnp.floor(turns + 0.5) + delta * low
    square = rest * rest
    value = square * COS_TERMS[-1] + COS_TERMS[-2]
    for term in COS_TERMS[-3::-1]:
        value = value * square + term
    return value


class Heads:
    def __init__(self, head_dim, rows):
        self.low = head_dim // 8 * 8
        self.high = pad_to(head_dim, 8)
        self.cut = head_dim - self.low
        self.rows = rows

    def split(self, lanes):
        return lax.broadcasted_iota(jnp.int32, (8, lanes), 0) < self.cut

    def sums(self, x):
        lanes = x.shape[1]
        mid = x[self.low : self.high]
        first = self.split(lanes)
        a = jnp.sum(x[: self.low].reshape(self.low // 8, 8, lanes), 0)
        b = jnp.sum(x[self.high :].reshape((self.rows - self.high) // 8, 8, lanes), 0)
        a = a + jnp.where(first, mid, 0.0)
        b = b + jnp.where(first, 0.0, mid)
        return jnp.sum(a, 0, keepdims=True), jnp.sum(b, 0, keepdims=True)

    def scale(self, x, p0, p1):
        lanes = x.shape[1]
        mid = jnp.where(self.split(lanes), p0, p1)
        return jnp.concatenate(
            [x[: self.low] * p0, x[self.low : self.high] * mid, x[self.high :] * p1], 0
        )


SQUARES = (
    "g0r g0z g0n g1r g1z g1n s0t s1t s2t g0r_back g0z_back g0n_back s0 s1 s2 oa ob".split()
)


def exchange_kernel(
    own, batch,
    mem_ref, last_ref, cand_ref, time_ref, mask_ref, src_ref, owner_ref, nbr_ref,
    msg_ref, gru_ref, square_ref, kv_ref, outw_ref,
    table_ref, ids_ref, flat_ref, pos_ref, newest_ref, mem3_ref,
    wsq_ref, wmsg_ref, wout_ref, wkv1_ref, wkv2_ref, wd_ref, wdt_ref,
    shard, ext, pairs, square_pad, wide_pad, kv_pad, batch_buf, own_buf,
    local_sem, table_send, table_recv, batch_send, batch_recv, own_send, own_recv,
):
    me = lax.axis_index("own")
    group = lax.axis_index("batch")
    barrier = pltpu.get_barrier_semaphore()
    for step in range(1, own):
        pl.semaphore_signal(barrier, inc=1, device_id=(group, lax.rem(me + step, own)), device_id_type=MESH)
    for step in range(1, batch):
        pl.semaphore_signal(barrier, inc=1, device_id=(lax.rem(group + step, batch), me), device_id_type=MESH)

    width, nodes = mem_ref.shape
    rows = pad_to(width, 16)
    ext[...] = jnp.zeros_like(ext)
    ext[0:width, :] = mem_ref[...]
    last = last_ref[...]
    ext[width : width + 1, :] = lax.div(last, 8).astype(f32)
    ext[width + 1 : width + 2, :] = lax.rem(last, 8).astype(f32)

    def turn(i, unused):
        block = ext[:, pl.ds(pl.multiple_of(i * 128, 128), 128)].T
        base = pl.multiple_of(i * 256, 256)
        pairs[pl.ds(base, 128, stride=2), :] = block[:, :128]
        pairs[pl.ds(base + 1, 128, stride=2), :] = block[:, 128:]
        return unused

    lax.fori_loop(0, nodes // 128, turn, 0)

    def pack(i, unused):
        got = [pairs[pl.ds(pl.multiple_of(i * 128, 128) + 2 * k, 2), :] for k in range(64)]
        for k in range(64):
            shard[i * 64 + k] = got[k].astype(bf16)
        return unused

    lax.fori_loop(0, nodes // 64, pack, 0)
    pl.semaphore_wait(barrier, own + batch - 2)

    half = nodes // 2
    bits = own.bit_length() - 1
    rest = list(range(1, bits))
    cut = len(rest) // 2
    orders = (rest + [0], rest[cut:] + rest[:cut] + [0])

    def shard_copy(stream, pattern, bit):
        peer = flip_bit(me, bit)
        source = me
        for b in range(bits):
            if pattern >> b & 1:
                source = flip_bit(source, b)
        part = pl.ds(pl.multiple_of(source * nodes + stream * half, half), half)
        slot = pattern | 1 << bit
        src = shard.at[pl.ds(stream * half, half)] if pattern == 0 else table_ref.at[part]
        return pltpu.make_async_remote_copy(
            src_ref=src, dst_ref=table_ref.at[part],
            send_sem=table_send.at[stream, slot], recv_sem=table_recv.at[stream, slot],
            device_id=(group, peer), device_id_type=MESH,
        )

    copies = [{}, {}]
    for step in range(bits):
        for stream in range(2):
            bit = orders[stream][step]
            copy = shard_copy(stream, 0, bit)
            copy.start()
            copies[stream][1 << bit] = copy
    mine = pltpu.make_async_copy(
        shard, table_ref.at[pl.ds(pl.multiple_of(me * nodes, nodes), nodes)], local_sem
    )
    mine.start()

    events = src_ref.shape[1]
    time_row = time_ref[...].astype(f32)
    src_row = src_ref[...]
    best = []
    tile = 256
    for start in range(0, nodes, tile):
        node = lax.broadcasted_iota(jnp.int32, (tile, 128), 0) + start
        top = jnp.full((tile, 128), -1.0, f32)
        for lane in range(0, events, 128):
            hit = src_row[:, lane : lane + 128] == node
            top = jnp.maximum(top, jnp.where(hit, time_row[:, lane : lane + 128], -1.0))
        best.append(jnp.max(top.T, 0, keepdims=True))
    newest = jnp.concatenate(best, 1).astype(jnp.int32)
    newest = jnp.maximum(newest, last)
    count = jnp.sum(mask_ref[...].astype(f32), 1, keepdims=True).astype(jnp.int32)
    batch_buf[0, 0:1, :] = newest
    batch_buf[0, 1:2, :] = jnp.broadcast_to(count, (1, nodes))

    def peer_copy(step):
        return pltpu.make_async_remote_copy(
            src_ref=batch_buf.at[0], dst_ref=batch_buf.at[step],
            send_sem=batch_send.at[step], recv_sem=batch_recv.at[step],
            device_id=(lax.rem(group + step, batch), me), device_id_type=MESH,
        )

    peers = [peer_copy(step) for step in range(1, batch)]
    for copy in peers:
        copy.start()

    picks = owner_ref.shape[0]
    per_pick = nbr_ref.shape[0]
    for s in range(per_pick):
        flat = owner_ref[...] * nodes + nbr_ref[s]
        for block in range(events // 128):
            at = (s * (events // 128) + block) * picks
            flat_ref[at : at + picks, :] = flat[:, block * 128 : block * 128 + 128]
    whole = ext[0:rows, :]
    part0 = whole.astype(bf16)
    whole = whole - part0.astype(f32)
    part1 = whole.astype(bf16)
    mem3_ref[0:rows, :] = part0
    mem3_ref[rows : 2 * rows, :] = part1
    mem3_ref[2 * rows :, :] = (whole - part1.astype(f32)).astype(bf16)

    square_pad[...] = jnp.zeros_like(square_pad)

    def put(name, value):
        square_pad[0:width, 0:width] = value
        wsq_ref[SQUARES.index(name)] = square_pad[...].astype(bf16)

    for index in range(2):
        for gate, letter in enumerate("rzn"):
            value = gru_ref[:, index, gate * width : gate * width + width]
            put(f"g{index}{letter}", value.T)
            if index == 0:
                put(f"g0{letter}_back", value)
    for index in range(3):
        value = square_ref[:, index, :]
        put(f"s{index}", value)
        put(f"s{index}t", value.T)
    put("oa", outw_ref[:, 0:width].T)
    put("ob", outw_ref[:, width : 2 * width].T)
    wide_pad[...] = jnp.zeros_like(wide_pad)
    wide_pad[0:width, 0 : 2 * width] = outw_ref[...]
    wout_ref[...] = wide_pad[:, 0 : wout_ref.shape[1]].astype(bf16)
    wide_pad[0:width, 0 : msg_ref.shape[1]] = msg_ref[...]
    wmsg_ref[...] = wide_pad[...].astype(bf16)
    last_square = square_ref[:, 3, :]
    kv_pad[...] = jnp.zeros_like(kv_pad)
    kv_pad[0:width, 0:width] = last_square
    wd_ref[...] = kv_pad[0 : wd_ref.shape[0], 0 : wd_ref.shape[1]].astype(bf16)
    kv_pad[0:width, 0:width] = last_square.T
    wdt_ref[...] = kv_pad[0 : wdt_ref.shape[0], 0 : wdt_ref.shape[1]].astype(bf16)
    times = wkv2_ref.shape[1]
    time_width = kv_ref.shape[0] - width
    lane = lax.broadcasted_iota(jnp.int32, (1, 256), 1)
    for index in range(2):
        part = kv_ref[:, index * width : index * width + width]
        kv_pad[index * rows : index * rows + width, 0:width] = part[0:width].T
    kv_pad[width : width + 1, :] = jnp.where(lane == width, 8.0, jnp.where(lane == width + 1, 1.0, 0.0))
    wkv1_ref[...] = kv_pad[...].astype(bf16)
    kv_pad[...] = jnp.zeros_like(kv_pad)
    for index in range(2):
        part = kv_ref[:, index * width : index * width + width]
        kv_pad[index * rows : index * rows + width, 0:time_width] = part[width:].T
    wkv2_ref[...] = kv_pad[:, 0:times].astype(bf16)

    total = count
    for step, copy in enumerate(peers, 1):
        copy.wait_recv()
        newest = jnp.maximum(newest, batch_buf[step, 0:1, :])
        total = total + batch_buf[step, 1:2, 0:1]
    newest_ref[...] = newest

    cands = cand_ref.shape[1]
    own_buf[0, 0:1, :] = cand_ref[...] + me * nodes
    own_buf[0, 1:2, :] = jnp.broadcast_to(total, (1, cands))

    def owner_copy(step):
        return pltpu.make_async_remote_copy(
            src_ref=own_buf.at[0], dst_ref=own_buf.at[step],
            send_sem=own_send.at[step], recv_sem=own_recv.at[step],
            device_id=(group, lax.rem(me + step, own)), device_id_type=MESH,
        )

    owners = [owner_copy(step) for step in range(1, own)]
    for copy in owners:
        copy.start()

    for step in range(bits):
        for stream in range(2):
            order = orders[stream]
            held = [0]
            for bit in order[:step]:
                held = held + [p | 1 << bit for p in held]
            for pattern in held:
                slot = pattern | 1 << order[step]
                copies[stream][slot].wait_recv()
                for bit in order[step + 1 :]:
                    copy = shard_copy(stream, slot, bit)
                    copy.start()
                    copies[stream][slot | 1 << bit] = copy

    for step in range(own):
        if step:
            owners[step - 1].wait_recv()
            total = total + own_buf[step, 1:2, 0:1]
        source = lax.rem(me - step + own, own)
        for block in range(cands // 128):
            ids_ref[pl.ds(source * (cands // 128) + block, 1), :] = own_buf[
                step, 0:1, block * 128 : block * 128 + 128
            ]
    pos_ref[...] = jnp.broadcast_to(jnp.maximum(total.astype(f32), 1.0), pos_ref.shape)
    mine.wait()
    for copy in peers + owners:
        copy.wait_send()
    for stream in range(2):
        for slot in copies[stream]:
            copies[stream][slot].wait_send()


def exchange(own, batch, args):
    mem, last, cand, time, mask, src, owner, nbr, msg, gru, square, kv, outw = args
    width, nodes = mem.shape
    events = src.shape[1]
    cands = cand.shape[1]
    rows = pad_to(width, 16)
    times = pad_to(kv.shape[0] - width, 16)
    wide = pad_to(msg.shape[1], 16)
    vmem = pl.BlockSpec(memory_space=pltpu.VMEM)
    hbm = pl.BlockSpec(memory_space=pl.ANY)
    low = lambda *shape: jax.ShapeDtypeStruct(shape, bf16)
    whole = lambda *shape: jax.ShapeDtypeStruct(shape, jnp.int32)
    return pl.pallas_call(
        partial(exchange_kernel, own, batch),
        out_shape=(
            low(own * nodes, 2, 128),
            whole(own * cands // 128, 128),
            whole(nbr.shape[0] * nbr.shape[1] * events // 128, 128),
            jax.ShapeDtypeStruct((8, 128), f32),
            whole(1, nodes),
            low(3 * rows, nodes),
            low(len(SQUARES), rows, rows),
            low(rows, wide),
            low(rows, 2 * rows),
            low(2 * rows, 256),
            low(2 * rows, times),
            low(256, rows),
            low(rows, 256),
        ),
        in_specs=[vmem] * len(args),
        out_specs=(hbm,) + (vmem,) * 12,
        scratch_shapes=[
            pltpu.VMEM((nodes, 2, 128), bf16),
            pltpu.VMEM((256, nodes), f32),
            pltpu.VMEM((2 * nodes, 128), f32),
            pltpu.VMEM((rows, rows), f32),
            pltpu.VMEM((rows, wide), f32),
            pltpu.VMEM((2 * rows, 256), f32),
            pltpu.VMEM((batch, 8, nodes), jnp.int32),
            pltpu.VMEM((own, 8, cands), jnp.int32),
            pltpu.SemaphoreType.DMA,
            pltpu.SemaphoreType.DMA((2, own)),
            pltpu.SemaphoreType.DMA((2, own)),
            pltpu.SemaphoreType.DMA((batch,)),
            pltpu.SemaphoreType.DMA((batch,)),
            pltpu.SemaphoreType.DMA((own,)),
            pltpu.SemaphoreType.DMA((own,)),
        ],
        compiler_params=pltpu.CompilerParams(
            collective_id=1, has_side_effects=True, vmem_limit_bytes=63 * 2**20
        ),
        name="exchange",
    )(*args)


class Layout:
    def __init__(self, width, wide, deep, gates, kv_rows, kv_cols, fold):
        rows = pad_to(width, 8)
        self.width = width
        self.pieces = {}
        row = 0
        for name, depth, columns in (
            ("msg", width, wide),
            ("out", width, deep),
            ("kv", kv_rows, kv_cols),
            ("gru0", width, gates),
            ("gru1", width, gates),
            ("square0", width, width),
            ("square1", width, width),
            ("square2", width, width),
            ("square3", width, width),
        ):
            tiles = []
            for column in range(0, columns, 128):
                size = min(128, columns - column)
                if size < 128 and name[:3] in ("gru", "squ"):
                    tiles.append([column, size, None, None])
                else:
                    tiles.append([column, size, row, 0])
                    row += pad_to(depth, 8)
            self.pieces[name] = (depth, tiles)
        host = self.pieces["msg"][1][-1]
        lane = pad_to(host[1], 8)
        for name in ("gru0", "gru1"):
            tile = self.pieces[name][1][-1]
            if tile[2] is None:
                assert lane + tile[1] <= 128
                tile[2:] = [host[2], lane]
                lane += tile[1]
        for pair in range(2):
            for side in range(2):
                tile = self.pieces[f"square{2 * pair + side}"][1][-1]
                assert tile[1] <= 64
                tile[2:] = [row, 64 * side]
            row += rows
        self.loss = row
        row += 8
        self.total = pad_to(row, fold)

    def put(self, ref, name, value):
        depth, tiles = self.pieces[name]
        for column, size, row, lane in tiles:
            ref[row : row + depth, lane : lane + size] = value[:depth, column : column + size]

    def tiles(self, ref, name):
        depth, tiles = self.pieces[name]
        for column, size, row, lane in tiles:
            yield slice(column, column + size), ref[row : row + depth, lane : lane + size]


def main_kernel(
    dims,
    ids_ref, cand_ref, pos_ref, table_ref, time_ref, mask_ref, src_ref, target_ref, valid_ref, mem3_ref, edge_ref,
    wsq_ref, wmsg_ref, wout_ref, wkv1_ref, wkv2_ref, wd_ref, wdt_ref, freq_ref,
    grad_ref,
    xs, x_all, t_all, kv_all, score, dest_rows, slab, eye_ref, stage,
    x_msg, mem_low, hidden, fresh_low, att_low, x_out, hid_out, emb, emb_rows,
    mem_src, pre_msg, reset_gate, update, cand_act, gate_n, queries, attended, pre_out,
    acc_a, grad_att, gkv_m, gkv_t, rows_ref,
):
    width, head_dim, keep_kv, cand_width, layout = dims
    events = time_ref.shape[1]
    per_pick, picks = valid_ref.shape[:2]
    slots = per_pick * picks
    rows = pad_to(width, 16)
    times = wkv2_ref.shape[1]
    wide = wmsg_ref.shape[1]
    time_width = layout.pieces["kv"][0] - width
    edge = edge_ref.shape[0]
    heads = Heads(head_dim, rows)
    scale = head_dim ** (-0.5)
    high, low = freq_ref[:, 0:1], freq_ref[:, 1:2]
    chunks = events // LANES
    owners = cand_ref.shape[0] // cand_width

    def w(name):
        return wsq_ref[SQUARES.index(name)]

    def gather(read_id, count):
        unroll = 128

        def body(i, unused):
            base = i * unroll
            first = read_id(i)
            got = [table_ref[first(k)] for k in range(unroll)]
            for k in range(unroll):
                xs[pl.ds(pl.multiple_of(2 * base, 2 * unroll) + 2 * k, 2), :] = got[k].astype(f32)
            return unused

        lax.fori_loop(0, count // unroll, body, 0)

    def gathered(start, count):
        base = pl.multiple_of(2 * start, 2 * count)
        return jnp.concatenate(
            [xs[pl.ds(base, count, stride=2), :], xs[pl.ds(base + 1, count, stride=2), :]], 1
        ).astype(bf16)

    grad_ref[layout.loss :, :] = jnp.zeros_like(grad_ref[layout.loss :, :])
    host = layout.pieces["msg"][1][-1][2]
    grad_ref[host : host + rows, :] = jnp.zeros((rows, 128), f32)
    eye = lax.broadcasted_iota(jnp.int32, (256, 256), 0) == lax.broadcasted_iota(jnp.int32, (256, 256), 1)
    eye_ref[...] = eye.astype(f32).astype(bf16)
    stage[...] = jnp.zeros_like(stage)

    def cand_body(o, unused):
        gather(lambda i: lambda k: cand_ref[o * cand_width + i * 128 + k], cand_width)
        at = pl.multiple_of(o * cand_width, cand_width)
        dest_rows[pl.ds(at, cand_width), :] = gathered(0, cand_width)
        return unused

    lax.fori_loop(0, owners, cand_body, 0)

    def lanes(c, size=LANES):
        return pl.ds(pl.multiple_of(c * size, size), size)

    def gru_body(c, unused):
        cs = lanes(c)
        node = lax.broadcasted_iota(jnp.int32, (mem3_ref.shape[1], LANES), 0)
        onehot = (node == src_ref[:, cs]).astype(f32).astype(bf16)
        parts = nn(mem3_ref[...], onehot)
        mem = parts[:rows] + parts[rows : 2 * rows] + parts[2 * rows :]
        mem_src[:, cs] = mem
        delta = time_ref[:, cs].astype(f32) - 8.0 * mem[width : width + 1] - mem[width + 1 : width + 2]
        stage[0:width, :] = mem[0:width]
        stage[width : width + edge, :] = edge_ref[:, cs].astype(f32)
        stage[width + edge : width + edge + time_width, :] = cos_rows(delta, high, low)[0:time_width]
        x = stage[...].astype(bf16)
        x_msg[:, cs] = x
        m_low = mem.astype(bf16)
        mem_low[:, cs] = m_low
        pre = nn(wmsg_ref[...], x)
        pre_msg[:, cs] = pre
        hid = (pre * jax.nn.sigmoid(pre)).astype(bf16)
        hidden[:, cs] = hid
        r = jax.nn.sigmoid(nn(w("g0r"), hid) + nn(w("g1r"), m_low))
        reset_gate[:, cs] = r
        u = jax.nn.sigmoid(nn(w("g0z"), hid) + nn(w("g1z"), m_low))
        update[:, cs] = u
        gn = nn(w("g1n"), m_low)
        gate_n[:, cs] = gn
        cand = jnp.tanh(nn(w("g0n"), hid) + r * gn)
        cand_act[:, cs] = cand
        fresh = ((1.0 - u) * cand + u * mem).astype(bf16)
        fresh_low[:, cs] = fresh
        queries[:, cs] = nn(w("s0t"), fresh).astype(bf16)
        return unused

    lax.fori_loop(0, chunks, gru_body, 0)

    def slot_body(j, unused):
        pick = lax.rem(j, picks)
        round_ = lax.div(j, picks)

        def first(i):
            base = ((round_ * (events // 128) + i) * picks + pick) * 128
            return lambda k: ids_ref[base + k]

        gather(first, events)

        def chunk_body(c, unused):
            cs = lanes(c)
            x = gathered(c * LANES, LANES)
            x_all[j, cs, :] = x
            kv = nt(wkv1_ref[...], x)
            delta = time_ref[:, cs].astype(f32) - kv[width : width + 1]
            t_low = cos_rows(delta, high, low).astype(bf16)
            t_all[j, :, cs] = t_low
            kv = (kv + nn(wkv2_ref[...], t_low)).astype(bf16)
            if keep_kv:
                kv_all[j, :, cs] = kv
            s0, s1 = heads.sums(kv[:rows].astype(f32) * queries[:, cs].astype(f32))
            live = valid_ref[round_, pl.ds(pick, 1), cs] > 0
            score[j, 0:1, cs] = jnp.where(live, s0 * scale, mask_fill)
            score[j, 1:2, cs] = jnp.where(live, s1 * scale, mask_fill)
            return unused

        lax.fori_loop(0, chunks, chunk_body, 0, unroll=True)
        return unused

    lax.fori_loop(0, slots, slot_body, 0)

    def soft_body(c, unused):
        cs = lanes(c, 128)
        s = score[:, 0:2, cs]
        top = jnp.max(s, 0, keepdims=True)
        p = jnp.where(s > 0.5 * mask_fill, jnp.exp(s - top), 0.0)
        score[:, 0:2, cs] = p / jnp.sum(p, 0, keepdims=True)
        return unused

    lax.fori_loop(0, events // 128, soft_body, 0)

    def kv_of(j, cs, part):
        if keep_kv:
            return kv_all[j, part, cs]
        return (nt(wkv1_ref[part, :], x_all[j, cs, :]) + nn(wkv2_ref[part, :], t_all[j, :, cs])).astype(bf16)

    def att_body(c, unused):
        cs = lanes(c, 128)

        def add(j, total):
            v = kv_of(j, cs, slice(rows, 2 * rows)).astype(f32)
            return total + heads.scale(v, score[j, 0:1, cs], score[j, 1:2, cs])

        att = lax.fori_loop(0, slots, add, jnp.zeros((rows, 128), f32))
        attended[:, cs] = att
        att_low[:, cs] = att.astype(bf16)
        return unused

    lax.fori_loop(0, events // 128, att_body, 0)

    def out_body(c, unused):
        cs = lanes(c)
        stage[0:width, :] = nn(w("s1t"), att_low[:, cs])[0:width]
        stage[width : 2 * width, :] = fresh_low[:, cs].astype(f32)[0:width]
        x = stage[0 : 2 * rows, :].astype(bf16)
        x_out[:, cs] = x
        pre = nn(wout_ref[...], x)
        pre_out[:, cs] = pre
        hid = (pre * jax.nn.sigmoid(pre)).astype(bf16)
        hid_out[:, cs] = hid
        e = nn(w("s2t"), hid).astype(bf16)
        emb[:, cs] = e
        emb_rows[cs, :] = nt(eye_ref[...], e).astype(bf16)
        return unused

    lax.fori_loop(0, chunks, out_body, 0)

    def row_init(c, unused):
        cs = lanes(c)
        rows_ref[0:1, cs] = jnp.full((1, LANES), mask_fill, f32)
        rows_ref[1:3, cs] = jnp.zeros((2, LANES), f32)
        acc_a[:, cs] = jnp.zeros((rows, LANES), f32)
        return unused

    lax.fori_loop(0, chunks, row_init, 0)

    def dest_of(o):
        at = pl.multiple_of(o * cand_width, cand_width)
        return dest_rows[pl.ds(at, cand_width), :]

    def lse_block(o, unused):
        dest = nn(dest_of(o), wd_ref[...]).astype(bf16)

        def chunk(c, unused):
            cs = lanes(c)
            logits = nn(dest, emb[:, cs])
            old = rows_ref[0:1, cs]
            top = jnp.maximum(old, jnp.max(logits, 0, keepdims=True))
            rows_ref[0:1, cs] = top
            rows_ref[1:2, cs] = rows_ref[1:2, cs] * jnp.exp(old - top) + jnp.sum(
                jnp.exp(logits - top), 0, keepdims=True
            )
            hit = lax.broadcasted_iota(jnp.int32, logits.shape, 0) == target_ref[:, cs] - o * cand_width
            rows_ref[2:3, cs] = rows_ref[2:3, cs] + jnp.sum(jnp.where(hit, logits, 0.0), 0, keepdims=True)
            return unused

        lax.fori_loop(0, chunks, chunk, 0, unroll=True)
        return unused

    lax.fori_loop(0, owners, lse_block, 0)

    mask_row = mask_ref[...].astype(f32)
    log_sum = rows_ref[0:1, :] + jnp.log(rows_ref[1:2, :])
    rows_ref[3:4, :] = log_sum
    rows_ref[4:5, :] = mask_row / jnp.broadcast_to(pos_ref[0:1, 0:1], mask_row.shape)
    loss = jnp.sum(mask_row * (log_sum - rows_ref[2:3, :]), 1, keepdims=True)
    grad_ref[layout.loss : layout.loss + 8, :] = jnp.broadcast_to(loss, (8, 128))

    def back_block(o, grad_dest_w):
        block = dest_of(o)
        dest = nn(block, wd_ref[...]).astype(bf16)
        dest_t = nt(wdt_ref[...], block).astype(bf16)
        block_t = nt(eye_ref[...], block).astype(bf16)

        def chunk(c, unused):
            cs = lanes(c)
            logits = nn(dest, emb[:, cs])
            coeff = rows_ref[4:5, cs]
            hit = lax.broadcasted_iota(jnp.int32, logits.shape, 0) == target_ref[:, cs] - o * cand_width
            grad = jnp.exp(logits - rows_ref[3:4, cs]) - jnp.where(hit, 1.0, 0.0)
            grad = (grad * coeff).astype(bf16)
            slab[0:cand_width, cs] = grad
            acc_a[:, cs] += nn(dest_t, grad)
            return unused

        lax.fori_loop(0, chunks, chunk, 0, unroll=True)
        grad_dest = nn(slab[0:cand_width, :], emb_rows[...]).astype(bf16)
        return grad_dest_w + nn(block_t, grad_dest)[:rows]

    grad_dest_w = lax.fori_loop(0, owners, back_block, jnp.zeros((rows, rows), f32))
    layout.put(grad_ref, "square3", grad_dest_w)

    r0, r1, r2 = slice(0, rows), slice(rows, 2 * rows), slice(2 * rows, 3 * rows)

    def out_back(c, unused):
        cs = lanes(c)
        ge = acc_a[:, cs].astype(bf16)
        slab[r0, cs] = ge
        pre = pre_out[:, cs]
        sig = jax.nn.sigmoid(pre)
        gp = (nn(w("s2"), ge) * (sig * (1.0 + pre * (1.0 - sig)))).astype(bf16)
        slab[r1, cs] = gp
        gm = nn(w("oa"), gp).astype(bf16)
        slab[r2, cs] = gm
        acc_a[:, cs] = nn(w("ob"), gp)
        ga = nn(w("s1"), gm).astype(bf16)
        grad_att[:, cs] = ga
        d0, d1 = heads.sums(ga.astype(f32) * attended[:, cs])
        rows_ref[5:6, cs] = d0
        rows_ref[6:7, cs] = d1
        return unused

    lax.fori_loop(0, chunks, out_back, 0)
    layout.put(grad_ref, "square2", nt(hid_out[...], slab[r0, :]))
    layout.put(grad_ref, "out", nt(slab[r1, :], x_out[...]))
    layout.put(grad_ref, "square1", nt(att_low[...], slab[r2, :]))

    attended[...] = jnp.zeros_like(attended)
    gkv_m[...] = jnp.zeros_like(gkv_m)
    gkv_t[...] = jnp.zeros_like(gkv_t)

    def slot_back(j, unused):
        def chunk(c, unused):
            cs = lanes(c, 128)
            kv = kv_of(j, cs, slice(0, 2 * rows)).astype(f32)
            ga = grad_att[:, cs].astype(f32)
            p0, p1 = score[j, 0:1, cs], score[j, 1:2, cs]
            g0, g1 = heads.sums(ga * kv[rows:])
            g0 = p0 * (g0 - rows_ref[5:6, cs]) * scale
            g1 = p1 * (g1 - rows_ref[6:7, cs]) * scale
            attended[:, cs] += heads.scale(kv[:rows], g0, g1)
            slab[r0, cs] = heads.scale(queries[:, cs].astype(f32), g0, g1).astype(bf16)
            slab[r1, cs] = heads.scale(ga, p0, p1).astype(bf16)
            return unused

        lax.fori_loop(0, events // 128, chunk, 0)
        both = slab[0 : 2 * rows, :]
        gkv_m[...] += nn(both, x_all[j])
        gkv_t[...] += nt(both, t_all[j])
        return unused

    lax.fori_loop(0, slots, slot_back, 0)
    gm = gkv_m[...].T
    gt = gkv_t[...].T
    both = [jnp.concatenate([g[:depth, :width], g[:depth, rows : rows + width]], 1)
            for g, depth in ((gm, width), (gt, time_width))]
    layout.put(grad_ref, "kv", jnp.concatenate(both, 0))

    def gru_back(c, unused):
        cs = lanes(c)
        gq = attended[:, cs].astype(bf16)
        slab[r0, cs] = gq
        gf = acc_a[:, cs] + nn(w("s0"), gq)
        u, cand, r = update[:, cs], cand_act[:, cs], reset_gate[:, cs]
        act = gf * (1.0 - u) * (1.0 - cand * cand)
        gr = (act * gate_n[:, cs] * r * (1.0 - r)).astype(bf16)
        gu = (gf * (mem_src[:, cs] - cand) * u * (1.0 - u)).astype(bf16)
        gn = act.astype(bf16)
        gh = (act * r).astype(bf16)
        slab[r1, cs] = gr
        slab[r2, cs] = gu
        x_out[0:rows, cs] = gn
        hid_out[:, cs] = gh
        pre = pre_msg[:, cs]
        sig = jax.nn.sigmoid(pre)
        back = nn(w("g0r_back"), gr) + nn(w("g0z_back"), gu) + nn(w("g0n_back"), gn)
        att_low[:, cs] = (back * (sig * (1.0 + pre * (1.0 - sig)))).astype(bf16)
        return unused

    lax.fori_loop(0, chunks, gru_back, 0)
    layout.put(grad_ref, "square0", nt(fresh_low[...], slab[r0, :]))
    for index, (left, last) in enumerate(((hidden, x_out[0:rows, :]), (mem_low, hid_out[...]))):
        left = left[...]
        parts = [nt(left, slab[r1, :]), nt(left, slab[r2, :]), nt(left, last)]
        layout.put(grad_ref, f"gru{index}", jnp.concatenate([p[:, :width] for p in parts], 1))
    layout.put(grad_ref, "msg", nt(att_low[...], x_msg[...]))


def main(layout, keep_kv, width, head_dim, cand_width, args):
    events = args[4].shape[1]
    slots = args[8].shape[0] * args[8].shape[1]
    wide = args[12].shape[1]
    times = args[15].shape[1]
    rows = pad_to(width, 16)
    cands = args[1].shape[0]
    smem = pl.BlockSpec(memory_space=pltpu.SMEM)
    vmem = pl.BlockSpec(memory_space=pltpu.VMEM)
    low = lambda *shape: pltpu.VMEM(shape, bf16)
    full = lambda *shape: pltpu.VMEM(shape, f32)
    return pl.pallas_call(
        partial(main_kernel, (width, head_dim, keep_kv, cand_width, layout)),
        out_shape=jax.ShapeDtypeStruct((layout.total, 128), f32),
        in_specs=[smem, smem] + [vmem] * (len(args) - 2),
        out_specs=vmem,
        scratch_shapes=[
            full(2 * events, 128),
            low(slots, events, 256),
            low(slots, times, events),
            low(slots if keep_kv else 1, 2 * rows if keep_kv else 16, events),
            full(slots, 8, events),
            low(cands, 256),
            low(max(3 * rows, cand_width), events),
            low(256, 256),
            full(wide, LANES),
            low(wide, events),
        ]
        + [low(rows, events)] * 4
        + [low(2 * rows, events)]
        + [low(rows, events)] * 2
        + [low(events, rows)]
        + [full(rows, events)] * 6
        + [low(rows, events)]
        + [full(rows, events)] * 3
        + [low(rows, events), full(2 * rows, 256), full(2 * rows, times), full(8, events)],
        compiler_params=pltpu.CompilerParams(vmem_limit_bytes=63 * 2**20),
        name="train",
    )(*args)


def reduce_kernel(own, batch, streams, grad_ref, out_ref, acc, recv, send_sem, recv_sem):
    place = {"own": lax.axis_index("own"), "batch": lax.axis_index("batch")}

    def peer(axis, bit):
        moved = dict(place)
        moved[axis] = flip_bit(place[axis], bit)
        return (moved["batch"], moved["own"])

    barrier = pltpu.get_barrier_semaphore()
    steps = streams[0][2]
    for axis, bit in steps:
        pl.semaphore_signal(barrier, inc=1, device_id=peer(axis, bit), device_id_type=MESH)
    pl.semaphore_wait(barrier, len(steps))

    base = [start for start, size, order in streams]
    sizes = [size for start, size, order in streams]
    inner = [start for start, size, order in streams]
    sent = []
    for step in range(len(steps)):
        source = grad_ref if step == 0 else acc
        copies = []
        for s, (start, size, order) in enumerate(streams):
            axis, bit = order[step]
            half = sizes[s] // 2
            mine = lax.div(place[axis], 1 << bit) % 2
            away = pl.multiple_of(base[s] + (1 - mine) * half, 8)
            copy = pltpu.make_async_remote_copy(
                src_ref=source.at[pl.ds(away, half), :],
                dst_ref=recv.at[pl.ds(inner[s], half), :],
                send_sem=send_sem.at[s, step], recv_sem=recv_sem.at[s, step],
                device_id=peer(axis, bit), device_id_type=MESH,
            )
            copy.start()
            copies.append(copy)
            base[s] = pl.multiple_of(base[s] + mine * half, 8)
            sizes[s] = half
        last = step == len(steps) - 1
        target = out_ref if last else acc
        for s, copy in enumerate(copies):
            copy.wait_recv()
            part = pl.ds(base[s], sizes[s])
            target[part, :] = source[part, :] + recv[pl.ds(inner[s], sizes[s]), :]
            inner[s] += sizes[s]
        sent += copies
    for step in reversed(range(len(steps))):
        copies = []
        for s, (start, size, order) in enumerate(streams):
            axis, bit = order[step]
            part = pl.ds(base[s], sizes[s])
            copy = pltpu.make_async_remote_copy(
                src_ref=out_ref.at[part, :], dst_ref=out_ref.at[part, :],
                send_sem=send_sem.at[s, step + len(steps)], recv_sem=recv_sem.at[s, step + len(steps)],
                device_id=peer(axis, bit), device_id_type=MESH,
            )
            copy.start()
            copies.append(copy)
            mine = lax.div(place[axis], 1 << bit) % 2
            base[s] = pl.multiple_of(base[s] - mine * sizes[s], 8)
            sizes[s] *= 2
        for copy in copies:
            copy.wait_recv()
        sent += copies
    for copy in sent:
        copy.wait_send()


def reduce_all(own, batch, packed):
    total = packed.shape[0]
    own_bits = own.bit_length() - 1
    batch_bits = batch.bit_length() - 1
    fold = 8 << (own_bits + batch_bits)
    rest = [("own", b) for b in range(1, own_bits)]
    cut = len(rest) // 2
    tail = [("batch", b) for b in range(batch_bits)]
    blocks = total // fold
    first = (blocks + 1) // 2 * fold
    streams = (
        (0, first, [("own", 0)] + rest + tail),
        (first, total - first, [("own", 0)] + rest[cut:] + rest[:cut] + tail),
    )
    count = 2 * (own_bits + batch_bits)
    return pl.pallas_call(
        partial(reduce_kernel, own, batch, streams),
        out_shape=jax.ShapeDtypeStruct(packed.shape, f32),
        in_specs=[pl.BlockSpec(memory_space=pltpu.VMEM)],
        out_specs=pl.BlockSpec(memory_space=pltpu.VMEM),
        scratch_shapes=[
            pltpu.VMEM(packed.shape, f32),
            pltpu.VMEM(packed.shape, f32),
            pltpu.SemaphoreType.DMA((2, count)),
            pltpu.SemaphoreType.DMA((2, count)),
        ],
        compiler_params=pltpu.CompilerParams(
            collective_id=2, has_side_effects=True, vmem_limit_bytes=63 * 2**20
        ),
        name="reduce",
    )(packed)


def update_kernel(layout, step_rate, grad_ref, *refs):
    weights, moments, averages, new_moments, new_weights, new_averages = (refs[5 * i : 5 * i + 5] for i in range(6))

    def step(index, at, gradient):
        moment = mu_coef * moments[index][at] + gradient
        weight = weights[index][at] - step_rate * (gradient + mu_coef * moment)
        new_moments[index][at] = moment
        new_weights[index][at] = weight
        new_averages[index][at] = (1.0 - avg_coef) * averages[index][at] + avg_coef * weight

    for index, name in ((0, "msg"), (3, "kv"), (4, "out")):
        for columns, gradient in layout.tiles(grad_ref, name):
            step(index, (slice(None), columns), gradient)
    for part in range(2):
        for columns, gradient in layout.tiles(grad_ref, f"gru{part}"):
            step(1, (slice(None), part, columns), gradient)
    for part in range(4):
        for columns, gradient in layout.tiles(grad_ref, f"square{part}"):
            step(2, (slice(None), part, columns), gradient)


def update_all(layout, step_rate, packed, params):
    vmem = pl.BlockSpec(memory_space=pltpu.VMEM)
    shapes = tuple(jax.ShapeDtypeStruct(p.shape, f32) for p in params)
    return pl.pallas_call(
        partial(update_kernel, layout, step_rate),
        out_shape=shapes,
        in_specs=[vmem] * (len(params) + 1),
        out_specs=(vmem,) * len(params),
        compiler_params=pltpu.CompilerParams(vmem_limit_bytes=63 * 2**20),
        name="update",
    )(packed, *params)


def turned(arrays):
    msg, gru, square, kv, out = arrays
    return (msg.T, gru.transpose(1, 0, 2), square.transpose(1, 0, 2), kv, out.T)


def local(
    memory, last_update, src_local, edge_feat, event_time, nbr_owner, nbr_ids, nbr_mask, event_mask,
    dest_local, target, w_msg, w_gru, w_square, w_key_value, w_output,
    mom_msg, mom_gru, mom_square, mom_key_value, mom_output,
    avg_msg, avg_gru, avg_square, avg_key_value, avg_output,
):
    own = lax.axis_size("own")
    batch = lax.axis_size("batch")
    events, edge = edge_feat.shape
    nodes, width = memory.shape
    head_dim = width // HEADS
    time_width = w_key_value.shape[0] - width
    times = pad_to(time_width, 16)
    layout = Layout(
        width, w_msg.shape[0], w_output.shape[0], w_gru.shape[2], *w_key_value.shape, 8 * own * batch
    )
    weights = turned((w_msg, w_gru, w_square, w_key_value, w_output))
    time_row, mask_row, src_row, target_row = (x[None, :] for x in (event_time, event_mask, src_local, target))
    table, cand_ids, flat_ids, positives, newest, mem3, *low_weights = exchange(
        own, batch,
        (memory.T, last_update[None, :], dest_local[None, :], time_row, mask_row, src_row,
         nbr_owner.T, nbr_ids.transpose(2, 1, 0)) + weights,
    )
    packed = main(
        layout, own * nodes <= 16384, width, head_dim, dest_local.shape[0],
        (flat_ids.reshape(-1), cand_ids.reshape(-1), positives, table, time_row, mask_row, src_row, target_row,
         nbr_mask.transpose(2, 1, 0), mem3, edge_feat.T, *low_weights, jnp.asarray(time_columns(time_width, times))),
    )
    summed = reduce_all(own, batch, packed)
    step_rate = rate_coef * math.sqrt(events * own * batch)
    states = update_all(
        layout, step_rate, summed,
        weights
        + turned((mom_msg, mom_gru, mom_square, mom_key_value, mom_output))
        + turned((avg_msg, avg_gru, avg_square, avg_key_value, avg_output)),
    )
    states = [x for i in range(3) for x in turned(states[5 * i : 5 * i + 5])]
    return (summed[layout.loss, 0], positives[0, 0], newest.reshape(-1), *states)


def solution(mesh):
    row = P(("batch", "own"))
    placed = (
        (P("own", None), P("own"), row, P(("batch", "own"), None), row, P(("batch", "own"), None))
        + (P(("batch", "own"), None, None),) * 2
        + (row,) * 3
        + (P(),) * 15
    )
    return jax.shard_map(
        local,
        mesh=mesh,
        in_specs=placed,
        out_specs=(P(), P(), P("own")) + (P(),) * 15,
        check_vma=False,
    )
```

```python
from functools import partial
import math

import jax
import jax.numpy as jnp
import numpy as np
from jax import lax
from jax.experimental import pallas as pl
from jax.experimental.pallas import tpu as pltpu
from jax.sharding import PartitionSpec as P

HEADS = 2
LANES = 256
MESH = pl.DeviceIdType.MESH
f32 = jnp.float32
bf16 = jnp.bfloat16

mu_coef = 0.9
avg_coef = 0.1
rate_coef = 0.008
mask_fill = -1e30

COS_TERMS = (
    1.0,
    -19.73920440673828,
    64.93911743164062,
    -85.45011901855469,
    60.16745376586914,
    -25.966907501220703,
    6.527653217315674,
)


def pad_to(size, step):
    return -(-size // step) * step


def nn(a, b):
    return lax.dot_general(a, b, (((1,), (0,)), ((), ())), preferred_element_type=f32)


def nt(a, b):
    return lax.dot_general(a, b, (((1,), (1,)), ((), ())), preferred_element_type=f32)


def flip_bit(index, bit):
    size = 1 << bit
    return index + size * (1 - 2 * (lax.div(index, size) % 2))


def time_columns(time_width, rows):
    turns = 10.0 ** (-np.linspace(0.0, 9.0, time_width)) / (2.0 * np.pi)
    mant, expo = np.frexp(turns)
    high = np.ldexp(np.round(mant * 4096.0) / 4096.0, expo)
    out = np.zeros((rows, 128), np.float32)
    out[:time_width, 0] = high
    out[:time_width, 1] = turns - high
    return out


def cos_rows(delta, high, low):
    turns = delta * high
    rest = turns - jnp.floor(turns + 0.5) + delta * low
    square = rest * rest
    value = square * COS_TERMS[-1] + COS_TERMS[-2]
    for term in COS_TERMS[-3::-1]:
        value = value * square + term
    return value


class Heads:
    def __init__(self, head_dim, rows):
        self.low = head_dim // 8 * 8
        self.high = pad_to(head_dim, 8)
        self.cut = head_dim - self.low
        self.rows = rows

    def split(self, lanes):
        return lax.broadcasted_iota(jnp.int32, (8, lanes), 0) < self.cut

    def sums(self, x):
        lanes = x.shape[1]
        mid = x[self.low : self.high]
        first = self.split(lanes)
        a = jnp.sum(x[: self.low].reshape(self.low // 8, 8, lanes), 0)
        b = jnp.sum(x[self.high :].reshape((self.rows - self.high) // 8, 8, lanes), 0)
        a = a + jnp.where(first, mid, 0.0)
        b = b + jnp.where(first, 0.0, mid)
        return jnp.sum(a, 0, keepdims=True), jnp.sum(b, 0, keepdims=True)

    def scale(self, x, p0, p1):
        lanes = x.shape[1]
        mid = jnp.where(self.split(lanes), p0, p1)
        return jnp.concatenate(
            [x[: self.low] * p0, x[self.low : self.high] * mid, x[self.high :] * p1], 0
        )


SQUARES = (
    "g0r", "g0z", "g0n", "g1r", "g1z", "g1n",
    "s0t", "s1t", "s2t", "g0r_back", "g0z_back", "g0n_back",
    "s0", "s1", "s2", "oa", "ob",
)


def exchange_kernel(
    own, batch,
    mem_ref, last_ref, cand_ref, time_ref, mask_ref, src_ref, owner_ref, nbr_ref,
    msg_ref, gru_ref, square_ref, kv_ref, outw_ref,
    table_ref, ids_ref, flat_ref, pos_ref, newest_ref, mem3_ref,
    wsq_ref, wmsg_ref, wout_ref, wkv1_ref, wkv2_ref, wd_ref, wdt_ref,
    shard, ext, pairs, square_pad, wide_pad, kv_pad, batch_buf, own_buf,
    local_sem, table_send, table_recv, batch_send, batch_recv, own_send, own_recv,
):
    me = lax.axis_index("own")
    group = lax.axis_index("batch")
    barrier = pltpu.get_barrier_semaphore()
    for step in range(1, own):
        pl.semaphore_signal(barrier, inc=1, device_id=(group, lax.rem(me + step, own)), device_id_type=MESH)
    for step in range(1, batch):
        pl.semaphore_signal(barrier, inc=1, device_id=(lax.rem(group + step, batch), me), device_id_type=MESH)

    width, nodes = mem_ref.shape
    rows = pad_to(width, 16)
    ext[...] = jnp.zeros_like(ext)
    ext[0:width, :] = mem_ref[...]
    last = last_ref[...]
    ext[width : width + 1, :] = lax.div(last, 8).astype(f32)
    ext[width + 1 : width + 2, :] = lax.rem(last, 8).astype(f32)

    def turn(i, unused):
        block = ext[:, pl.ds(pl.multiple_of(i * 128, 128), 128)].T
        base = pl.multiple_of(i * 256, 256)
        pairs[pl.ds(base, 128, stride=2), :] = block[:, :128]
        pairs[pl.ds(base + 1, 128, stride=2), :] = block[:, 128:]
        return unused

    lax.fori_loop(0, nodes // 128, turn, 0)

    def pack(i, unused):
        got = [pairs[pl.ds(pl.multiple_of(i * 128, 128) + 2 * k, 2), :] for k in range(64)]
        for k in range(64):
            shard[i * 64 + k] = got[k].astype(bf16)
        return unused

    lax.fori_loop(0, nodes // 64, pack, 0)
    pl.semaphore_wait(barrier, own + batch - 2)

    half = nodes // 2
    bits = own.bit_length() - 1
    rest = list(range(1, bits))
    cut = len(rest) // 2
    orders = (rest + [0], rest[cut:] + rest[:cut] + [0])

    def shard_copy(stream, pattern, bit):
        peer = flip_bit(me, bit)
        source = me
        for b in range(bits):
            if pattern >> b & 1:
                source = flip_bit(source, b)
        part = pl.ds(pl.multiple_of(source * nodes + stream * half, half), half)
        slot = pattern | 1 << bit
        src = shard.at[pl.ds(stream * half, half)] if pattern == 0 else table_ref.at[part]
        return pltpu.make_async_remote_copy(
            src_ref=src, dst_ref=table_ref.at[part],
            send_sem=table_send.at[stream, slot], recv_sem=table_recv.at[stream, slot],
            device_id=(group, peer), device_id_type=MESH,
        )

    copies = [{}, {}]
    for step in range(bits):
        for stream in range(2):
            bit = orders[stream][step]
            copy = shard_copy(stream, 0, bit)
            copy.start()
            copies[stream][1 << bit] = copy
    mine = pltpu.make_async_copy(
        shard, table_ref.at[pl.ds(pl.multiple_of(me * nodes, nodes), nodes)], local_sem
    )
    mine.start()

    events = src_ref.shape[1]
    time_row = time_ref[...].astype(f32)
    src_row = src_ref[...]
    best = []
    tile = 256
    for start in range(0, nodes, tile):
        node = lax.broadcasted_iota(jnp.int32, (tile, 128), 0) + start
        top = jnp.full((tile, 128), -1.0, f32)
        for lane in range(0, events, 128):
            hit = src_row[:, lane : lane + 128] == node
            top = jnp.maximum(top, jnp.where(hit, time_row[:, lane : lane + 128], -1.0))
        best.append(jnp.max(top.T, 0, keepdims=True))
    newest = jnp.concatenate(best, 1).astype(jnp.int32)
    newest = jnp.maximum(newest, last)
    count = jnp.sum(mask_ref[...].astype(f32), 1, keepdims=True).astype(jnp.int32)
    batch_buf[0, 0:1, :] = newest
    batch_buf[0, 1:2, :] = jnp.broadcast_to(count, (1, nodes))

    def peer_copy(step):
        return pltpu.make_async_remote_copy(
            src_ref=batch_buf.at[0], dst_ref=batch_buf.at[step],
            send_sem=batch_send.at[step], recv_sem=batch_recv.at[step],
            device_id=(lax.rem(group + step, batch), me), device_id_type=MESH,
        )

    peers = [peer_copy(step) for step in range(1, batch)]
    for copy in peers:
        copy.start()

    picks = owner_ref.shape[0]
    per_pick = nbr_ref.shape[0]
    for s in range(per_pick):
        flat = owner_ref[...] * nodes + nbr_ref[s]
        for block in range(events // 128):
            at = (s * (events // 128) + block) * picks
            flat_ref[at : at + picks, :] = flat[:, block * 128 : block * 128 + 128]
    whole = ext[0:rows, :]
    part0 = whole.astype(bf16)
    whole = whole - part0.astype(f32)
    part1 = whole.astype(bf16)
    mem3_ref[0:rows, :] = part0
    mem3_ref[rows : 2 * rows, :] = part1
    mem3_ref[2 * rows :, :] = (whole - part1.astype(f32)).astype(bf16)

    square_pad[...] = jnp.zeros_like(square_pad)

    def put(name, value):
        square_pad[0:width, 0:width] = value
        wsq_ref[SQUARES.index(name)] = square_pad[...].astype(bf16)

    for index in range(2):
        for gate, letter in enumerate("rzn"):
            value = gru_ref[:, index, gate * width : gate * width + width]
            put(f"g{index}{letter}", value.T)
            if index == 0:
                put(f"g0{letter}_back", value)
    for index in range(3):
        value = square_ref[:, index, :]
        put(f"s{index}", value)
        put(f"s{index}t", value.T)
    put("oa", outw_ref[:, 0:width].T)
    put("ob", outw_ref[:, width : 2 * width].T)
    wide_pad[...] = jnp.zeros_like(wide_pad)
    wide_pad[0:width, 0 : 2 * width] = outw_ref[...]
    wout_ref[...] = wide_pad[:, 0 : wout_ref.shape[1]].astype(bf16)
    wide_pad[0:width, 0 : msg_ref.shape[1]] = msg_ref[...]
    wmsg_ref[...] = wide_pad[...].astype(bf16)
    last_square = square_ref[:, 3, :]
    kv_pad[...] = jnp.zeros_like(kv_pad)
    kv_pad[0:width, 0:width] = last_square
    wd_ref[...] = kv_pad[0 : wd_ref.shape[0], 0 : wd_ref.shape[1]].astype(bf16)
    kv_pad[0:width, 0:width] = last_square.T
    wdt_ref[...] = kv_pad[0 : wdt_ref.shape[0], 0 : wdt_ref.shape[1]].astype(bf16)
    times = wkv2_ref.shape[1]
    time_width = kv_ref.shape[0] - width
    lane = lax.broadcasted_iota(jnp.int32, (1, 256), 1)
    for index in range(2):
        part = kv_ref[:, index * width : index * width + width]
        kv_pad[index * rows : index * rows + width, 0:width] = part[0:width].T
    kv_pad[width : width + 1, :] = jnp.where(lane == width, 8.0, jnp.where(lane == width + 1, 1.0, 0.0))
    wkv1_ref[...] = kv_pad[...].astype(bf16)
    kv_pad[...] = jnp.zeros_like(kv_pad)
    for index in range(2):
        part = kv_ref[:, index * width : index * width + width]
        kv_pad[index * rows : index * rows + width, 0:time_width] = part[width:].T
    wkv2_ref[...] = kv_pad[:, 0:times].astype(bf16)

    total = count
    for step, copy in enumerate(peers, 1):
        copy.wait_recv()
        newest = jnp.maximum(newest, batch_buf[step, 0:1, :])
        total = total + batch_buf[step, 1:2, 0:1]
    newest_ref[...] = newest

    cands = cand_ref.shape[1]
    own_buf[0, 0:1, :] = cand_ref[...] + me * nodes
    own_buf[0, 1:2, :] = jnp.broadcast_to(total, (1, cands))

    def owner_copy(step):
        return pltpu.make_async_remote_copy(
            src_ref=own_buf.at[0], dst_ref=own_buf.at[step],
            send_sem=own_send.at[step], recv_sem=own_recv.at[step],
            device_id=(group, lax.rem(me + step, own)), device_id_type=MESH,
        )

    owners = [owner_copy(step) for step in range(1, own)]
    for copy in owners:
        copy.start()

    for step in range(bits):
        for stream in range(2):
            order = orders[stream]
            held = [0]
            for bit in order[:step]:
                held = held + [p | 1 << bit for p in held]
            for pattern in held:
                slot = pattern | 1 << order[step]
                copies[stream][slot].wait_recv()
                for bit in order[step + 1 :]:
                    copy = shard_copy(stream, slot, bit)
                    copy.start()
                    copies[stream][slot | 1 << bit] = copy

    for step in range(own):
        if step:
            owners[step - 1].wait_recv()
            total = total + own_buf[step, 1:2, 0:1]
        source = lax.rem(me - step + own, own)
        for block in range(cands // 128):
            ids_ref[pl.ds(source * (cands // 128) + block, 1), :] = own_buf[
                step, 0:1, block * 128 : block * 128 + 128
            ]
    pos_ref[...] = jnp.broadcast_to(jnp.maximum(total.astype(f32), 1.0), pos_ref.shape)
    mine.wait()
    for copy in peers + owners:
        copy.wait_send()
    for stream in range(2):
        for slot in copies[stream]:
            copies[stream][slot].wait_send()


def exchange(own, batch, args):
    mem, last, cand, time, mask, src, owner, nbr, msg, gru, square, kv, outw = args
    width, nodes = mem.shape
    events = src.shape[1]
    cands = cand.shape[1]
    rows = pad_to(width, 16)
    times = pad_to(kv.shape[0] - width, 16)
    wide = pad_to(msg.shape[1], 16)
    vmem = pl.BlockSpec(memory_space=pltpu.VMEM)
    hbm = pl.BlockSpec(memory_space=pl.ANY)
    low = lambda *shape: jax.ShapeDtypeStruct(shape, bf16)
    whole = lambda *shape: jax.ShapeDtypeStruct(shape, jnp.int32)
    return pl.pallas_call(
        partial(exchange_kernel, own, batch),
        out_shape=(
            low(own * nodes, 2, 128),
            whole(own * cands // 128, 128),
            whole(nbr.shape[0] * nbr.shape[1] * events // 128, 128),
            jax.ShapeDtypeStruct((8, 128), f32),
            whole(1, nodes),
            low(3 * rows, nodes),
            low(len(SQUARES), rows, rows),
            low(rows, wide),
            low(rows, 2 * rows),
            low(2 * rows, 256),
            low(2 * rows, times),
            low(256, rows),
            low(rows, 256),
        ),
        in_specs=[vmem] * len(args),
        out_specs=(hbm,) + (vmem,) * 12,
        scratch_shapes=[
            pltpu.VMEM((nodes, 2, 128), bf16),
            pltpu.VMEM((256, nodes), f32),
            pltpu.VMEM((2 * nodes, 128), f32),
            pltpu.VMEM((rows, rows), f32),
            pltpu.VMEM((rows, wide), f32),
            pltpu.VMEM((2 * rows, 256), f32),
            pltpu.VMEM((batch, 8, nodes), jnp.int32),
            pltpu.VMEM((own, 8, cands), jnp.int32),
            pltpu.SemaphoreType.DMA,
            pltpu.SemaphoreType.DMA((2, own)),
            pltpu.SemaphoreType.DMA((2, own)),
            pltpu.SemaphoreType.DMA((batch,)),
            pltpu.SemaphoreType.DMA((batch,)),
            pltpu.SemaphoreType.DMA((own,)),
            pltpu.SemaphoreType.DMA((own,)),
        ],
        compiler_params=pltpu.CompilerParams(
            collective_id=1, has_side_effects=True, vmem_limit_bytes=63 * 2**20
        ),
        name="exchange",
    )(*args)


class Layout:
    def __init__(self, width, wide, deep, gates, kv_rows, kv_cols, fold):
        rows = pad_to(width, 8)
        self.width = width
        self.pieces = {}
        row = 0
        for name, depth, columns in (
            ("msg", width, wide),
            ("out", width, deep),
            ("kv", kv_rows, kv_cols),
            ("gru0", width, gates),
            ("gru1", width, gates),
            ("square0", width, width),
            ("square1", width, width),
            ("square2", width, width),
            ("square3", width, width),
        ):
            tiles = []
            for column in range(0, columns, 128):
                size = min(128, columns - column)
                if size < 128 and name[:3] in ("gru", "squ"):
                    tiles.append([column, size, None, None])
                else:
                    tiles.append([column, size, row, 0])
                    row += pad_to(depth, 8)
            self.pieces[name] = (depth, tiles)
        host = self.pieces["msg"][1][-1]
        lane = pad_to(host[1], 8)
        for name in ("gru0", "gru1"):
            tile = self.pieces[name][1][-1]
            if tile[2] is None:
                assert lane + tile[1] <= 128
                tile[2:] = [host[2], lane]
                lane += tile[1]
        for pair in range(2):
            for side in range(2):
                tile = self.pieces[f"square{2 * pair + side}"][1][-1]
                assert tile[1] <= 64
                tile[2:] = [row, 64 * side]
            row += rows
        self.loss = row
        row += 8
        self.total = pad_to(row, fold)

    def put(self, ref, name, value):
        depth, tiles = self.pieces[name]
        for column, size, row, lane in tiles:
            ref[row : row + depth, lane : lane + size] = value[:depth, column : column + size]

    def tiles(self, ref, name):
        depth, tiles = self.pieces[name]
        for column, size, row, lane in tiles:
            yield slice(column, column + size), ref[row : row + depth, lane : lane + size]


def main_kernel(
    dims,
    ids_ref, cand_ref, pos_ref, table_ref, time_ref, mask_ref, src_ref, target_ref, valid_ref, mem3_ref, edge_ref,
    wsq_ref, wmsg_ref, wout_ref, wkv1_ref, wkv2_ref, wd_ref, wdt_ref, freq_ref,
    grad_ref,
    xs, xs2, x_all, t_all, kv_all, score, dest_rows, slab, eye_ref, gslab, stage,
    x_msg, mem_low, hidden, fresh_low, att_low, x_out, hid_out, emb, emb_rows,
    mem_src, pre_msg, reset_gate, update, cand_act, gate_n, queries, attended, pre_out,
    acc_a, grad_att, gkv_m, gkv_t, rows_ref,
):
    width, head_dim, keep_kv, cand_width, layout = dims
    events = time_ref.shape[1]
    per_pick, picks = valid_ref.shape[:2]
    slots = per_pick * picks
    rows = pad_to(width, 16)
    times = wkv2_ref.shape[1]
    wide = wmsg_ref.shape[1]
    time_width = layout.pieces["kv"][0] - width
    edge = edge_ref.shape[0]
    heads = Heads(head_dim, rows)
    scale = head_dim ** (-0.5)
    high, low = freq_ref[:, 0:1], freq_ref[:, 1:2]
    chunks = events // LANES
    owners = cand_ref.shape[0] // cand_width

    def w(name):
        return wsq_ref[SQUARES.index(name)]

    def gather(buf, read_id, at):
        got = [table_ref[read_id(k)] for k in range(128)]
        for k in range(128):
            buf[pl.ds(pl.multiple_of(2 * at, 256) + 2 * k, 2), :] = got[k].astype(f32)

    def gathered(buf, start, count):
        base = pl.multiple_of(2 * start, 2 * count)
        return jnp.concatenate(
            [buf[pl.ds(base, count, stride=2), :], buf[pl.ds(base + 1, count, stride=2), :]], 1
        ).astype(bf16)

    grad_ref[layout.loss :, :] = jnp.zeros_like(grad_ref[layout.loss :, :])
    host = layout.pieces["msg"][1][-1][2]
    grad_ref[host : host + rows, :] = jnp.zeros((rows, 128), f32)
    eye = lax.broadcasted_iota(jnp.int32, (256, 256), 0) == lax.broadcasted_iota(jnp.int32, (256, 256), 1)
    eye_ref[...] = eye.astype(f32).astype(bf16)
    stage[...] = jnp.zeros_like(stage)

    def cand_body(o, unused):
        def fill(i, unused):
            gather(xs, lambda k: cand_ref[o * cand_width + i * 128 + k], i * 128)
            return unused

        lax.fori_loop(0, cand_width // 128, fill, 0)
        at = pl.multiple_of(o * cand_width, cand_width)
        dest_rows[pl.ds(at, cand_width), :] = gathered(xs, 0, cand_width)
        return unused

    lax.fori_loop(0, owners, cand_body, 0)

    def lanes(c, size=LANES):
        return pl.ds(pl.multiple_of(c * size, size), size)

    def gru_body(c, unused):
        cs = lanes(c)
        node = lax.broadcasted_iota(jnp.int32, (mem3_ref.shape[1], LANES), 0)
        onehot = (node == src_ref[:, cs]).astype(f32).astype(bf16)
        parts = nn(mem3_ref[...], onehot)
        mem = parts[:rows] + parts[rows : 2 * rows] + parts[2 * rows :]
        mem_src[:, cs] = mem
        delta = time_ref[:, cs].astype(f32) - 8.0 * mem[width : width + 1] - mem[width + 1 : width + 2]
        stage[0:width, :] = mem[0:width]
        stage[width : width + edge, :] = edge_ref[:, cs].astype(f32)
        stage[width + edge : width + edge + time_width, :] = cos_rows(delta, high, low)[0:time_width]
        x = stage[...].astype(bf16)
        x_msg[:, cs] = x
        m_low = mem.astype(bf16)
        mem_low[:, cs] = m_low
        pre = nn(wmsg_ref[...], x)
        pre_msg[:, cs] = pre
        hid = (pre * jax.nn.sigmoid(pre)).astype(bf16)
        hidden[:, cs] = hid
        r = jax.nn.sigmoid(nn(w("g0r"), hid) + nn(w("g1r"), m_low))
        reset_gate[:, cs] = r
        u = jax.nn.sigmoid(nn(w("g0z"), hid) + nn(w("g1z"), m_low))
        update[:, cs] = u
        gn = nn(w("g1n"), m_low)
        gate_n[:, cs] = gn
        cand = jnp.tanh(nn(w("g0n"), hid) + r * gn)
        cand_act[:, cs] = cand
        fresh = ((1.0 - u) * cand + u * mem).astype(bf16)
        fresh_low[:, cs] = fresh
        queries[:, cs] = nn(w("s0t"), fresh).astype(bf16)
        return unused

    lax.fori_loop(0, chunks, gru_body, 0)

    def fetch(buf, j, i):
        base = ((lax.div(j, picks) * (events // 128) + i) * picks + lax.rem(j, picks)) * 128
        gather(buf, lambda k: ids_ref[base + k], i * 128)

    def slot_chunk(buf, j, c):
        cs = lanes(c)
        x = gathered(buf, c * LANES, LANES)
        x_all[j, cs, :] = x
        kv = nt(wkv1_ref[...], x)
        delta = time_ref[:, cs].astype(f32) - kv[width : width + 1]
        t_low = cos_rows(delta, high, low).astype(bf16)
        t_all[j, :, cs] = t_low
        kv = (kv + nn(wkv2_ref[...], t_low)).astype(bf16)
        if keep_kv:
            kv_all[j, :, cs] = kv
        s0, s1 = heads.sums(kv[:rows].astype(f32) * queries[:, cs].astype(f32))
        live = valid_ref[lax.div(j, picks), pl.ds(lax.rem(j, picks), 1), cs] > 0
        score[j, 0:1, cs] = jnp.where(live, s0 * scale, mask_fill)
        score[j, 1:2, cs] = jnp.where(live, s1 * scale, mask_fill)

    def first_slot(i, unused):
        fetch(xs, 0, i)
        return unused

    lax.fori_loop(0, events // 128, first_slot, 0)

    def slot_pair(i, unused):
        for side, (now, later) in enumerate(((xs, xs2), (xs2, xs))):
            j = 2 * i + side
            ahead = jnp.minimum(j + 1, slots - 1)
            for c in range(chunks):
                for block in range(LANES // 128):
                    fetch(later, ahead, c * (LANES // 128) + block)
                slot_chunk(now, j, c)
        return unused

    lax.fori_loop(0, slots // 2, slot_pair, 0)

    def soft_body(c, unused):
        cs = lanes(c, 128)
        s = score[:, 0:2, cs]
        top = jnp.max(s, 0, keepdims=True)
        p = jnp.where(s > 0.5 * mask_fill, jnp.exp(s - top), 0.0)
        score[:, 0:2, cs] = p / jnp.sum(p, 0, keepdims=True)
        return unused

    lax.fori_loop(0, events // 128, soft_body, 0)

    def kv_of(j, cs, part):
        if keep_kv:
            return kv_all[j, part, cs]
        return (nt(wkv1_ref[part, :], x_all[j, cs, :]) + nn(wkv2_ref[part, :], t_all[j, :, cs])).astype(bf16)

    def att_body(c, unused):
        cs = lanes(c, 128)
        total = jnp.zeros((rows, 128), f32)
        for j in range(slots):
            v = kv_of(j, cs, slice(rows, 2 * rows)).astype(f32)
            total = total + heads.scale(v, score[j, 0:1, cs], score[j, 1:2, cs])
        attended[:, cs] = total
        att_low[:, cs] = total.astype(bf16)
        return unused

    lax.fori_loop(0, events // 128, att_body, 0)

    def out_body(c, unused):
        cs = lanes(c)
        stage[0:width, :] = nn(w("s1t"), att_low[:, cs])[0:width]
        stage[width : 2 * width, :] = fresh_low[:, cs].astype(f32)[0:width]
        x = stage[0 : 2 * rows, :].astype(bf16)
        x_out[:, cs] = x
        pre = nn(wout_ref[...], x)
        pre_out[:, cs] = pre
        hid = (pre * jax.nn.sigmoid(pre)).astype(bf16)
        hid_out[:, cs] = hid
        e = nn(w("s2t"), hid).astype(bf16)
        emb[:, cs] = e
        emb_rows[cs, :] = nt(eye_ref[...], e).astype(bf16)
        return unused

    lax.fori_loop(0, chunks, out_body, 0, unroll=2)

    def row_init(c, unused):
        cs = lanes(c)
        rows_ref[0:1, cs] = jnp.full((1, LANES), mask_fill, f32)
        rows_ref[1:3, cs] = jnp.zeros((2, LANES), f32)
        acc_a[:, cs] = jnp.zeros((rows, LANES), f32)
        return unused

    lax.fori_loop(0, chunks, row_init, 0)

    def dest_of(o):
        at = pl.multiple_of(o * cand_width, cand_width)
        return dest_rows[pl.ds(at, cand_width), :]

    def lse_block(i, unused):
        for side in range(2):
            o = 2 * i + side
            dest = nn(dest_of(o), wd_ref[...]).astype(bf16)
            for c in range(chunks):
                cs = lanes(c)
                logits = nn(dest, emb[:, cs])
                old = rows_ref[0:1, cs]
                top = jnp.maximum(old, jnp.max(logits, 0, keepdims=True))
                rows_ref[0:1, cs] = top
                rows_ref[1:2, cs] = rows_ref[1:2, cs] * jnp.exp(old - top) + jnp.sum(
                    jnp.exp(logits - top), 0, keepdims=True
                )
                hit = lax.broadcasted_iota(jnp.int32, logits.shape, 0) == target_ref[:, cs] - o * cand_width
                rows_ref[2:3, cs] = rows_ref[2:3, cs] + jnp.sum(jnp.where(hit, logits, 0.0), 0, keepdims=True)
        return unused

    lax.fori_loop(0, owners // 2, lse_block, 0)

    mask_row = mask_ref[...].astype(f32)
    log_sum = rows_ref[0:1, :] + jnp.log(rows_ref[1:2, :])
    rows_ref[3:4, :] = log_sum
    rows_ref[4:5, :] = mask_row / jnp.broadcast_to(pos_ref[0:1, 0:1], mask_row.shape)
    loss = jnp.sum(mask_row * (log_sum - rows_ref[2:3, :]), 1, keepdims=True)
    grad_ref[layout.loss : layout.loss + 8, :] = jnp.broadcast_to(loss, (8, 128))

    def back_block(o, grad_dest_w):
        block = dest_of(o)
        dest = nn(block, wd_ref[...]).astype(bf16)
        dest_t = nt(wdt_ref[...], block).astype(bf16)
        block_t = nt(eye_ref[...], block).astype(bf16)

        def chunk(c, unused):
            cs = lanes(c)
            logits = nn(dest, emb[:, cs])
            coeff = rows_ref[4:5, cs]
            hit = lax.broadcasted_iota(jnp.int32, logits.shape, 0) == target_ref[:, cs] - o * cand_width
            grad = jnp.exp(logits - rows_ref[3:4, cs]) - jnp.where(hit, 1.0, 0.0)
            grad = (grad * coeff).astype(bf16)
            slab[0:cand_width, cs] = grad
            return unused

        lax.fori_loop(0, chunks, chunk, 0, unroll=True)
        acc_a[...] += nn(dest_t, slab[0:cand_width, :])
        grad_dest = nn(slab[0:cand_width, :], emb_rows[...]).astype(bf16)
        return grad_dest_w + nn(block_t, grad_dest)[:rows]

    grad_dest_w = lax.fori_loop(0, owners, back_block, jnp.zeros((rows, rows), f32))
    layout.put(grad_ref, "square3", grad_dest_w)

    r0, r1, r2 = slice(0, rows), slice(rows, 2 * rows), slice(2 * rows, 3 * rows)

    def out_back(c, unused):
        cs = lanes(c)
        ge = acc_a[:, cs].astype(bf16)
        slab[r0, cs] = ge
        pre = pre_out[:, cs]
        sig = jax.nn.sigmoid(pre)
        gp = (nn(w("s2"), ge) * (sig * (1.0 + pre * (1.0 - sig)))).astype(bf16)
        slab[r1, cs] = gp
        gm = nn(w("oa"), gp).astype(bf16)
        slab[r2, cs] = gm
        acc_a[:, cs] = nn(w("ob"), gp)
        ga = nn(w("s1"), gm).astype(bf16)
        grad_att[:, cs] = ga
        d0, d1 = heads.sums(ga.astype(f32) * attended[:, cs])
        rows_ref[5:6, cs] = d0
        rows_ref[6:7, cs] = d1
        return unused

    lax.fori_loop(0, chunks, out_back, 0, unroll=2)
    layout.put(grad_ref, "square2", nt(hid_out[...], slab[r0, :]))
    layout.put(grad_ref, "out", nt(slab[r1, :], x_out[...]))
    layout.put(grad_ref, "square1", nt(att_low[...], slab[r2, :]))

    attended[...] = jnp.zeros_like(attended)
    gkv_m[...] = jnp.zeros_like(gkv_m)
    gkv_t[...] = jnp.zeros_like(gkv_t)

    def slot_back(i, unused):
        for side in range(2):
            j = 2 * i + side
            for c in range(events // 256):
                cs = lanes(c, 256)
                kv = kv_of(j, cs, slice(0, 2 * rows)).astype(f32)
                ga = grad_att[:, cs].astype(f32)
                p0, p1 = score[j, 0:1, cs], score[j, 1:2, cs]
                g0, g1 = heads.sums(ga * kv[rows:])
                g0 = p0 * (g0 - rows_ref[5:6, cs]) * scale
                g1 = p1 * (g1 - rows_ref[6:7, cs]) * scale
                attended[:, cs] += heads.scale(kv[:rows], g0, g1)
                gslab[side, 0:rows, cs] = heads.scale(queries[:, cs].astype(f32), g0, g1).astype(bf16)
                gslab[side, rows:2*rows, cs] = heads.scale(ga, p0, p1).astype(bf16)
            both = gslab[side, 0 : 2 * rows, :]
            gkv_m[...] += nn(both, x_all[j])
            gkv_t[...] += nt(both, t_all[j])
        return unused

    lax.fori_loop(0, slots // 2, slot_back, 0)
    gm = gkv_m[...].T
    gt = gkv_t[...].T
    both = [jnp.concatenate([g[:depth, :width], g[:depth, rows : rows + width]], 1)
            for g, depth in ((gm, width), (gt, time_width))]
    layout.put(grad_ref, "kv", jnp.concatenate(both, 0))

    def gru_back(c, unused):
        cs = lanes(c)
        gq = attended[:, cs].astype(bf16)
        slab[r0, cs] = gq
        gf = acc_a[:, cs] + nn(w("s0"), gq)
        u, cand, r = update[:, cs], cand_act[:, cs], reset_gate[:, cs]
        act = gf * (1.0 - u) * (1.0 - cand * cand)
        gr = (act * gate_n[:, cs] * r * (1.0 - r)).astype(bf16)
        gu = (gf * (mem_src[:, cs] - cand) * u * (1.0 - u)).astype(bf16)
        gn = act.astype(bf16)
        gh = (act * r).astype(bf16)
        slab[r1, cs] = gr
        slab[r2, cs] = gu
        x_out[0:rows, cs] = gn
        hid_out[:, cs] = gh
        pre = pre_msg[:, cs]
        sig = jax.nn.sigmoid(pre)
        back = nn(w("g0r_back"), gr) + nn(w("g0z_back"), gu) + nn(w("g0n_back"), gn)
        att_low[:, cs] = (back * (sig * (1.0 + pre * (1.0 - sig)))).astype(bf16)
        return unused

    lax.fori_loop(0, chunks, gru_back, 0, unroll=2)
    layout.put(grad_ref, "square0", nt(fresh_low[...], slab[r0, :]))
    for index, (left, last) in enumerate(((hidden, x_out[0:rows, :]), (mem_low, hid_out[...]))):
        left = left[...]
        parts = [nt(left, slab[r1, :]), nt(left, slab[r2, :]), nt(left, last)]
        layout.put(grad_ref, f"gru{index}", jnp.concatenate([p[:, :width] for p in parts], 1))
    layout.put(grad_ref, "msg", nt(att_low[...], x_msg[...]))


def main(layout, keep_kv, width, head_dim, cand_width, args):
    events = args[4].shape[1]
    slots = args[8].shape[0] * args[8].shape[1]
    wide = args[12].shape[1]
    times = args[15].shape[1]
    rows = pad_to(width, 16)
    cands = args[1].shape[0]
    smem = pl.BlockSpec(memory_space=pltpu.SMEM)
    vmem = pl.BlockSpec(memory_space=pltpu.VMEM)
    low = lambda *shape: pltpu.VMEM(shape, bf16)
    full = lambda *shape: pltpu.VMEM(shape, f32)
    return pl.pallas_call(
        partial(main_kernel, (width, head_dim, keep_kv, cand_width, layout)),
        out_shape=jax.ShapeDtypeStruct((layout.total, 128), f32),
        in_specs=[smem, smem] + [vmem] * (len(args) - 2),
        out_specs=vmem,
        scratch_shapes=[
            full(2 * events, 128),
            full(2 * events, 128),
            low(slots, events, 256),
            low(slots, times, events),
            low(slots if keep_kv else 1, 2 * rows if keep_kv else 16, events),
            full(slots, 8, events),
            low(cands, 256),
            low(max(3 * rows, cand_width), events),
            low(256, 256),
            low(2, cand_width, events),
            full(wide, LANES),
            low(wide, events),
        ]
        + [low(rows, events)] * 4
        + [low(2 * rows, events)]
        + [low(rows, events)] * 2
        + [low(events, rows)]
        + [full(rows, events)] * 6
        + [low(rows, events)]
        + [full(rows, events)] * 3
        + [low(rows, events), full(2 * rows, 256), full(2 * rows, times), full(8, events)],
        compiler_params=pltpu.CompilerParams(vmem_limit_bytes=63 * 2**20),
        name="train",
    )(*args)


def reduce_kernel(own, batch, streams, grad_ref, out_ref, acc, recv, send_sem, recv_sem):
    place = {"own": lax.axis_index("own"), "batch": lax.axis_index("batch")}
    rounds = len(streams[0][2])

    def peers(axis, bit):
        if axis == "own":
            return [(place["batch"], flip_bit(place["own"], bit))]
        return [(lax.rem(place["batch"] + d, batch), place["own"]) for d in range(1, batch)]

    barrier = pltpu.get_barrier_semaphore()
    signals = 0
    for axis, bit in streams[0][2]:
        for peer in peers(axis, bit):
            pl.semaphore_signal(barrier, inc=1, device_id=peer, device_id_type=MESH)
            signals += 1
    pl.semaphore_wait(barrier, signals)

    sent = []

    class Stream:
        def __init__(self, index, start, size, order):
            self.index, self.base, self.size, self.inner, self.order = index, start, size, start, order
            self.copies = []

        def copy(self, source, target, peer, slot):
            copy = pltpu.make_async_remote_copy(
                src_ref=source, dst_ref=target,
                send_sem=send_sem.at[self.index, slot], recv_sem=recv_sem.at[self.index, slot],
                device_id=peer, device_id_type=MESH,
            )
            copy.start()
            self.copies.append(copy)
            sent.append(copy)

        def parts(self, axis, bit):
            if axis == "own":
                return 2, lax.div(place["own"], 1 << bit) % 2
            return batch, place["batch"]

        def scatter(self, step):
            axis, bit = self.order[step]
            count, mine = self.parts(axis, bit)
            piece = self.size // count
            source = grad_ref if step == 0 else acc
            for d, peer in enumerate(peers(axis, bit), 1):
                theirs = 1 - mine if axis == "own" else peer[0]
                away = pl.multiple_of(self.base + theirs * piece, 8)
                self.copy(
                    source.at[pl.ds(away, piece), :], recv.at[pl.ds(self.inner + (d - 1) * piece, piece), :],
                    peer, step * (batch - 1) + d - 1,
                )
            self.base = pl.multiple_of(self.base + mine * piece, 8)
            self.size = piece

        def add(self, step):
            source = grad_ref if step == 0 else acc
            target = out_ref if step == rounds - 1 else acc
            part = pl.ds(self.base, self.size)
            total = source[part, :]
            for copy in self.copies:
                copy.wait_recv()
                total = total + recv[pl.ds(self.inner, self.size), :]
                self.inner += self.size
            target[part, :] = total
            self.copies = []

        def gather(self, step):
            axis, bit = self.order[step]
            count, mine = self.parts(axis, bit)
            part = pl.ds(self.base, self.size)
            for d, peer in enumerate(peers(axis, bit), 1):
                self.copy(out_ref.at[part, :], out_ref.at[part, :], peer, (rounds + step) * (batch - 1) + d - 1)
            self.base = pl.multiple_of(self.base - mine * self.size, 8)
            self.size *= count

        def gathered(self):
            for copy in self.copies:
                copy.wait_recv()
            self.copies = []

    flows = [Stream(index, *stream) for index, stream in enumerate(streams)]
    for step in range(2 * rounds + 1):
        for flow in flows:
            if 0 < step <= rounds:
                flow.add(step - 1)
            elif step > rounds:
                flow.gathered()
            if step < rounds:
                flow.scatter(step)
            elif step < 2 * rounds:
                flow.gather(2 * rounds - 1 - step)
    for copy in sent:
        copy.wait_send()


def reduce_all(own, batch, packed):
    total = packed.shape[0]
    own_bits = own.bit_length() - 1
    fold = 8 * own * batch
    rest = [("own", b) for b in range(1, own_bits)]
    cut = len(rest) // 2
    axes = [rest[:cut], rest[cut:], [("batch", 0)]]
    blocks = total // fold
    halves = 1
    streams = []
    start = 0
    for index in range(3 * halves):
        size = (blocks + 3 * halves - 1 - index) // (3 * halves) * fold
        turn = index % 3
        order = [("own", 0)] + [bit for part in axes[turn:] + axes[:turn] for bit in part]
        if size:
            streams.append((start, size, order))
            start += size
    count = 2 * len(streams[0][2]) * (batch - 1)
    return pl.pallas_call(
        partial(reduce_kernel, own, batch, streams),
        out_shape=jax.ShapeDtypeStruct(packed.shape, f32),
        in_specs=[pl.BlockSpec(memory_space=pltpu.VMEM)],
        out_specs=pl.BlockSpec(memory_space=pltpu.VMEM),
        scratch_shapes=[
            pltpu.VMEM(packed.shape, f32),
            pltpu.VMEM(packed.shape, f32),
            pltpu.SemaphoreType.DMA((len(streams), count)),
            pltpu.SemaphoreType.DMA((len(streams), count)),
        ],
        compiler_params=pltpu.CompilerParams(
            collective_id=2, has_side_effects=True, vmem_limit_bytes=63 * 2**20
        ),
        name="reduce",
    )(packed)


def update_kernel(layout, step_rate, grad_ref, *refs):
    sources, targets, held, laid = refs[:15], refs[15:30], refs[30:45], refs[45:47]
    in_sem, out_sem = refs[47:]
    arrive = [pltpu.make_async_copy(sources[i], held[i], in_sem.at[i]) for i in range(15)]
    leave = [pltpu.make_async_copy(held[i], targets[(i + 5) % 10 if i < 10 else i], out_sem.at[i]) for i in range(15)]
    order = (1, 2, 0, 3, 4)
    for index in order:
        for kind in range(3):
            arrive[5 * kind + index].start()

    for ref, name, parts in ((laid[0], "gru", 2), (laid[1], "square", 4)):
        for part in range(parts):
            for columns, gradient in layout.tiles(grad_ref, f"{name}{part}"):
                ref[:, part, columns] = gradient

    def step(index, at, gradient):
        weights, moments, averages = (held[5 * kind + index] for kind in range(3))
        moment = mu_coef * moments[at] + gradient
        weight = weights[at] - step_rate * (gradient + mu_coef * moment)
        moments[at] = moment
        weights[at] = weight
        averages[at] = (1.0 - avg_coef) * averages[at] + avg_coef * weight

    for index in order:
        for kind in range(3):
            arrive[5 * kind + index].wait()
        if index in (1, 2):
            step(index, slice(None), laid[index - 1][...])
        else:
            for columns, gradient in layout.tiles(grad_ref, ("msg", "", "", "kv", "out")[index]):
                step(index, (slice(None), columns), gradient)
        for kind in range(3):
            leave[5 * kind + index].start()
    for copy in leave:
        copy.wait()


def update_all(layout, step_rate, packed, params):
    vmem = pl.BlockSpec(memory_space=pltpu.VMEM)
    hbm = pl.BlockSpec(memory_space=pl.ANY)
    buffers = [pltpu.VMEM(p.shape, f32) for p in params]
    return pl.pallas_call(
        partial(update_kernel, layout, step_rate),
        out_shape=tuple(jax.ShapeDtypeStruct(p.shape, f32) for p in params[5:10] + params[:5] + params[10:]),
        in_specs=[vmem] + [hbm] * 15,
        out_specs=(hbm,) * 15,
        scratch_shapes=buffers + buffers[1:3] + [pltpu.SemaphoreType.DMA((15,))] * 2,
        compiler_params=pltpu.CompilerParams(vmem_limit_bytes=63 * 2**20),
        name="update",
    )(packed, *params)


def turned(arrays):
    msg, gru, square, kv, out = arrays
    return (msg.T, gru.transpose(1, 0, 2), square.transpose(1, 0, 2), kv, out.T)


def local(
    memory, last_update, src_local, edge_feat, event_time, nbr_owner, nbr_ids, nbr_mask, event_mask,
    dest_local, target, w_msg, w_gru, w_square, w_key_value, w_output,
    mom_msg, mom_gru, mom_square, mom_key_value, mom_output,
    avg_msg, avg_gru, avg_square, avg_key_value, avg_output,
):
    own = lax.axis_size("own")
    batch = lax.axis_size("batch")
    events, edge = edge_feat.shape
    nodes, width = memory.shape
    head_dim = width // HEADS
    time_width = w_key_value.shape[0] - width
    times = pad_to(time_width, 16)
    layout = Layout(
        width, w_msg.shape[0], w_output.shape[0], w_gru.shape[2], *w_key_value.shape, 8 * own * batch
    )
    weights = turned((w_msg, w_gru, w_square, w_key_value, w_output))
    time_row, mask_row, src_row, target_row = (x[None, :] for x in (event_time, event_mask, src_local, target))
    table, cand_ids, flat_ids, positives, newest, mem3, *low_weights = exchange(
        own, batch,
        (memory.T, last_update[None, :], dest_local[None, :], time_row, mask_row, src_row,
         nbr_owner.T, nbr_ids.transpose(2, 1, 0)) + weights,
    )
    packed = main(
        layout, own * nodes <= 16384, width, head_dim, dest_local.shape[0],
        (flat_ids.reshape(-1), cand_ids.reshape(-1), positives, table, time_row, mask_row, src_row, target_row,
         nbr_mask.transpose(2, 1, 0), mem3, edge_feat.T, *low_weights, jnp.asarray(time_columns(time_width, times))),
    )
    summed = reduce_all(own, batch, packed)
    step_rate = rate_coef * math.sqrt(events * own * batch)
    states = update_all(
        layout, step_rate, summed,
        weights
        + turned((mom_msg, mom_gru, mom_square, mom_key_value, mom_output))
        + turned((avg_msg, avg_gru, avg_square, avg_key_value, avg_output)),
    )
    states = [x for i in range(3) for x in turned(states[5 * i : 5 * i + 5])]
    return (summed[layout.loss, 0], positives[0, 0], newest.reshape(-1), *states)


def solution(mesh):
    row = P(("batch", "own"))
    placed = (
        (P("own", None), P("own"), row, P(("batch", "own"), None), row, P(("batch", "own"), None))
        + (P(("batch", "own"), None, None),) * 2
        + (row,) * 3
        + (P(),) * 15
    )
    return jax.shard_map(
        local,
        mesh=mesh,
        in_specs=placed,
        out_specs=(P(), P(), P("own")) + (P(),) * 15,
        check_vma=False,
    )
```

```python
from functools import partial
import math

import jax
import jax.numpy as jnp
import numpy as np
from jax import lax
from jax.experimental import pallas as pl
from jax.experimental.pallas import tpu as pltpu
from jax.sharding import PartitionSpec as P

HEADS = 2
LANES = 256
MESH = pl.DeviceIdType.MESH
f32 = jnp.float32
bf16 = jnp.bfloat16

mu_coef = 0.9
avg_coef = 0.1
rate_coef = 0.008
mask_fill = -1e30

COS_TERMS = (
    1.0,
    -19.73920440673828,
    64.93911743164062,
    -85.45011901855469,
    60.16745376586914,
    -25.966907501220703,
    6.527653217315674,
)


def pad_to(size, step):
    return -(-size // step) * step


def nn(a, b):
    return lax.dot_general(a, b, (((1,), (0,)), ((), ())), preferred_element_type=f32)


def nt(a, b):
    return lax.dot_general(a, b, (((1,), (1,)), ((), ())), preferred_element_type=f32)


def flip_bit(index, bit):
    size = 1 << bit
    return index + size * (1 - 2 * (lax.div(index, size) % 2))


def time_columns(time_width, rows):
    turns = 10.0 ** (-np.linspace(0.0, 9.0, time_width)) / (2.0 * np.pi)
    mant, expo = np.frexp(turns)
    high = np.ldexp(np.round(mant * 4096.0) / 4096.0, expo)
    out = np.zeros((rows, 128), np.float32)
    out[:time_width, 0] = high
    out[:time_width, 1] = turns - high
    return out


def cos_rows(delta, high, low):
    turns = delta * high
    rest = turns - jnp.floor(turns + 0.5) + delta * low
    square = rest * rest
    value = square * COS_TERMS[-1] + COS_TERMS[-2]
    for term in COS_TERMS[-3::-1]:
        value = value * square + term
    return value


class Heads:
    def __init__(self, head_dim, rows):
        self.low = head_dim // 8 * 8
        self.high = pad_to(head_dim, 8)
        self.cut = head_dim - self.low
        self.rows = rows

    def split(self, lanes):
        return lax.broadcasted_iota(jnp.int32, (8, lanes), 0) < self.cut

    def sums(self, x):
        lanes = x.shape[1]
        mid = x[self.low : self.high]
        first = self.split(lanes)
        a = jnp.sum(x[: self.low].reshape(self.low // 8, 8, lanes), 0)
        b = jnp.sum(x[self.high :].reshape((self.rows - self.high) // 8, 8, lanes), 0)
        a = a + jnp.where(first, mid, 0.0)
        b = b + jnp.where(first, 0.0, mid)
        return jnp.sum(a, 0, keepdims=True), jnp.sum(b, 0, keepdims=True)

    def scale(self, x, p0, p1):
        lanes = x.shape[1]
        mid = jnp.where(self.split(lanes), p0, p1)
        return jnp.concatenate(
            [x[: self.low] * p0, x[self.low : self.high] * mid, x[self.high :] * p1], 0
        )


GATES = ("g0r", "g0z", "g0n", "g1r", "g1z", "g1n", "s0t")
SQUARES = ("s1t", "s2t", "g0r_back", "g0z_back", "g0n_back", "s0", "s1", "s2", "oa", "ob")
LOW_STATE = ("queries", "fresh_low", "x_msg", "mem_low", "hidden")
STATE = ("mem_src", "pre_msg", "reset_gate", "update", "cand_act", "gate_n")


def exchange_kernel(
    own, batch,
    mem_ref, last_ref, cand_ref, time_ref, mask_ref, src_ref, owner_ref, nbr_ref, freq_ref,
    msg_hbm, gru_hbm, square_hbm, kv_hbm, outw_hbm, edge_hbm,
    table_ref, ids_ref, flat_ref, pos_ref, newest_ref, *rest,
):
    handed = rest[: 5 + len(LOW_STATE) + len(STATE)]
    rest = rest[len(handed) :]
    staged = rest[: len(handed)]
    wsq_ref, wout_ref, wkv_ref, wd_ref, wdt_ref = staged[:5]
    state = dict(zip(LOW_STATE + STATE, staged[5:]))
    (msg_ref, gru_ref, square_ref, kv_ref, outw_ref, edge_ref, gates_ref, wmsg_ref, mem3_ref, stage,
     shard, ext, pairs, square_pad, wide_pad, kv_pad, batch_buf, own_buf,
     local_sem, load_sem, hand_sem,
     table_send, table_recv, batch_send, batch_recv, own_send, own_recv) = rest[len(handed) :]
    loads = [
        pltpu.make_async_copy(source, target, load_sem.at[i])
        for i, (source, target) in enumerate((
            (gru_hbm, gru_ref), (square_hbm, square_ref), (outw_hbm, outw_ref),
            (msg_hbm, msg_ref), (kv_hbm, kv_ref), (edge_hbm, edge_ref),
        ))
    ]
    for copy in loads:
        copy.start()
    hands = [pltpu.make_async_copy(staged[i], handed[i], hand_sem.at[i]) for i in range(len(handed))]
    me = lax.axis_index("own")
    group = lax.axis_index("batch")
    barrier = pltpu.get_barrier_semaphore()
    for step in range(1, own):
        pl.semaphore_signal(barrier, inc=1, device_id=(group, lax.rem(me + step, own)), device_id_type=MESH)
    for step in range(1, batch):
        pl.semaphore_signal(barrier, inc=1, device_id=(lax.rem(group + step, batch), me), device_id_type=MESH)

    width, nodes = mem_ref.shape
    rows = pad_to(width, 16)
    ext[...] = jnp.zeros_like(ext)
    ext[0:width, :] = mem_ref[...]
    last = last_ref[...]
    ext[width : width + 1, :] = lax.div(last, 8).astype(f32)
    ext[width + 1 : width + 2, :] = lax.rem(last, 8).astype(f32)

    def turn(i, unused):
        block = ext[:, pl.ds(pl.multiple_of(i * 128, 128), 128)].T
        base = pl.multiple_of(i * 256, 256)
        pairs[pl.ds(base, 128, stride=2), :] = block[:, :128]
        pairs[pl.ds(base + 1, 128, stride=2), :] = block[:, 128:]
        return unused

    lax.fori_loop(0, nodes // 128, turn, 0)

    def pack(i, unused):
        got = [pairs[pl.ds(pl.multiple_of(i * 128, 128) + 2 * k, 2), :] for k in range(64)]
        for k in range(64):
            shard[i * 64 + k] = got[k].astype(bf16)
        return unused

    lax.fori_loop(0, nodes // 64, pack, 0)
    pl.semaphore_wait(barrier, own + batch - 2)

    half = nodes // 2
    bits = own.bit_length() - 1
    others = list(range(1, bits))
    cut = len(others) // 2
    orders = (others + [0], others[cut:] + others[:cut] + [0])

    def shard_copy(stream, pattern, bit):
        peer = flip_bit(me, bit)
        source = me
        for b in range(bits):
            if pattern >> b & 1:
                source = flip_bit(source, b)
        part = pl.ds(pl.multiple_of(source * nodes + stream * half, half), half)
        slot = pattern | 1 << bit
        src = shard.at[pl.ds(stream * half, half)] if pattern == 0 else table_ref.at[part]
        return pltpu.make_async_remote_copy(
            src_ref=src, dst_ref=table_ref.at[part],
            send_sem=table_send.at[stream, slot], recv_sem=table_recv.at[stream, slot],
            device_id=(group, peer), device_id_type=MESH,
        )

    copies = [{}, {}]
    for step in range(bits):
        for stream in range(2):
            bit = orders[stream][step]
            copy = shard_copy(stream, 0, bit)
            copy.start()
            copies[stream][1 << bit] = copy
    mine = pltpu.make_async_copy(
        shard, table_ref.at[pl.ds(pl.multiple_of(me * nodes, nodes), nodes)], local_sem
    )
    mine.start()

    events = src_ref.shape[1]
    time_row = time_ref[...].astype(f32)
    src_row = src_ref[...]
    best = []
    tile = 256
    for start in range(0, nodes, tile):
        node = lax.broadcasted_iota(jnp.int32, (tile, 128), 0) + start
        top = jnp.full((tile, 128), -1.0, f32)
        for lane in range(0, events, 128):
            hit = src_row[:, lane : lane + 128] == node
            top = jnp.maximum(top, jnp.where(hit, time_row[:, lane : lane + 128], -1.0))
        best.append(jnp.max(top.T, 0, keepdims=True))
    newest = jnp.concatenate(best, 1).astype(jnp.int32)
    newest = jnp.maximum(newest, last)
    count = jnp.sum(mask_ref[...].astype(f32), 1, keepdims=True).astype(jnp.int32)
    batch_buf[0, 0:1, :] = newest
    batch_buf[0, 1:2, :] = jnp.broadcast_to(count, (1, nodes))

    def peer_copy(step):
        return pltpu.make_async_remote_copy(
            src_ref=batch_buf.at[0], dst_ref=batch_buf.at[step],
            send_sem=batch_send.at[step], recv_sem=batch_recv.at[step],
            device_id=(lax.rem(group + step, batch), me), device_id_type=MESH,
        )

    peers = [peer_copy(step) for step in range(1, batch)]
    for copy in peers:
        copy.start()

    picks = owner_ref.shape[0]
    per_pick = nbr_ref.shape[0]
    for s in range(per_pick):
        flat = owner_ref[...] * nodes + nbr_ref[s]
        for block in range(events // 128):
            at = (s * (events // 128) + block) * picks
            flat_ref[at : at + picks, :] = flat[:, block * 128 : block * 128 + 128]
    whole = ext[0:rows, :]
    part0 = whole.astype(bf16)
    whole = whole - part0.astype(f32)
    part1 = whole.astype(bf16)
    mem3_ref[0:rows, :] = part0
    mem3_ref[rows : 2 * rows, :] = part1
    mem3_ref[2 * rows :, :] = (whole - part1.astype(f32)).astype(bf16)

    square_pad[...] = jnp.zeros_like(square_pad)
    for copy in loads:
        copy.wait()

    def put(name, value):
        square_pad[0:width, 0:width] = value
        if name in GATES:
            gates_ref[GATES.index(name)] = square_pad[...].astype(bf16)
        else:
            wsq_ref[SQUARES.index(name)] = square_pad[...].astype(bf16)

    for index in range(2):
        for gate, letter in enumerate("rzn"):
            value = gru_ref[:, index, gate * width : gate * width + width]
            put(f"g{index}{letter}", value.T)
            if index == 0:
                put(f"g0{letter}_back", value)
    for index in range(3):
        value = square_ref[:, index, :]
        put(f"s{index}", value)
        put(f"s{index}t", value.T)
    put("oa", outw_ref[:, 0:width].T)
    put("ob", outw_ref[:, width : 2 * width].T)
    wide_pad[...] = jnp.zeros_like(wide_pad)
    wide_pad[0:width, 0 : 2 * width] = outw_ref[...]
    wout_ref[...] = wide_pad[:, 0 : wout_ref.shape[1]].astype(bf16)
    wide_pad[0:width, 0 : msg_ref.shape[1]] = msg_ref[...]
    wmsg_ref[...] = wide_pad[...].astype(bf16)
    last_square = square_ref[:, 3, :]
    kv_pad[...] = jnp.zeros_like(kv_pad)
    kv_pad[0:width, 0:width] = last_square
    wd_ref[...] = kv_pad[0 : wd_ref.shape[0], 0 : wd_ref.shape[1]].astype(bf16)
    kv_pad[0:width, 0:width] = last_square.T
    wdt_ref[...] = kv_pad[0 : wdt_ref.shape[0], 0 : wdt_ref.shape[1]].astype(bf16)
    time_width = kv_ref.shape[0] - width
    kv_pad[...] = jnp.zeros_like(kv_pad)
    for index in range(2):
        part = kv_ref[:, index * width : index * width + width]
        kv_pad[index * rows : index * rows + width, 0:width] = part[0:width].T
        kv_pad[index * rows : index * rows + width, 256 : 256 + time_width] = part[width:].T
    wkv_ref[...] = kv_pad[...].astype(bf16)
    for copy in hands[:5]:
        copy.start()

    def forward(step):
        for stream in range(2):
            order = orders[stream]
            held = [0]
            for bit in order[:step]:
                held = held + [p | 1 << bit for p in held]
            for pattern in held:
                slot = pattern | 1 << order[step]
                copies[stream][slot].wait_recv()
                for bit in order[step + 1 :]:
                    copy = shard_copy(stream, slot, bit)
                    copy.start()
                    copies[stream][slot | 1 << bit] = copy

    forward(0)
    total = count
    for step, copy in enumerate(peers, 1):
        copy.wait_recv()
        newest = jnp.maximum(newest, batch_buf[step, 0:1, :])
        total = total + batch_buf[step, 1:2, 0:1]
    newest_ref[...] = newest

    cands = cand_ref.shape[1]
    own_buf[0, 0:1, :] = cand_ref[...] + me * nodes
    own_buf[0, 1:2, :] = jnp.broadcast_to(total, (1, cands))

    def owner_copy(step):
        return pltpu.make_async_remote_copy(
            src_ref=own_buf.at[0], dst_ref=own_buf.at[step],
            send_sem=own_send.at[step], recv_sem=own_recv.at[step],
            device_id=(group, lax.rem(me + step, own)), device_id_type=MESH,
        )

    owners = [owner_copy(step) for step in range(1, own)]
    for copy in owners:
        copy.start()

    edge = edge_ref.shape[0]
    high, low = freq_ref[:, 0:1], freq_ref[:, 1:2]
    stage[...] = jnp.zeros_like(stage)

    def w(name):
        return gates_ref[GATES.index(name)]

    def gru_body(c, unused):
        cs = pl.ds(pl.multiple_of(c * LANES, LANES), LANES)
        node = lax.broadcasted_iota(jnp.int32, (nodes, LANES), 0)
        onehot = (node == src_ref[:, cs]).astype(f32).astype(bf16)
        parts = nn(mem3_ref[...], onehot)
        mem = parts[:rows] + parts[rows : 2 * rows] + parts[2 * rows :]
        state["mem_src"][:, cs] = mem
        delta = time_ref[:, cs].astype(f32) - 8.0 * mem[width : width + 1] - mem[width + 1 : width + 2]
        stage[0:width, :] = mem[0:width]
        stage[width : width + edge, :] = edge_ref[:, cs].astype(f32)
        stage[width + edge : width + edge + time_width, :] = cos_rows(delta, high, low)[0:time_width]
        x = stage[...].astype(bf16)
        state["x_msg"][:, cs] = x
        m_low = mem.astype(bf16)
        state["mem_low"][:, cs] = m_low
        pre = nn(wmsg_ref[...], x)
        state["pre_msg"][:, cs] = pre
        hid = (pre * jax.nn.sigmoid(pre)).astype(bf16)
        state["hidden"][:, cs] = hid
        r = jax.nn.sigmoid(nn(w("g0r"), hid) + nn(w("g1r"), m_low))
        state["reset_gate"][:, cs] = r
        u = jax.nn.sigmoid(nn(w("g0z"), hid) + nn(w("g1z"), m_low))
        state["update"][:, cs] = u
        gn = nn(w("g1n"), m_low)
        state["gate_n"][:, cs] = gn
        cand = jnp.tanh(nn(w("g0n"), hid) + r * gn)
        state["cand_act"][:, cs] = cand
        fresh = ((1.0 - u) * cand + u * mem).astype(bf16)
        state["fresh_low"][:, cs] = fresh
        state["queries"][:, cs] = nn(w("s0t"), fresh).astype(bf16)
        return unused

    lax.fori_loop(0, events // LANES, gru_body, 0)
    for copy in hands[5:]:
        copy.start()
    for step in range(1, bits):
        forward(step)

    for step in range(own):
        if step:
            owners[step - 1].wait_recv()
            total = total + own_buf[step, 1:2, 0:1]
        source = lax.rem(me - step + own, own)
        for block in range(cands // 128):
            ids_ref[pl.ds(source * (cands // 128) + block, 1), :] = own_buf[
                step, 0:1, block * 128 : block * 128 + 128
            ]
    pos_ref[...] = jnp.broadcast_to(jnp.maximum(total.astype(f32), 1.0), pos_ref.shape)
    mine.wait()
    for copy in hands:
        copy.wait()
    for copy in peers + owners:
        copy.wait_send()
    for stream in range(2):
        for slot in copies[stream]:
            copies[stream][slot].wait_send()


def exchange(own, batch, args):
    mem, last, cand, time, mask, src, owner, nbr, freq, msg, gru, square, kv, outw, edge = args
    width, nodes = mem.shape
    events = src.shape[1]
    cands = cand.shape[1]
    rows = pad_to(width, 16)
    wide = pad_to(msg.shape[1], 16)
    vmem = pl.BlockSpec(memory_space=pltpu.VMEM)
    hbm = pl.BlockSpec(memory_space=pl.ANY)
    whole = lambda *shape: jax.ShapeDtypeStruct(shape, jnp.int32)
    handed = [
        ((len(SQUARES), rows, rows), bf16),
        ((rows, 2 * rows), bf16),
        ((2 * rows, 384), bf16),
        ((256, rows), bf16),
        ((rows, 256), bf16),
    ]
    handed += [((wide if name == "x_msg" else rows, events), bf16) for name in LOW_STATE]
    handed += [((rows, events), f32) for name in STATE]
    return pl.pallas_call(
        partial(exchange_kernel, own, batch),
        out_shape=(
            jax.ShapeDtypeStruct((own * nodes, 2, 128), bf16),
            whole(own * cands // 128, 128),
            whole(nbr.shape[0] * nbr.shape[1] * events // 128, 128),
            jax.ShapeDtypeStruct((8, 128), f32),
            whole(1, nodes),
        )
        + tuple(jax.ShapeDtypeStruct(*h) for h in handed),
        in_specs=[vmem] * 9 + [hbm] * 6,
        out_specs=(hbm,) + (vmem,) * 4 + (hbm,) * len(handed),
        scratch_shapes=[pltpu.VMEM(*h) for h in handed]
        + [pltpu.VMEM(x.shape, x.dtype) for x in (msg, gru, square, kv, outw, edge)]
        + [
            pltpu.VMEM((len(GATES), rows, rows), bf16),
            pltpu.VMEM((rows, wide), bf16),
            pltpu.VMEM((3 * rows, nodes), bf16),
            pltpu.VMEM((wide, LANES), f32),
            pltpu.VMEM((nodes, 2, 128), bf16),
            pltpu.VMEM((256, nodes), f32),
            pltpu.VMEM((2 * nodes, 128), f32),
            pltpu.VMEM((rows, rows), f32),
            pltpu.VMEM((rows, wide), f32),
            pltpu.VMEM((2 * rows, 384), f32),
            pltpu.VMEM((batch, 8, nodes), jnp.int32),
            pltpu.VMEM((own, 8, cands), jnp.int32),
            pltpu.SemaphoreType.DMA,
            pltpu.SemaphoreType.DMA((6,)),
            pltpu.SemaphoreType.DMA((len(handed),)),
            pltpu.SemaphoreType.DMA((2, own)),
            pltpu.SemaphoreType.DMA((2, own)),
            pltpu.SemaphoreType.DMA((batch,)),
            pltpu.SemaphoreType.DMA((batch,)),
            pltpu.SemaphoreType.DMA((own,)),
            pltpu.SemaphoreType.DMA((own,)),
        ],
        compiler_params=pltpu.CompilerParams(
            collective_id=1, has_side_effects=True, vmem_limit_bytes=63 * 2**20
        ),
        name="exchange",
    )(*args)


class Layout:
    def __init__(self, width, wide, deep, gates, kv_rows, kv_cols, fold):
        rows = pad_to(width, 8)
        self.width = width
        self.pieces = {}
        row = 0
        for name, depth, columns in (
            ("msg", width, wide),
            ("out", width, deep),
            ("kv", kv_rows, kv_cols),
            ("gru0", width, gates),
            ("gru1", width, gates),
            ("square0", width, width),
            ("square1", width, width),
            ("square2", width, width),
            ("square3", width, width),
        ):
            tiles = []
            for column in range(0, columns, 128):
                size = min(128, columns - column)
                if size < 128 and name[:3] in ("gru", "squ"):
                    tiles.append([column, size, None, None])
                else:
                    tiles.append([column, size, row, 0])
                    row += pad_to(depth, 8)
            self.pieces[name] = (depth, tiles)
        host = self.pieces["msg"][1][-1]
        lane = pad_to(host[1], 8)
        for name in ("gru0", "gru1"):
            tile = self.pieces[name][1][-1]
            if tile[2] is None:
                assert lane + tile[1] <= 128
                tile[2:] = [host[2], lane]
                lane += tile[1]
        for pair in range(2):
            for side in range(2):
                tile = self.pieces[f"square{2 * pair + side}"][1][-1]
                assert tile[1] <= 64
                tile[2:] = [row, 64 * side]
            row += rows
        self.loss = row
        row += 8
        self.total = pad_to(row, fold)

    def put(self, ref, name, value):
        depth, tiles = self.pieces[name]
        for column, size, row, lane in tiles:
            ref[row : row + depth, lane : lane + size] = value[:depth, column : column + size]

    def tiles(self, ref, name):
        depth, tiles = self.pieces[name]
        for column, size, row, lane in tiles:
            yield slice(column, column + size), ref[row : row + depth, lane : lane + size]


def main_kernel(
    dims,
    ids_ref, cand_ref, pos_ref, table_ref, time_ref, mask_ref, target_ref, valid_ref,
    wsq_ref, wout_ref, wkv_ref, wd_ref, wdt_ref, freq_row_ref, queries, fresh_low, *rest,
):
    late = rest[: len(LOW_STATE) + len(STATE) - 2]
    grad_ref, load_sem = rest[len(late)], rest[-1]
    held = rest[len(late) + 1 : 2 * len(late) + 1]
    x_msg, mem_low, hidden, mem_src, pre_msg, reset_gate, update, cand_act, gate_n = held
    (
        xs, xs2, x_all, time_all, kv_all, score, dest_rows, slab, eye_ref, gslab, stage,
        att_low, x_out, hid_out, emb, emb_rows, attended, pre_out,
        acc_a, grad_att, gkv_m, pick_last, rows_ref,
    ) = rest[2 * len(late) + 1 : -1]
    loads = [pltpu.make_async_copy(late[i], held[i], load_sem.at[i]) for i in range(len(late))]
    for copy in loads:
        copy.start()
    width, head_dim, keep_kv, cand_width, layout = dims
    events = time_ref.shape[1]
    per_pick, picks = valid_ref.shape[:2]
    slots = per_pick * picks
    rows = pad_to(width, 16)
    time_width = layout.pieces["kv"][0] - width
    heads = Heads(head_dim, rows)
    scale = head_dim ** (-0.5)
    high_row, low_row = freq_row_ref[0:1, :], freq_row_ref[1:2, :]
    chunks = events // LANES
    owners = cand_ref.shape[0] // cand_width

    def w(name):
        return wsq_ref[SQUARES.index(name)]

    def gather(buf, read_id, at):
        got = [table_ref[read_id(k)] for k in range(128)]
        for k in range(128):
            buf[pl.ds(pl.multiple_of(2 * at, 256) + 2 * k, 2), :] = got[k].astype(f32)

    def gathered(buf, start, count):
        base = pl.multiple_of(2 * start, 2 * count)
        return jnp.concatenate(
            [buf[pl.ds(base, count, stride=2), :], buf[pl.ds(base + 1, count, stride=2), :]], 1
        ).astype(bf16)

    grad_ref[layout.loss :, :] = jnp.zeros_like(grad_ref[layout.loss :, :])
    host = layout.pieces["msg"][1][-1][2]
    grad_ref[host : host + rows, :] = jnp.zeros((rows, 128), f32)
    eye = lax.broadcasted_iota(jnp.int32, (256, 256), 0) == lax.broadcasted_iota(jnp.int32, (256, 256), 1)
    eye_ref[...] = eye.astype(f32).astype(bf16)
    stage[...] = jnp.zeros_like(stage)
    lane = lax.broadcasted_iota(jnp.int32, (256, 128), 0)
    pick_last[...] = jnp.where(lane == width, 8.0, jnp.where(lane == width + 1, 1.0, 0.0)).astype(bf16)
    for start in range(0, events, 128):
        time_all[start : start + 128, :] = jnp.broadcast_to(
            time_ref[:, start : start + 128].astype(f32), (128, 128)
        ).T

    def cand_body(o, unused):
        def fill(i, unused):
            gather(xs, lambda k: cand_ref[o * cand_width + i * 128 + k], i * 128)
            return unused

        lax.fori_loop(0, cand_width // 128, fill, 0)
        at = pl.multiple_of(o * cand_width, cand_width)
        dest_rows[pl.ds(at, cand_width), :] = gathered(xs, 0, cand_width)
        return unused

    lax.fori_loop(0, owners, cand_body, 0)

    def lanes(c, size=LANES):
        return pl.ds(pl.multiple_of(c * size, size), size)

    def fetch(buf, j, i):
        base = ((lax.div(j, picks) * (events // 128) + i) * picks + lax.rem(j, picks)) * 128
        gather(buf, lambda k: ids_ref[base + k], i * 128)

    def slot_chunk(buf, j, c):
        cs = lanes(c)
        x = gathered(buf, c * LANES, LANES)
        delta = time_all[cs, :] - nn(x, pick_last[...])
        x = jnp.concatenate([x, cos_rows(delta, high_row, low_row).astype(bf16)], 1)
        x_all[j, cs, :] = x
        kv = nt(wkv_ref[...], x).astype(bf16)
        if keep_kv:
            kv_all[j, :, cs] = kv
        s0, s1 = heads.sums(kv[:rows].astype(f32) * queries[:, cs].astype(f32))
        live = valid_ref[lax.div(j, picks), pl.ds(lax.rem(j, picks), 1), cs] > 0
        score[j, 0:1, cs] = jnp.where(live, s0 * scale, mask_fill)
        score[j, 1:2, cs] = jnp.where(live, s1 * scale, mask_fill)

    def first_slot(i, unused):
        fetch(xs, 0, i)
        return unused

    lax.fori_loop(0, events // 128, first_slot, 0)

    def slot_pair(i, unused):
        for side, (now, later) in enumerate(((xs, xs2), (xs2, xs))):
            j = 2 * i + side
            ahead = jnp.minimum(j + 1, slots - 1)
            for c in range(chunks):
                for block in range(LANES // 128):
                    fetch(later, ahead, c * (LANES // 128) + block)
                slot_chunk(now, j, c)
        return unused

    lax.fori_loop(0, slots // 2, slot_pair, 0)

    def soft_body(c, unused):
        cs = lanes(c, 128)
        s = score[:, 0:2, cs]
        top = jnp.max(s, 0, keepdims=True)
        p = jnp.where(s > 0.5 * mask_fill, jnp.exp(s - top), 0.0)
        score[:, 0:2, cs] = p / jnp.sum(p, 0, keepdims=True)
        return unused

    lax.fori_loop(0, events // 128, soft_body, 0)

    def kv_of(j, cs, part):
        if keep_kv:
            return kv_all[j, part, cs]
        return nt(wkv_ref[part, :], x_all[j, cs, :]).astype(bf16)

    def att_body(c, unused):
        cs = lanes(c, 128)
        total = jnp.zeros((rows, 128), f32)
        for j in range(slots):
            v = kv_of(j, cs, slice(rows, 2 * rows)).astype(f32)
            total = total + heads.scale(v, score[j, 0:1, cs], score[j, 1:2, cs])
        attended[:, cs] = total
        att_low[:, cs] = total.astype(bf16)
        return unused

    lax.fori_loop(0, events // 128, att_body, 0)

    def out_body(c, unused):
        cs = lanes(c)
        stage[0:width, :] = nn(w("s1t"), att_low[:, cs])[0:width]
        stage[width : 2 * width, :] = fresh_low[:, cs].astype(f32)[0:width]
        x = stage[0 : 2 * rows, :].astype(bf16)
        x_out[:, cs] = x
        pre = nn(wout_ref[...], x)
        pre_out[:, cs] = pre
        hid = (pre * jax.nn.sigmoid(pre)).astype(bf16)
        hid_out[:, cs] = hid
        e = nn(w("s2t"), hid).astype(bf16)
        emb[:, cs] = e
        emb_rows[cs, :] = nt(eye_ref[...], e).astype(bf16)
        return unused

    lax.fori_loop(0, chunks, out_body, 0, unroll=2)

    def row_init(c, unused):
        cs = lanes(c)
        rows_ref[0:1, cs] = jnp.full((1, LANES), mask_fill, f32)
        rows_ref[1:3, cs] = jnp.zeros((2, LANES), f32)
        acc_a[:, cs] = jnp.zeros((rows, LANES), f32)
        return unused

    lax.fori_loop(0, chunks, row_init, 0)

    def dest_of(o):
        at = pl.multiple_of(o * cand_width, cand_width)
        return dest_rows[pl.ds(at, cand_width), :]

    def lse_block(i, unused):
        for side in range(2):
            o = 2 * i + side
            dest = nn(dest_of(o), wd_ref[...]).astype(bf16)
            for c in range(chunks):
                cs = lanes(c)
                logits = nn(dest, emb[:, cs])
                old = rows_ref[0:1, cs]
                top = jnp.maximum(old, jnp.max(logits, 0, keepdims=True))
                rows_ref[0:1, cs] = top
                rows_ref[1:2, cs] = rows_ref[1:2, cs] * jnp.exp(old - top) + jnp.sum(
                    jnp.exp(logits - top), 0, keepdims=True
                )
                hit = lax.broadcasted_iota(jnp.int32, logits.shape, 0) == target_ref[:, cs] - o * cand_width
                rows_ref[2:3, cs] = rows_ref[2:3, cs] + jnp.sum(jnp.where(hit, logits, 0.0), 0, keepdims=True)
        return unused

    lax.fori_loop(0, owners // 2, lse_block, 0)

    mask_row = mask_ref[...].astype(f32)
    log_sum = rows_ref[0:1, :] + jnp.log(rows_ref[1:2, :])
    rows_ref[3:4, :] = log_sum
    rows_ref[4:5, :] = mask_row / jnp.broadcast_to(pos_ref[0:1, 0:1], mask_row.shape)
    loss = jnp.sum(mask_row * (log_sum - rows_ref[2:3, :]), 1, keepdims=True)
    grad_ref[layout.loss : layout.loss + 8, :] = jnp.broadcast_to(loss, (8, 128))

    def back_block(o, grad_dest_w):
        block = dest_of(o)
        dest = nn(block, wd_ref[...]).astype(bf16)
        dest_t = nt(wdt_ref[...], block).astype(bf16)
        block_t = nt(eye_ref[...], block).astype(bf16)

        def chunk(c, unused):
            cs = lanes(c)
            logits = nn(dest, emb[:, cs])
            coeff = rows_ref[4:5, cs]
            hit = lax.broadcasted_iota(jnp.int32, logits.shape, 0) == target_ref[:, cs] - o * cand_width
            grad = jnp.exp(logits - rows_ref[3:4, cs]) - jnp.where(hit, 1.0, 0.0)
            grad = (grad * coeff).astype(bf16)
            slab[0:cand_width, cs] = grad
            return unused

        lax.fori_loop(0, chunks, chunk, 0, unroll=True)
        acc_a[...] += nn(dest_t, slab[0:cand_width, :])
        grad_dest = nn(slab[0:cand_width, :], emb_rows[...]).astype(bf16)
        return grad_dest_w + nn(block_t, grad_dest)[:rows]

    grad_dest_w = lax.fori_loop(0, owners, back_block, jnp.zeros((rows, rows), f32))
    layout.put(grad_ref, "square3", grad_dest_w)

    r0, r1, r2 = slice(0, rows), slice(rows, 2 * rows), slice(2 * rows, 3 * rows)

    def out_back(c, unused):
        cs = lanes(c)
        ge = acc_a[:, cs].astype(bf16)
        slab[r0, cs] = ge
        pre = pre_out[:, cs]
        sig = jax.nn.sigmoid(pre)
        gp = (nn(w("s2"), ge) * (sig * (1.0 + pre * (1.0 - sig)))).astype(bf16)
        slab[r1, cs] = gp
        gm = nn(w("oa"), gp).astype(bf16)
        slab[r2, cs] = gm
        acc_a[:, cs] = nn(w("ob"), gp)
        ga = nn(w("s1"), gm).astype(bf16)
        grad_att[:, cs] = ga
        d0, d1 = heads.sums(ga.astype(f32) * attended[:, cs])
        rows_ref[5:6, cs] = d0
        rows_ref[6:7, cs] = d1
        return unused

    lax.fori_loop(0, chunks, out_back, 0, unroll=2)
    layout.put(grad_ref, "square2", nt(hid_out[...], slab[r0, :]))
    layout.put(grad_ref, "out", nt(slab[r1, :], x_out[...]))
    layout.put(grad_ref, "square1", nt(att_low[...], slab[r2, :]))

    attended[...] = jnp.zeros_like(attended)
    gkv_m[...] = jnp.zeros_like(gkv_m)

    def slot_back(i, unused):
        for side in range(2):
            j = 2 * i + side
            for c in range(events // 256):
                cs = lanes(c, 256)
                kv = kv_of(j, cs, slice(0, 2 * rows)).astype(f32)
                ga = grad_att[:, cs].astype(f32)
                p0, p1 = score[j, 0:1, cs], score[j, 1:2, cs]
                g0, g1 = heads.sums(ga * kv[rows:])
                g0 = p0 * (g0 - rows_ref[5:6, cs]) * scale
                g1 = p1 * (g1 - rows_ref[6:7, cs]) * scale
                attended[:, cs] += heads.scale(kv[:rows], g0, g1)
                gslab[side, 0:rows, cs] = heads.scale(queries[:, cs].astype(f32), g0, g1).astype(bf16)
                gslab[side, rows:2*rows, cs] = heads.scale(ga, p0, p1).astype(bf16)
            both = gslab[side, 0 : 2 * rows, :]
            gkv_m[...] += nn(both, x_all[j])
        return unused

    lax.fori_loop(0, slots // 2, slot_back, 0)
    gkv = gkv_m[...].T
    both = [jnp.concatenate([g[:, :width], g[:, rows : rows + width]], 1)
            for g in (gkv[:width], gkv[256 : 256 + time_width])]
    layout.put(grad_ref, "kv", jnp.concatenate(both, 0))

    for copy in loads:
        copy.wait()
    def gru_back(c, unused):
        cs = lanes(c)
        gq = attended[:, cs].astype(bf16)
        slab[r0, cs] = gq
        gf = acc_a[:, cs] + nn(w("s0"), gq)
        u, cand, r = update[:, cs], cand_act[:, cs], reset_gate[:, cs]
        act = gf * (1.0 - u) * (1.0 - cand * cand)
        gr = (act * gate_n[:, cs] * r * (1.0 - r)).astype(bf16)
        gu = (gf * (mem_src[:, cs] - cand) * u * (1.0 - u)).astype(bf16)
        gn = act.astype(bf16)
        gh = (act * r).astype(bf16)
        slab[r1, cs] = gr
        slab[r2, cs] = gu
        x_out[0:rows, cs] = gn
        hid_out[:, cs] = gh
        pre = pre_msg[:, cs]
        sig = jax.nn.sigmoid(pre)
        back = nn(w("g0r_back"), gr) + nn(w("g0z_back"), gu) + nn(w("g0n_back"), gn)
        att_low[:, cs] = (back * (sig * (1.0 + pre * (1.0 - sig)))).astype(bf16)
        return unused

    lax.fori_loop(0, chunks, gru_back, 0, unroll=2)
    layout.put(grad_ref, "square0", nt(fresh_low[...], slab[r0, :]))
    for index, (left, last) in enumerate(((hidden, x_out[0:rows, :]), (mem_low, hid_out[...]))):
        left = left[...]
        parts = [nt(left, slab[r1, :]), nt(left, slab[r2, :]), nt(left, last)]
        layout.put(grad_ref, f"gru{index}", jnp.concatenate([p[:, :width] for p in parts], 1))
    layout.put(grad_ref, "msg", nt(att_low[...], x_msg[...]))


def main(layout, keep_kv, width, head_dim, cand_width, args):
    events = args[4].shape[1]
    slots = args[7].shape[0] * args[7].shape[1]
    late = args[16:]
    rows = pad_to(width, 16)
    cands = args[1].shape[0]
    smem = pl.BlockSpec(memory_space=pltpu.SMEM)
    vmem = pl.BlockSpec(memory_space=pltpu.VMEM)
    hbm = pl.BlockSpec(memory_space=pl.ANY)
    low = lambda *shape: pltpu.VMEM(shape, bf16)
    full = lambda *shape: pltpu.VMEM(shape, f32)
    return pl.pallas_call(
        partial(main_kernel, (width, head_dim, keep_kv, cand_width, layout)),
        out_shape=jax.ShapeDtypeStruct((layout.total, 128), f32),
        in_specs=[smem, smem] + [vmem] * 14 + [hbm] * len(late),
        out_specs=vmem,
        scratch_shapes=[pltpu.VMEM(x.shape, x.dtype) for x in late]
        + [
            full(2 * events, 128),
            full(2 * events, 128),
            low(slots, events, 384),
            full(events, 128),
            low(slots if keep_kv else 1, 2 * rows if keep_kv else 16, events),
            full(slots, 8, events),
            low(cands, 256),
            low(max(3 * rows, cand_width), events),
            low(256, 256),
            low(2, max(2 * rows, cand_width), events),
            full(2 * rows, LANES),
            low(rows, events),
            low(2 * rows, events),
            low(rows, events),
            low(rows, events),
            low(events, rows),
            full(rows, events),
            full(rows, events),
            full(rows, events),
            low(rows, events),
            full(2 * rows, 384),
            low(256, 128),
            full(8, events),
            pltpu.SemaphoreType.DMA((len(late),)),
        ],
        compiler_params=pltpu.CompilerParams(vmem_limit_bytes=63 * 2**20),
        name="train",
    )(*args)


def reduce_kernel(own, batch, streams, grad_ref, out_ref, acc, recv, send_sem, recv_sem):
    place = {"own": lax.axis_index("own"), "batch": lax.axis_index("batch")}
    rounds = len(streams[0][2])

    def peers(axis, bit):
        if axis == "own":
            return [(place["batch"], flip_bit(place["own"], bit))]
        return [(lax.rem(place["batch"] + d, batch), place["own"]) for d in range(1, batch)]

    barrier = pltpu.get_barrier_semaphore()
    signals = 0
    for axis, bit in streams[0][2]:
        for peer in peers(axis, bit):
            pl.semaphore_signal(barrier, inc=1, device_id=peer, device_id_type=MESH)
            signals += 1
    pl.semaphore_wait(barrier, signals)

    sent = []

    class Stream:
        def __init__(self, index, start, size, order):
            self.index, self.base, self.size, self.inner, self.order = index, start, size, start, order
            self.copies = []

        def copy(self, source, target, peer, slot):
            copy = pltpu.make_async_remote_copy(
                src_ref=source, dst_ref=target,
                send_sem=send_sem.at[self.index, slot], recv_sem=recv_sem.at[self.index, slot],
                device_id=peer, device_id_type=MESH,
            )
            copy.start()
            self.copies.append(copy)
            sent.append(copy)

        def parts(self, axis, bit):
            if axis == "own":
                return 2, lax.div(place["own"], 1 << bit) % 2
            return batch, place["batch"]

        def scatter(self, step):
            axis, bit = self.order[step]
            count, mine = self.parts(axis, bit)
            piece = self.size // count
            source = grad_ref if step == 0 else acc
            for d, peer in enumerate(peers(axis, bit), 1):
                theirs = 1 - mine if axis == "own" else peer[0]
                away = pl.multiple_of(self.base + theirs * piece, 8)
                self.copy(
                    source.at[pl.ds(away, piece), :], recv.at[pl.ds(self.inner + (d - 1) * piece, piece), :],
                    peer, step * (batch - 1) + d - 1,
                )
            self.base = pl.multiple_of(self.base + mine * piece, 8)
            self.size = piece

        def add(self, step):
            source = grad_ref if step == 0 else acc
            target = out_ref if step == rounds - 1 else acc
            part = pl.ds(self.base, self.size)
            total = source[part, :]
            for copy in self.copies:
                copy.wait_recv()
                total = total + recv[pl.ds(self.inner, self.size), :]
                self.inner += self.size
            target[part, :] = total
            self.copies = []

        def gather(self, step):
            axis, bit = self.order[step]
            count, mine = self.parts(axis, bit)
            part = pl.ds(self.base, self.size)
            for d, peer in enumerate(peers(axis, bit), 1):
                self.copy(out_ref.at[part, :], out_ref.at[part, :], peer, (rounds + step) * (batch - 1) + d - 1)
            self.base = pl.multiple_of(self.base - mine * self.size, 8)
            self.size *= count

        def gathered(self):
            for copy in self.copies:
                copy.wait_recv()
            self.copies = []

    flows = [Stream(index, *stream) for index, stream in enumerate(streams)]
    for step in range(2 * rounds + 1):
        for flow in flows:
            if 0 < step <= rounds:
                flow.add(step - 1)
            elif step > rounds:
                flow.gathered()
            if step < rounds:
                flow.scatter(step)
            elif step < 2 * rounds:
                flow.gather(2 * rounds - 1 - step)
    for copy in sent:
        copy.wait_send()


def reduce_all(own, batch, packed):
    total = packed.shape[0]
    own_bits = own.bit_length() - 1
    fold = 8 * own * batch
    rest = [("own", b) for b in range(1, own_bits)]
    cut = len(rest) // 2
    axes = [rest[:cut], rest[cut:], [("batch", 0)]]
    blocks = total // fold
    halves = 1
    streams = []
    start = 0
    for index in range(3 * halves):
        size = (blocks + 3 * halves - 1 - index) // (3 * halves) * fold
        turn = index % 3
        order = [("own", 0)] + [bit for part in axes[turn:] + axes[:turn] for bit in part]
        if size:
            streams.append((start, size, order))
            start += size
    count = 2 * len(streams[0][2]) * (batch - 1)
    return pl.pallas_call(
        partial(reduce_kernel, own, batch, streams),
        out_shape=jax.ShapeDtypeStruct(packed.shape, f32),
        in_specs=[pl.BlockSpec(memory_space=pltpu.VMEM)],
        out_specs=pl.BlockSpec(memory_space=pltpu.VMEM),
        scratch_shapes=[
            pltpu.VMEM(packed.shape, f32),
            pltpu.VMEM(packed.shape, f32),
            pltpu.SemaphoreType.DMA((len(streams), count)),
            pltpu.SemaphoreType.DMA((len(streams), count)),
        ],
        compiler_params=pltpu.CompilerParams(
            collective_id=2, has_side_effects=True, vmem_limit_bytes=63 * 2**20
        ),
        name="reduce",
    )(packed)


def update_kernel(layout, step_rate, grad_ref, pos_ref, *refs):
    sources, targets, loss_ref, count_ref = refs[:15], refs[15:30], refs[30], refs[31]
    held, laid = refs[32:47], refs[47:49]
    in_sem, out_sem = refs[49:]
    loss_ref[...] = grad_ref[layout.loss : layout.loss + 1, 0:1]
    count_ref[...] = pos_ref[0:1, 0:1]
    arrive = [pltpu.make_async_copy(sources[i], held[i], in_sem.at[i]) for i in range(15)]
    leave = [pltpu.make_async_copy(held[i], targets[(i + 5) % 10 if i < 10 else i], out_sem.at[i]) for i in range(15)]
    order = (1, 2, 0, 3, 4)
    for index in order:
        for kind in range(3):
            arrive[5 * kind + index].start()

    for ref, name, parts in ((laid[0], "gru", 2), (laid[1], "square", 4)):
        for part in range(parts):
            for columns, gradient in layout.tiles(grad_ref, f"{name}{part}"):
                ref[:, part, columns] = gradient

    def step(index, at, gradient):
        weights, moments, averages = (held[5 * kind + index] for kind in range(3))
        moment = mu_coef * moments[at] + gradient
        weight = weights[at] - step_rate * (gradient + mu_coef * moment)
        moments[at] = moment
        weights[at] = weight
        averages[at] = (1.0 - avg_coef) * averages[at] + avg_coef * weight

    for index in order:
        for kind in range(3):
            arrive[5 * kind + index].wait()
        if index in (1, 2):
            step(index, slice(None), laid[index - 1][...])
        else:
            for columns, gradient in layout.tiles(grad_ref, ("msg", "", "", "kv", "out")[index]):
                step(index, (slice(None), columns), gradient)
        for kind in range(3):
            leave[5 * kind + index].start()
    for copy in leave:
        copy.wait()


def update_all(layout, step_rate, packed, positives, params):
    vmem = pl.BlockSpec(memory_space=pltpu.VMEM)
    hbm = pl.BlockSpec(memory_space=pl.ANY)
    buffers = [pltpu.VMEM(p.shape, f32) for p in params]
    return pl.pallas_call(
        partial(update_kernel, layout, step_rate),
        out_shape=tuple(jax.ShapeDtypeStruct(p.shape, f32) for p in params[5:10] + params[:5] + params[10:])
        + (jax.ShapeDtypeStruct((1, 1), f32),) * 2,
        in_specs=[vmem] * 2 + [hbm] * 15,
        out_specs=(hbm,) * 15 + (vmem,) * 2,
        scratch_shapes=buffers + buffers[1:3] + [pltpu.SemaphoreType.DMA((15,))] * 2,
        compiler_params=pltpu.CompilerParams(vmem_limit_bytes=63 * 2**20),
        name="update",
    )(packed, positives, *params)


def turned(arrays):
    msg, gru, square, kv, out = arrays
    return (msg.T, gru.transpose(1, 0, 2), square.transpose(1, 0, 2), kv, out.T)


def local(
    memory, last_update, src_local, edge_feat, event_time, nbr_owner, nbr_ids, nbr_mask, event_mask,
    dest_local, target, w_msg, w_gru, w_square, w_key_value, w_output,
    mom_msg, mom_gru, mom_square, mom_key_value, mom_output,
    avg_msg, avg_gru, avg_square, avg_key_value, avg_output,
):
    own = lax.axis_size("own")
    batch = lax.axis_size("batch")
    events, edge = edge_feat.shape
    nodes, width = memory.shape
    head_dim = width // HEADS
    time_width = w_key_value.shape[0] - width
    columns = time_columns(time_width, 128)
    layout = Layout(
        width, w_msg.shape[0], w_output.shape[0], w_gru.shape[2], *w_key_value.shape, 8 * own * batch
    )
    weights = turned((w_msg, w_gru, w_square, w_key_value, w_output))
    time_row, mask_row, src_row, target_row = (x[None, :] for x in (event_time, event_mask, src_local, target))
    table, cand_ids, flat_ids, positives, newest, *handed = exchange(
        own, batch,
        (memory.T, last_update[None, :], dest_local[None, :], time_row, mask_row, src_row,
         nbr_owner.T, nbr_ids.transpose(2, 1, 0), jnp.asarray(columns)) + weights + (edge_feat.T,),
    )
    packed = main(
        layout, own * nodes <= 16384, width, head_dim, dest_local.shape[0],
        (flat_ids.reshape(-1), cand_ids.reshape(-1), positives, table, time_row, mask_row, target_row,
         nbr_mask.transpose(2, 1, 0), *handed[:5], jnp.asarray(columns.T[:8]), *handed[5:]),
    )
    summed = reduce_all(own, batch, packed)
    step_rate = rate_coef * math.sqrt(events * own * batch)
    *states, loss, count = update_all(
        layout, step_rate, summed, positives,
        weights
        + turned((mom_msg, mom_gru, mom_square, mom_key_value, mom_output))
        + turned((avg_msg, avg_gru, avg_square, avg_key_value, avg_output)),
    )
    states = [x for i in range(3) for x in turned(states[5 * i : 5 * i + 5])]
    return (loss.reshape(()), count.reshape(()), newest.reshape(-1), *states)


def solution(mesh):
    row = P(("batch", "own"))
    placed = (
        (P("own", None), P("own"), row, P(("batch", "own"), None), row, P(("batch", "own"), None))
        + (P(("batch", "own"), None, None),) * 2
        + (row,) * 3
        + (P(),) * 15
    )
    return jax.shard_map(
        local,
        mesh=mesh,
        in_specs=placed,
        out_specs=(P(), P(), P("own")) + (P(),) * 15,
        check_vma=False,
    )
```

```python
from functools import partial
import math

import jax
import jax.numpy as jnp
import numpy as np
from jax import lax
from jax.experimental import pallas as pl
from jax.experimental.pallas import tpu as pltpu
from jax.sharding import PartitionSpec as P

HEADS = 2
LANES = 256
MESH = pl.DeviceIdType.MESH
f32 = jnp.float32
bf16 = jnp.bfloat16

mu_coef = 0.9
avg_coef = 0.1
rate_coef = 0.008
mask_fill = -1e30

COS_TERMS = (
    1.0,
    -19.73920440673828,
    64.93911743164062,
    -85.45011901855469,
    60.16745376586914,
    -25.966907501220703,
    6.527653217315674,
)


def pad_to(size, step):
    return -(-size // step) * step


def nn(a, b):
    return lax.dot_general(a, b, (((1,), (0,)), ((), ())), preferred_element_type=f32)


def nt(a, b):
    return lax.dot_general(a, b, (((1,), (1,)), ((), ())), preferred_element_type=f32)


def flip_bit(index, bit):
    size = 1 << bit
    return index + size * (1 - 2 * (lax.div(index, size) % 2))


def time_columns(time_width, rows):
    turns = 10.0 ** (-np.linspace(0.0, 9.0, time_width)) / (2.0 * np.pi)
    mant, expo = np.frexp(turns)
    high = np.ldexp(np.round(mant * 4096.0) / 4096.0, expo)
    out = np.zeros((rows, 128), np.float32)
    out[:time_width, 0] = high
    out[:time_width, 1] = turns - high
    return out


def cos_rows(delta, high, low):
    turns = delta * high
    rest = turns - jnp.floor(turns + 0.5) + delta * low
    square = rest * rest
    value = square * COS_TERMS[-1] + COS_TERMS[-2]
    for term in COS_TERMS[-3::-1]:
        value = value * square + term
    return value


class Heads:
    def __init__(self, head_dim, rows):
        self.low = head_dim // 8 * 8
        self.high = pad_to(head_dim, 8)
        self.cut = head_dim - self.low
        self.rows = rows

    def split(self, lanes):
        return lax.broadcasted_iota(jnp.int32, (8, lanes), 0) < self.cut

    def sums(self, x):
        lanes = x.shape[1]
        mid = x[self.low : self.high]
        first = self.split(lanes)
        a = jnp.sum(x[: self.low].reshape(self.low // 8, 8, lanes), 0)
        b = jnp.sum(x[self.high :].reshape((self.rows - self.high) // 8, 8, lanes), 0)
        a = a + jnp.where(first, mid, 0.0)
        b = b + jnp.where(first, 0.0, mid)
        return jnp.sum(a, 0, keepdims=True), jnp.sum(b, 0, keepdims=True)

    def scale(self, x, p0, p1):
        lanes = x.shape[1]
        mid = jnp.where(self.split(lanes), p0, p1)
        return jnp.concatenate(
            [x[: self.low] * p0, x[self.low : self.high] * mid, x[self.high :] * p1], 0
        )


GATES = ("g0r", "g0z", "g0n", "g1r", "g1z", "g1n", "s0t")
SQUARES = ("s1t", "s2t", "g0r_back", "g0z_back", "g0n_back", "s0", "s1", "s2", "oa", "ob")
LOW_STATE = ("queries", "fresh_low", "x_msg", "mem_low", "hidden")
STATE = ("mem_src", "pre_msg", "reset_gate", "update", "cand_act", "gate_n")


def exchange_kernel(
    own, batch,
    mem_ref, last_ref, cand_ref, time_ref, mask_ref, src_ref, owner_ref, nbr_ref, freq_ref,
    msg_hbm, gru_hbm, square_hbm, kv_hbm, outw_hbm, edge_hbm,
    table_ref, ids_ref, flat_ref, pos_ref, newest_ref, *rest,
):
    handed = rest[: 5 + len(LOW_STATE) + len(STATE)]
    rest = rest[len(handed) :]
    staged = rest[: len(handed)]
    wsq_ref, wout_ref, wkv_ref, wd_ref, wdt_ref = staged[:5]
    state = dict(zip(LOW_STATE + STATE, staged[5:]))
    (msg_ref, gru_ref, square_ref, kv_ref, outw_ref, edge_ref, gates_ref, wmsg_ref, mem3_ref, stage,
     shard, ext, pairs, square_pad, wide_pad, kv_pad, batch_buf, own_buf,
     local_sem, load_sem, hand_sem,
     table_send, table_recv, batch_send, batch_recv, own_send, own_recv) = rest[len(handed) :]
    loads = [
        pltpu.make_async_copy(source, target, load_sem.at[i])
        for i, (source, target) in enumerate((
            (gru_hbm, gru_ref), (square_hbm, square_ref), (outw_hbm, outw_ref),
            (msg_hbm, msg_ref), (kv_hbm, kv_ref), (edge_hbm, edge_ref),
        ))
    ]
    for copy in loads:
        copy.start()
    hands = [pltpu.make_async_copy(staged[i], handed[i], hand_sem.at[i]) for i in range(len(handed))]
    me = lax.axis_index("own")
    group = lax.axis_index("batch")
    barrier = pltpu.get_barrier_semaphore()
    for step in range(1, own):
        pl.semaphore_signal(barrier, inc=1, device_id=(group, lax.rem(me + step, own)), device_id_type=MESH)
    for step in range(1, batch):
        pl.semaphore_signal(barrier, inc=1, device_id=(lax.rem(group + step, batch), me), device_id_type=MESH)

    width, nodes = mem_ref.shape
    rows = pad_to(width, 16)
    ext[...] = jnp.zeros_like(ext)
    ext[0:width, :] = mem_ref[...]
    last = last_ref[...]
    ext[width : width + 1, :] = lax.div(last, 8).astype(f32)
    ext[width + 1 : width + 2, :] = lax.rem(last, 8).astype(f32)

    def turn(i, unused):
        block = ext[:, pl.ds(pl.multiple_of(i * 128, 128), 128)].T
        base = pl.multiple_of(i * 256, 256)
        pairs[pl.ds(base, 128, stride=2), :] = block[:, :128]
        pairs[pl.ds(base + 1, 128, stride=2), :] = block[:, 128:]
        return unused

    lax.fori_loop(0, nodes // 128, turn, 0)

    def pack(i, unused):
        got = [pairs[pl.ds(pl.multiple_of(i * 128, 128) + 2 * k, 2), :] for k in range(64)]
        for k in range(64):
            shard[i * 64 + k] = got[k].astype(bf16)
        return unused

    lax.fori_loop(0, nodes // 64, pack, 0)
    pl.semaphore_wait(barrier, own + batch - 2)

    half = nodes // 2
    bits = own.bit_length() - 1
    others = list(range(1, bits))
    cut = len(others) // 2
    orders = (others + [0], others[cut:] + others[:cut] + [0])

    def shard_copy(stream, pattern, bit):
        peer = flip_bit(me, bit)
        source = me
        for b in range(bits):
            if pattern >> b & 1:
                source = flip_bit(source, b)
        part = pl.ds(pl.multiple_of(source * nodes + stream * half, half), half)
        slot = pattern | 1 << bit
        src = shard.at[pl.ds(stream * half, half)] if pattern == 0 else table_ref.at[part]
        return pltpu.make_async_remote_copy(
            src_ref=src, dst_ref=table_ref.at[part],
            send_sem=table_send.at[stream, slot], recv_sem=table_recv.at[stream, slot],
            device_id=(group, peer), device_id_type=MESH,
        )

    copies = [{}, {}]
    for step in range(bits):
        for stream in range(2):
            bit = orders[stream][step]
            copy = shard_copy(stream, 0, bit)
            copy.start()
            copies[stream][1 << bit] = copy
    mine = pltpu.make_async_copy(
        shard, table_ref.at[pl.ds(pl.multiple_of(me * nodes, nodes), nodes)], local_sem
    )
    mine.start()

    events = src_ref.shape[1]
    time_row = time_ref[...].astype(f32)
    src_row = src_ref[...]
    best = []
    tile = 256
    for start in range(0, nodes, tile):
        node = lax.broadcasted_iota(jnp.int32, (tile, 128), 0) + start
        top = jnp.full((tile, 128), -1.0, f32)
        for lane in range(0, events, 128):
            hit = src_row[:, lane : lane + 128] == node
            top = jnp.maximum(top, jnp.where(hit, time_row[:, lane : lane + 128], -1.0))
        best.append(jnp.max(top.T, 0, keepdims=True))
    newest = jnp.concatenate(best, 1).astype(jnp.int32)
    newest = jnp.maximum(newest, last)
    count = jnp.sum(mask_ref[...].astype(f32), 1, keepdims=True).astype(jnp.int32)
    batch_buf[0, 0:1, :] = newest
    batch_buf[0, 1:2, :] = jnp.broadcast_to(count, (1, nodes))

    def peer_copy(step):
        return pltpu.make_async_remote_copy(
            src_ref=batch_buf.at[0], dst_ref=batch_buf.at[step],
            send_sem=batch_send.at[step], recv_sem=batch_recv.at[step],
            device_id=(lax.rem(group + step, batch), me), device_id_type=MESH,
        )

    peers = [peer_copy(step) for step in range(1, batch)]
    for copy in peers:
        copy.start()

    picks = owner_ref.shape[0]
    per_pick = nbr_ref.shape[0]
    for s in range(per_pick):
        flat = owner_ref[...] * nodes + nbr_ref[s]
        for block in range(events // 128):
            at = (s * (events // 128) + block) * picks
            flat_ref[at : at + picks, :] = flat[:, block * 128 : block * 128 + 128]
    whole = ext[0:rows, :]
    part0 = whole.astype(bf16)
    whole = whole - part0.astype(f32)
    part1 = whole.astype(bf16)
    mem3_ref[0:rows, :] = part0
    mem3_ref[rows : 2 * rows, :] = part1
    mem3_ref[2 * rows :, :] = (whole - part1.astype(f32)).astype(bf16)

    square_pad[...] = jnp.zeros_like(square_pad)
    for copy in loads:
        copy.wait()

    def put(name, value):
        square_pad[0:width, 0:width] = value
        if name in GATES:
            gates_ref[GATES.index(name)] = square_pad[...].astype(bf16)
        else:
            wsq_ref[SQUARES.index(name)] = square_pad[...].astype(bf16)

    for index in range(2):
        for gate, letter in enumerate("rzn"):
            value = gru_ref[:, index, gate * width : gate * width + width]
            put(f"g{index}{letter}", value.T)
            if index == 0:
                put(f"g0{letter}_back", value)
    for index in range(3):
        value = square_ref[:, index, :]
        put(f"s{index}", value)
        put(f"s{index}t", value.T)
    put("oa", outw_ref[:, 0:width].T)
    put("ob", outw_ref[:, width : 2 * width].T)
    wide_pad[...] = jnp.zeros_like(wide_pad)
    wide_pad[0:width, 0 : 2 * width] = outw_ref[...]
    wout_ref[...] = wide_pad[:, 0 : wout_ref.shape[1]].astype(bf16)
    wide_pad[0:width, 0 : msg_ref.shape[1]] = msg_ref[...]
    wmsg_ref[...] = wide_pad[...].astype(bf16)
    last_square = square_ref[:, 3, :]
    kv_pad[...] = jnp.zeros_like(kv_pad)
    kv_pad[0:width, 0:width] = last_square
    wd_ref[...] = kv_pad[0 : wd_ref.shape[0], 0 : wd_ref.shape[1]].astype(bf16)
    kv_pad[0:width, 0:width] = last_square.T
    wdt_ref[...] = kv_pad[0 : wdt_ref.shape[0], 0 : wdt_ref.shape[1]].astype(bf16)
    time_width = kv_ref.shape[0] - width
    kv_pad[...] = jnp.zeros_like(kv_pad)
    for index in range(2):
        part = kv_ref[:, index * width : index * width + width]
        kv_pad[index * rows : index * rows + width, 0:width] = part[0:width].T
        kv_pad[index * rows : index * rows + width, 256 : 256 + time_width] = part[width:].T
    wkv_ref[...] = kv_pad[...].astype(bf16)
    for copy in hands[:5]:
        copy.start()

    def forward(step):
        for stream in range(2):
            order = orders[stream]
            held = [0]
            for bit in order[:step]:
                held = held + [p | 1 << bit for p in held]
            for pattern in held:
                slot = pattern | 1 << order[step]
                copies[stream][slot].wait_recv()
                for bit in order[step + 1 :]:
                    copy = shard_copy(stream, slot, bit)
                    copy.start()
                    copies[stream][slot | 1 << bit] = copy

    forward(0)
    total = count
    for step, copy in enumerate(peers, 1):
        copy.wait_recv()
        newest = jnp.maximum(newest, batch_buf[step, 0:1, :])
        total = total + batch_buf[step, 1:2, 0:1]
    newest_ref[...] = newest

    cands = cand_ref.shape[1]
    own_buf[0, 0:1, :] = cand_ref[...] + me * nodes
    own_buf[0, 1:2, :] = jnp.broadcast_to(total, (1, cands))

    def owner_copy(step):
        return pltpu.make_async_remote_copy(
            src_ref=own_buf.at[0], dst_ref=own_buf.at[step],
            send_sem=own_send.at[step], recv_sem=own_recv.at[step],
            device_id=(group, lax.rem(me + step, own)), device_id_type=MESH,
        )

    owners = [owner_copy(step) for step in range(1, own)]
    for copy in owners:
        copy.start()

    edge = edge_ref.shape[0]
    high, low = freq_ref[:, 0:1], freq_ref[:, 1:2]
    stage[...] = jnp.zeros_like(stage)

    def w(name):
        return gates_ref[GATES.index(name)]

    def gru_body(c, unused):
        cs = pl.ds(pl.multiple_of(c * LANES, LANES), LANES)
        node = lax.broadcasted_iota(jnp.int32, (nodes, LANES), 0)
        onehot = (node == src_ref[:, cs]).astype(f32).astype(bf16)
        parts = nn(mem3_ref[...], onehot)
        mem = parts[:rows] + parts[rows : 2 * rows] + parts[2 * rows :]
        state["mem_src"][:, cs] = mem
        delta = time_ref[:, cs].astype(f32) - 8.0 * mem[width : width + 1] - mem[width + 1 : width + 2]
        stage[0:width, :] = mem[0:width]
        stage[width : width + edge, :] = edge_ref[:, cs].astype(f32)
        stage[width + edge : width + edge + time_width, :] = cos_rows(delta, high, low)[0:time_width]
        x = stage[...].astype(bf16)
        state["x_msg"][:, cs] = x
        m_low = mem.astype(bf16)
        state["mem_low"][:, cs] = m_low
        pre = nn(wmsg_ref[...], x)
        state["pre_msg"][:, cs] = pre
        hid = (pre * jax.nn.sigmoid(pre)).astype(bf16)
        state["hidden"][:, cs] = hid
        r = jax.nn.sigmoid(nn(w("g0r"), hid) + nn(w("g1r"), m_low))
        state["reset_gate"][:, cs] = r
        u = jax.nn.sigmoid(nn(w("g0z"), hid) + nn(w("g1z"), m_low))
        state["update"][:, cs] = u
        gn = nn(w("g1n"), m_low)
        state["gate_n"][:, cs] = gn
        cand = jnp.tanh(nn(w("g0n"), hid) + r * gn)
        state["cand_act"][:, cs] = cand
        fresh = ((1.0 - u) * cand + u * mem).astype(bf16)
        state["fresh_low"][:, cs] = fresh
        state["queries"][:, cs] = nn(w("s0t"), fresh).astype(bf16)
        return unused

    lax.fori_loop(0, events // LANES, gru_body, 0)
    for copy in hands[5:]:
        copy.start()
    for step in range(1, bits):
        forward(step)

    for step in range(own):
        if step:
            owners[step - 1].wait_recv()
            total = total + own_buf[step, 1:2, 0:1]
        source = lax.rem(me - step + own, own)
        for block in range(cands // 128):
            ids_ref[pl.ds(source * (cands // 128) + block, 1), :] = own_buf[
                step, 0:1, block * 128 : block * 128 + 128
            ]
    pos_ref[...] = jnp.broadcast_to(jnp.maximum(total.astype(f32), 1.0), pos_ref.shape)
    mine.wait()
    for copy in hands:
        copy.wait()
    for copy in peers + owners:
        copy.wait_send()
    for stream in range(2):
        for slot in copies[stream]:
            copies[stream][slot].wait_send()


def exchange(own, batch, args):
    mem, last, cand, time, mask, src, owner, nbr, freq, msg, gru, square, kv, outw, edge = args
    width, nodes = mem.shape
    events = src.shape[1]
    cands = cand.shape[1]
    rows = pad_to(width, 16)
    wide = pad_to(msg.shape[1], 16)
    vmem = pl.BlockSpec(memory_space=pltpu.VMEM)
    hbm = pl.BlockSpec(memory_space=pl.ANY)
    whole = lambda *shape: jax.ShapeDtypeStruct(shape, jnp.int32)
    handed = [
        ((len(SQUARES), rows, rows), bf16),
        ((rows, 2 * rows), bf16),
        ((2 * rows, 384), bf16),
        ((256, rows), bf16),
        ((rows, 256), bf16),
    ]
    handed += [((wide if name == "x_msg" else rows, events), bf16) for name in LOW_STATE]
    handed += [((rows, events), f32) for name in STATE]
    return pl.pallas_call(
        partial(exchange_kernel, own, batch),
        out_shape=(
            jax.ShapeDtypeStruct((own * nodes, 2, 128), bf16),
            whole(own * cands // 128, 128),
            whole(nbr.shape[0] * nbr.shape[1] * events // 128, 128),
            jax.ShapeDtypeStruct((8, 128), f32),
            whole(1, nodes),
        )
        + tuple(jax.ShapeDtypeStruct(*h) for h in handed),
        in_specs=[vmem] * 9 + [hbm] * 6,
        out_specs=(hbm,) + (vmem,) * 4 + (hbm,) * len(handed),
        scratch_shapes=[pltpu.VMEM(*h) for h in handed]
        + [pltpu.VMEM(x.shape, x.dtype) for x in (msg, gru, square, kv, outw, edge)]
        + [
            pltpu.VMEM((len(GATES), rows, rows), bf16),
            pltpu.VMEM((rows, wide), bf16),
            pltpu.VMEM((3 * rows, nodes), bf16),
            pltpu.VMEM((wide, LANES), f32),
            pltpu.VMEM((nodes, 2, 128), bf16),
            pltpu.VMEM((256, nodes), f32),
            pltpu.VMEM((2 * nodes, 128), f32),
            pltpu.VMEM((rows, rows), f32),
            pltpu.VMEM((rows, wide), f32),
            pltpu.VMEM((2 * rows, 384), f32),
            pltpu.VMEM((batch, 8, nodes), jnp.int32),
            pltpu.VMEM((own, 8, cands), jnp.int32),
            pltpu.SemaphoreType.DMA,
            pltpu.SemaphoreType.DMA((6,)),
            pltpu.SemaphoreType.DMA((len(handed),)),
            pltpu.SemaphoreType.DMA((2, own)),
            pltpu.SemaphoreType.DMA((2, own)),
            pltpu.SemaphoreType.DMA((batch,)),
            pltpu.SemaphoreType.DMA((batch,)),
            pltpu.SemaphoreType.DMA((own,)),
            pltpu.SemaphoreType.DMA((own,)),
        ],
        compiler_params=pltpu.CompilerParams(
            collective_id=1, has_side_effects=True, vmem_limit_bytes=63 * 2**20
        ),
        name="exchange",
    )(*args)


class Layout:
    def __init__(self, width, wide, deep, gates, kv_rows, kv_cols, fold):
        rows = pad_to(width, 8)
        self.width = width
        self.pieces = {}
        row = 0
        for name, depth, columns in (
            ("msg", width, wide),
            ("out", width, deep),
            ("kv", kv_rows, kv_cols),
            ("gru0", width, gates),
            ("gru1", width, gates),
            ("square0", width, width),
            ("square1", width, width),
            ("square2", width, width),
            ("square3", width, width),
        ):
            tiles = []
            for column in range(0, columns, 128):
                size = min(128, columns - column)
                if size < 128 and name[:3] in ("gru", "squ"):
                    tiles.append([column, size, None, None])
                else:
                    tiles.append([column, size, row, 0])
                    row += pad_to(depth, 8)
            self.pieces[name] = (depth, tiles)
        host = self.pieces["msg"][1][-1]
        lane = pad_to(host[1], 8)
        for name in ("gru0", "gru1"):
            tile = self.pieces[name][1][-1]
            if tile[2] is None:
                assert lane + tile[1] <= 128
                tile[2:] = [host[2], lane]
                lane += tile[1]
        for pair in range(2):
            for side in range(2):
                tile = self.pieces[f"square{2 * pair + side}"][1][-1]
                assert tile[1] <= 64
                tile[2:] = [row, 64 * side]
            row += rows
        self.loss = row
        row += 8
        self.total = pad_to(row, fold)

    def put(self, ref, name, value):
        depth, tiles = self.pieces[name]
        for column, size, row, lane in tiles:
            ref[row : row + depth, lane : lane + size] = value[:depth, column : column + size]

    def tiles(self, ref, name):
        depth, tiles = self.pieces[name]
        for column, size, row, lane in tiles:
            yield slice(column, column + size), ref[row : row + depth, lane : lane + size]


def main_kernel(
    dims,
    ids_ref, cand_ref, pos_ref, table_ref, time_ref, mask_ref, target_ref, valid_ref,
    wsq_ref, wout_ref, wkv_ref, wd_ref, wdt_ref, freq_row_ref, queries, fresh_low, *rest,
):
    late = rest[: len(LOW_STATE) + len(STATE) - 2]
    grad_ref, load_sem = rest[len(late)], rest[-1]
    held = rest[len(late) + 1 : 2 * len(late) + 1]
    x_msg, mem_low, hidden, mem_src, pre_msg, reset_gate, update, cand_act, gate_n = held
    (
        xs, xs2, x_all, time_all, kv_all, score, dest_rows, slab, eye_ref, gslab, stage,
        att_low, x_out, hid_out, emb, emb_rows, attended, pre_out,
        acc_a, grad_att, gkv_m, pick_last, rows_ref,
    ) = rest[2 * len(late) + 1 : -1]
    loads = [pltpu.make_async_copy(late[i], held[i], load_sem.at[i]) for i in range(len(late))]
    for copy in loads:
        copy.start()
    width, head_dim, keep_kv, cand_width, layout = dims
    events = time_ref.shape[1]
    per_pick, picks = valid_ref.shape[:2]
    slots = per_pick * picks
    rows = pad_to(width, 16)
    time_width = layout.pieces["kv"][0] - width
    heads = Heads(head_dim, rows)
    scale = head_dim ** (-0.5)
    high_row, low_row = freq_row_ref[0:1, :], freq_row_ref[1:2, :]
    chunks = events // LANES
    owners = cand_ref.shape[0] // cand_width

    def w(name):
        return wsq_ref[SQUARES.index(name)]

    def gather(buf, read_id, at):
        got = [table_ref[read_id(k)] for k in range(128)]
        for k in range(0, 128, 2):
            pair = jnp.concatenate([got[k].astype(f32), got[k + 1].astype(f32)], 0)
            buf[pl.ds(pl.multiple_of(2 * at, 256) + 2 * k, 4), :] = pair

    def gathered(buf, start, count):
        base = pl.multiple_of(2 * start, 2 * count)
        return jnp.concatenate(
            [buf[pl.ds(base, count, stride=2), :], buf[pl.ds(base + 1, count, stride=2), :]], 1
        ).astype(bf16)

    grad_ref[layout.loss :, :] = jnp.zeros_like(grad_ref[layout.loss :, :])
    host = layout.pieces["msg"][1][-1][2]
    grad_ref[host : host + rows, :] = jnp.zeros((rows, 128), f32)
    eye = lax.broadcasted_iota(jnp.int32, (256, 256), 0) == lax.broadcasted_iota(jnp.int32, (256, 256), 1)
    eye_ref[...] = eye.astype(f32).astype(bf16)
    stage[...] = jnp.zeros_like(stage)
    lane = lax.broadcasted_iota(jnp.int32, (256, 128), 0)
    pick_last[...] = jnp.where(lane == width, 8.0, jnp.where(lane == width + 1, 1.0, 0.0)).astype(bf16)
    for start in range(0, events, 128):
        time_all[start : start + 128, :] = jnp.broadcast_to(
            time_ref[:, start : start + 128].astype(f32), (128, 128)
        ).T

    def cand_body(o, unused):
        def fill(i, unused):
            gather(xs, lambda k: cand_ref[o * cand_width + i * 128 + k], i * 128)
            return unused

        lax.fori_loop(0, cand_width // 128, fill, 0)
        at = pl.multiple_of(o * cand_width, cand_width)
        dest_rows[pl.ds(at, cand_width), :] = gathered(xs, 0, cand_width)
        return unused

    lax.fori_loop(0, owners, cand_body, 0)

    def lanes(c, size=LANES):
        return pl.ds(pl.multiple_of(c * size, size), size)

    def fetch(buf, j, i):
        base = ((lax.div(j, picks) * (events // 128) + i) * picks + lax.rem(j, picks)) * 128
        gather(buf, lambda k: ids_ref[base + k], i * 128)

    def slot_chunk(buf, j, c):
        cs = lanes(c)
        x = gathered(buf, c * LANES, LANES)
        delta = time_all[cs, :] - nn(x, pick_last[...])
        x = jnp.concatenate([x, cos_rows(delta, high_row, low_row).astype(bf16)], 1)
        x_all[j, cs, :] = x
        kv = nt(wkv_ref[...], x).astype(bf16)
        if keep_kv:
            kv_all[j, :, cs] = kv
        s0, s1 = heads.sums(kv[:rows].astype(f32) * queries[:, cs].astype(f32))
        live = valid_ref[lax.div(j, picks), pl.ds(lax.rem(j, picks), 1), cs] > 0
        score[j, 0:1, cs] = jnp.where(live, s0 * scale, mask_fill)
        score[j, 1:2, cs] = jnp.where(live, s1 * scale, mask_fill)

    def first_slot(i, unused):
        fetch(xs, 0, i)
        return unused

    lax.fori_loop(0, events // 128, first_slot, 0)

    def slot_pair(i, unused):
        for side, (now, later) in enumerate(((xs, xs2), (xs2, xs))):
            j = 2 * i + side
            ahead = jnp.minimum(j + 1, slots - 1)
            for c in range(chunks):
                for block in range(LANES // 128):
                    fetch(later, ahead, c * (LANES // 128) + block)
                slot_chunk(now, j, c)
        return unused

    lax.fori_loop(0, slots // 2, slot_pair, 0)

    def soft_body(c, unused):
        cs = lanes(c, 128)
        s = score[:, 0:2, cs]
        top = jnp.max(s, 0, keepdims=True)
        p = jnp.where(s > 0.5 * mask_fill, jnp.exp(s - top), 0.0)
        score[:, 0:2, cs] = p / jnp.sum(p, 0, keepdims=True)
        return unused

    lax.fori_loop(0, events // 128, soft_body, 0)

    def kv_of(j, cs, part):
        if keep_kv:
            return kv_all[j, part, cs]
        return nt(wkv_ref[part, :], x_all[j, cs, :]).astype(bf16)

    def att_body(c, unused):
        cs = lanes(c, 128)
        total = jnp.zeros((rows, 128), f32)
        for j in range(slots):
            v = kv_of(j, cs, slice(rows, 2 * rows)).astype(f32)
            total = total + heads.scale(v, score[j, 0:1, cs], score[j, 1:2, cs])
        attended[:, cs] = total
        att_low[:, cs] = total.astype(bf16)
        return unused

    lax.fori_loop(0, events // 128, att_body, 0)

    def out_body(c, unused):
        cs = lanes(c)
        stage[0:width, :] = nn(w("s1t"), att_low[:, cs])[0:width]
        stage[width : 2 * width, :] = fresh_low[:, cs].astype(f32)[0:width]
        x = stage[0 : 2 * rows, :].astype(bf16)
        x_out[:, cs] = x
        pre = nn(wout_ref[...], x)
        pre_out[:, cs] = pre
        hid = (pre * jax.nn.sigmoid(pre)).astype(bf16)
        hid_out[:, cs] = hid
        e = nn(w("s2t"), hid).astype(bf16)
        emb[:, cs] = e
        emb_rows[cs, :] = nt(eye_ref[...], e).astype(bf16)
        return unused

    lax.fori_loop(0, chunks, out_body, 0, unroll=2)

    def row_init(c, unused):
        cs = lanes(c)
        rows_ref[0:1, cs] = jnp.full((1, LANES), mask_fill, f32)
        rows_ref[1:3, cs] = jnp.zeros((2, LANES), f32)
        acc_a[:, cs] = jnp.zeros((rows, LANES), f32)
        return unused

    lax.fori_loop(0, chunks, row_init, 0)

    def dest_of(o):
        at = pl.multiple_of(o * cand_width, cand_width)
        return dest_rows[pl.ds(at, cand_width), :]

    def lse_block(i, unused):
        for side in range(2):
            o = 2 * i + side
            dest = nn(dest_of(o), wd_ref[...]).astype(bf16)
            for c in range(chunks):
                cs = lanes(c)
                logits = nn(dest, emb[:, cs])
                old = rows_ref[0:1, cs]
                top = jnp.maximum(old, jnp.max(logits, 0, keepdims=True))
                rows_ref[0:1, cs] = top
                rows_ref[1:2, cs] = rows_ref[1:2, cs] * jnp.exp(old - top) + jnp.sum(
                    jnp.exp(logits - top), 0, keepdims=True
                )
                hit = lax.broadcasted_iota(jnp.int32, logits.shape, 0) == target_ref[:, cs] - o * cand_width
                rows_ref[2:3, cs] = rows_ref[2:3, cs] + jnp.sum(jnp.where(hit, logits, 0.0), 0, keepdims=True)
        return unused

    lax.fori_loop(0, owners // 2, lse_block, 0)

    mask_row = mask_ref[...].astype(f32)
    log_sum = rows_ref[0:1, :] + jnp.log(rows_ref[1:2, :])
    rows_ref[3:4, :] = log_sum
    rows_ref[4:5, :] = mask_row / jnp.broadcast_to(pos_ref[0:1, 0:1], mask_row.shape)
    loss = jnp.sum(mask_row * (log_sum - rows_ref[2:3, :]), 1, keepdims=True)
    grad_ref[layout.loss : layout.loss + 8, :] = jnp.broadcast_to(loss, (8, 128))

    def back_block(o, grad_dest_w):
        block = dest_of(o)
        dest = nn(block, wd_ref[...]).astype(bf16)
        dest_t = nt(wdt_ref[...], block).astype(bf16)
        block_t = nt(eye_ref[...], block).astype(bf16)

        def chunk(c, unused):
            cs = lanes(c)
            logits = nn(dest, emb[:, cs])
            coeff = rows_ref[4:5, cs]
            hit = lax.broadcasted_iota(jnp.int32, logits.shape, 0) == target_ref[:, cs] - o * cand_width
            grad = jnp.exp(logits - rows_ref[3:4, cs]) - jnp.where(hit, 1.0, 0.0)
            grad = (grad * coeff).astype(bf16)
            slab[0:cand_width, cs] = grad
            return unused

        lax.fori_loop(0, chunks, chunk, 0, unroll=True)
        acc_a[...] += nn(dest_t, slab[0:cand_width, :])
        grad_dest = nn(slab[0:cand_width, :], emb_rows[...]).astype(bf16)
        return grad_dest_w + nn(block_t, grad_dest)[:rows]

    grad_dest_w = lax.fori_loop(0, owners, back_block, jnp.zeros((rows, rows), f32))
    layout.put(grad_ref, "square3", grad_dest_w)

    r0, r1, r2 = slice(0, rows), slice(rows, 2 * rows), slice(2 * rows, 3 * rows)

    def out_back(c, unused):
        cs = lanes(c)
        ge = acc_a[:, cs].astype(bf16)
        slab[r0, cs] = ge
        pre = pre_out[:, cs]
        sig = jax.nn.sigmoid(pre)
        gp = (nn(w("s2"), ge) * (sig * (1.0 + pre * (1.0 - sig)))).astype(bf16)
        slab[r1, cs] = gp
        gm = nn(w("oa"), gp).astype(bf16)
        slab[r2, cs] = gm
        acc_a[:, cs] = nn(w("ob"), gp)
        ga = nn(w("s1"), gm).astype(bf16)
        grad_att[:, cs] = ga
        d0, d1 = heads.sums(ga.astype(f32) * attended[:, cs])
        rows_ref[5:6, cs] = d0
        rows_ref[6:7, cs] = d1
        return unused

    lax.fori_loop(0, chunks, out_back, 0, unroll=2)
    layout.put(grad_ref, "square2", nt(hid_out[...], slab[r0, :]))
    layout.put(grad_ref, "out", nt(slab[r1, :], x_out[...]))
    layout.put(grad_ref, "square1", nt(att_low[...], slab[r2, :]))

    attended[...] = jnp.zeros_like(attended)
    gkv_m[...] = jnp.zeros_like(gkv_m)

    def slot_back(i, unused):
        for side in range(2):
            j = 2 * i + side
            for c in range(events // 256):
                cs = lanes(c, 256)
                kv = kv_of(j, cs, slice(0, 2 * rows)).astype(f32)
                ga = grad_att[:, cs].astype(f32)
                p0, p1 = score[j, 0:1, cs], score[j, 1:2, cs]
                g0, g1 = heads.sums(ga * kv[rows:])
                g0 = p0 * (g0 - rows_ref[5:6, cs]) * scale
                g1 = p1 * (g1 - rows_ref[6:7, cs]) * scale
                attended[:, cs] += heads.scale(kv[:rows], g0, g1)
                gslab[side, 0:rows, cs] = heads.scale(queries[:, cs].astype(f32), g0, g1).astype(bf16)
                gslab[side, rows:2*rows, cs] = heads.scale(ga, p0, p1).astype(bf16)
            both = gslab[side, 0 : 2 * rows, :]
            gkv_m[...] += nn(both, x_all[j])
        return unused

    lax.fori_loop(0, slots // 2, slot_back, 0)
    gkv = gkv_m[...].T
    both = [jnp.concatenate([g[:, :width], g[:, rows : rows + width]], 1)
            for g in (gkv[:width], gkv[256 : 256 + time_width])]
    layout.put(grad_ref, "kv", jnp.concatenate(both, 0))

    for copy in loads:
        copy.wait()
    def gru_back(c, unused):
        cs = lanes(c)
        gq = attended[:, cs].astype(bf16)
        slab[r0, cs] = gq
        gf = acc_a[:, cs] + nn(w("s0"), gq)
        u, cand, r = update[:, cs], cand_act[:, cs], reset_gate[:, cs]
        act = gf * (1.0 - u) * (1.0 - cand * cand)
        gr = (act * gate_n[:, cs] * r * (1.0 - r)).astype(bf16)
        gu = (gf * (mem_src[:, cs] - cand) * u * (1.0 - u)).astype(bf16)
        gn = act.astype(bf16)
        gh = (act * r).astype(bf16)
        slab[r1, cs] = gr
        slab[r2, cs] = gu
        x_out[0:rows, cs] = gn
        hid_out[:, cs] = gh
        pre = pre_msg[:, cs]
        sig = jax.nn.sigmoid(pre)
        back = nn(w("g0r_back"), gr) + nn(w("g0z_back"), gu) + nn(w("g0n_back"), gn)
        att_low[:, cs] = (back * (sig * (1.0 + pre * (1.0 - sig)))).astype(bf16)
        return unused

    lax.fori_loop(0, chunks, gru_back, 0, unroll=2)
    layout.put(grad_ref, "square0", nt(fresh_low[...], slab[r0, :]))
    for index, (left, last) in enumerate(((hidden, x_out[0:rows, :]), (mem_low, hid_out[...]))):
        left = left[...]
        parts = [nt(left, slab[r1, :]), nt(left, slab[r2, :]), nt(left, last)]
        layout.put(grad_ref, f"gru{index}", jnp.concatenate([p[:, :width] for p in parts], 1))
    layout.put(grad_ref, "msg", nt(att_low[...], x_msg[...]))


def main(layout, keep_kv, width, head_dim, cand_width, args):
    events = args[4].shape[1]
    slots = args[7].shape[0] * args[7].shape[1]
    late = args[16:]
    rows = pad_to(width, 16)
    cands = args[1].shape[0]
    smem = pl.BlockSpec(memory_space=pltpu.SMEM)
    vmem = pl.BlockSpec(memory_space=pltpu.VMEM)
    hbm = pl.BlockSpec(memory_space=pl.ANY)
    low = lambda *shape: pltpu.VMEM(shape, bf16)
    full = lambda *shape: pltpu.VMEM(shape, f32)
    return pl.pallas_call(
        partial(main_kernel, (width, head_dim, keep_kv, cand_width, layout)),
        out_shape=jax.ShapeDtypeStruct((layout.total, 128), f32),
        in_specs=[smem, smem] + [vmem] * 14 + [hbm] * len(late),
        out_specs=vmem,
        scratch_shapes=[pltpu.VMEM(x.shape, x.dtype) for x in late]
        + [
            full(2 * events, 128),
            full(2 * events, 128),
            low(slots, events, 384),
            full(events, 128),
            low(slots if keep_kv else 1, 2 * rows if keep_kv else 16, events),
            full(slots, 8, events),
            low(cands, 256),
            low(max(3 * rows, cand_width), events),
            low(256, 256),
            low(2, max(2 * rows, cand_width), events),
            full(2 * rows, LANES),
            low(rows, events),
            low(2 * rows, events),
            low(rows, events),
            low(rows, events),
            low(events, rows),
            full(rows, events),
            full(rows, events),
            full(rows, events),
            low(rows, events),
            full(2 * rows, 384),
            low(256, 128),
            full(8, events),
            pltpu.SemaphoreType.DMA((len(late),)),
        ],
        compiler_params=pltpu.CompilerParams(vmem_limit_bytes=63 * 2**20),
        name="train",
    )(*args)


def reduce_kernel(own, batch, streams, grad_ref, out_ref, acc, recv, local_sem, send_sem, recv_sem):
    place = {"own": lax.axis_index("own"), "batch": lax.axis_index("batch")}

    digits = [lax.div(place["own"], 1 << b) % 2 for b in range(own.bit_length() - 1)]

    def parts(bits):
        if not bits:
            return batch, place["batch"]
        return 1 << len(bits), sum(digits[b] * (1 << i) for i, b in enumerate(bits))

    def peers(bits):
        if not bits:
            for d in range(1, batch):
                there = lax.rem(place["batch"] + d, batch)
                yield (there, place["own"]), there
            return
        for pattern in range(1, 1 << len(bits)):
            there, at = place["own"], 0
            for i, b in enumerate(bits):
                digit = digits[b]
                if pattern >> i & 1:
                    there, digit = there + (1 << b) * (1 - 2 * digit), 1 - digit
                at = at + digit * (1 << i)
            yield (place["batch"], there), at

    load = pltpu.make_async_copy(grad_ref, acc, local_sem)
    load.start()
    barrier = pltpu.get_barrier_semaphore()
    devices = {}
    for order in [order for start, size, order in streams]:
        for bits in order:
            devices.setdefault(tuple(sorted(bits)), [device for device, there in peers(sorted(bits))])
    greeted = [device for bits in devices if all(set(bits) >= set(other) or not set(bits) & set(other) for other in devices)
               for device in devices[bits]]
    for device in greeted:
        pl.semaphore_signal(barrier, inc=1, device_id=device, device_id_type=MESH)
    pl.semaphore_wait(barrier, len(greeted))
    load.wait()

    sent = []
    longest = max(len(order) for start, size, order in streams)

    class Stream:
        def __init__(self, index, start, size, order):
            self.index, self.base, self.size, self.inner, self.order = index, start, size, start, order
            self.copies = []
            self.slots = [0]
            for bits in order:
                self.slots.append(self.slots[-1] + parts(bits)[0] - 1)

        def copy(self, source, target, peer, slot):
            copy = pltpu.make_async_remote_copy(
                src_ref=source, dst_ref=target,
                send_sem=send_sem.at[self.index, slot], recv_sem=recv_sem.at[self.index, slot],
                device_id=peer, device_id_type=MESH,
            )
            copy.start()
            self.copies.append(copy)
            sent.append(copy)

        def scatter(self, step):
            count, mine = parts(self.order[step])
            piece = self.size // count
            for d, (peer, theirs) in enumerate(peers(self.order[step]), 1):
                away = pl.multiple_of(self.base + theirs * piece, 8)
                self.copy(
                    acc.at[pl.ds(away, piece), :], recv.at[pl.ds(self.inner + (d - 1) * piece, piece), :],
                    peer, self.slots[step] + d - 1,
                )
            self.base = pl.multiple_of(self.base + mine * piece, 8)
            self.size = piece

        def add(self, step):
            target = out_ref if step == len(self.order) - 1 else acc
            part = pl.ds(self.base, self.size)
            total = acc[part, :]
            for copy in self.copies:
                copy.wait_recv()
                total = total + recv[pl.ds(self.inner, self.size), :]
                self.inner += self.size
            target[part, :] = total
            self.copies = []

        def gather(self, step):
            count, mine = parts(self.order[step])
            part = pl.ds(self.base, self.size)
            for d, (peer, theirs) in enumerate(peers(self.order[step]), 1):
                self.copy(out_ref.at[part, :], out_ref.at[part, :], peer, self.slots[-1] + self.slots[step] + d - 1)
            self.base = pl.multiple_of(self.base - mine * self.size, 8)
            self.size *= count

        def gathered(self):
            for copy in self.copies:
                copy.wait_recv()
            self.copies = []

    flows = [Stream(index, *stream) for index, stream in enumerate(streams)]
    for step in range(2 * longest + 1):
        for flow in flows:
            rounds = len(flow.order)
            if 0 < step <= rounds:
                flow.add(step - 1)
            elif rounds < step <= 2 * rounds:
                flow.gathered()
            if step < rounds:
                flow.scatter(step)
            elif step < 2 * rounds:
                flow.gather(2 * rounds - 1 - step)
    for copy in sent:
        copy.wait_send()


def reduce_all(own, batch, packed):
    total = packed.shape[0]
    own_bits = own.bit_length() - 1
    fold = 8 * own * batch
    core, xs, ys, zs = (0,), tuple(range(1, (own_bits + 1) // 2)), tuple(range((own_bits + 1) // 2, own_bits)), ()
    plan = ((6, (core, xs + ys, zs)), (3, (core, zs, xs + ys)), (6, (core, ys + xs, zs)), (3, (core, zs, ys + xs)))
    streams = []
    start = 0
    blocks = total // fold
    shares = sum(share for share, order in plan)
    for index, (share, order) in enumerate(plan):
        size = total - start if index == len(plan) - 1 else blocks * share // shares * fold
        if size:
            streams.append((start, size, order))
        start += size
    count = 2 * (own * batch)
    return pl.pallas_call(
        partial(reduce_kernel, own, batch, streams),
        out_shape=jax.ShapeDtypeStruct(packed.shape, f32),
        in_specs=[pl.BlockSpec(memory_space=pl.ANY)],
        out_specs=pl.BlockSpec(memory_space=pltpu.VMEM),
        scratch_shapes=[
            pltpu.VMEM(packed.shape, f32),
            pltpu.VMEM(packed.shape, f32),
            pltpu.SemaphoreType.DMA,
            pltpu.SemaphoreType.DMA((len(streams), count)),
            pltpu.SemaphoreType.DMA((len(streams), count)),
        ],
        compiler_params=pltpu.CompilerParams(
            collective_id=2, has_side_effects=True, vmem_limit_bytes=63 * 2**20
        ),
        name="reduce",
    )(packed)


def update_kernel(layout, step_rate, grad_ref, pos_ref, *refs):
    sources, targets, loss_ref, count_ref = refs[:15], refs[15:30], refs[30], refs[31]
    held, laid = refs[32:47], refs[47:49]
    in_sem, out_sem = refs[49:]
    loss_ref[...] = grad_ref[layout.loss : layout.loss + 1, 0:1]
    count_ref[...] = pos_ref[0:1, 0:1]
    arrive = [pltpu.make_async_copy(sources[i], held[i], in_sem.at[i]) for i in range(15)]
    leave = [pltpu.make_async_copy(held[i], targets[(i + 5) % 10 if i < 10 else i], out_sem.at[i]) for i in range(15)]
    order = (1, 2, 0, 3, 4)
    for index in order:
        for kind in range(3):
            arrive[5 * kind + index].start()

    for ref, name, parts in ((laid[0], "gru", 2), (laid[1], "square", 4)):
        for part in range(parts):
            for columns, gradient in layout.tiles(grad_ref, f"{name}{part}"):
                ref[:, part, columns] = gradient

    def step(index, at, gradient):
        weights, moments, averages = (held[5 * kind + index] for kind in range(3))
        moment = mu_coef * moments[at] + gradient
        weight = weights[at] - step_rate * (gradient + mu_coef * moment)
        moments[at] = moment
        weights[at] = weight
        averages[at] = (1.0 - avg_coef) * averages[at] + avg_coef * weight

    for index in order:
        for kind in range(3):
            arrive[5 * kind + index].wait()
        if index in (1, 2):
            step(index, slice(None), laid[index - 1][...])
        else:
            for columns, gradient in layout.tiles(grad_ref, ("msg", "", "", "kv", "out")[index]):
                step(index, (slice(None), columns), gradient)
        for kind in range(3):
            leave[5 * kind + index].start()
    for copy in leave:
        copy.wait()


def update_all(layout, step_rate, packed, positives, params):
    vmem = pl.BlockSpec(memory_space=pltpu.VMEM)
    hbm = pl.BlockSpec(memory_space=pl.ANY)
    buffers = [pltpu.VMEM(p.shape, f32) for p in params]
    return pl.pallas_call(
        partial(update_kernel, layout, step_rate),
        out_shape=tuple(jax.ShapeDtypeStruct(p.shape, f32) for p in params[5:10] + params[:5] + params[10:])
        + (jax.ShapeDtypeStruct((1, 1), f32),) * 2,
        in_specs=[vmem] * 2 + [hbm] * 15,
        out_specs=(hbm,) * 15 + (vmem,) * 2,
        scratch_shapes=buffers + buffers[1:3] + [pltpu.SemaphoreType.DMA((15,))] * 2,
        compiler_params=pltpu.CompilerParams(vmem_limit_bytes=63 * 2**20),
        name="update",
    )(packed, positives, *params)


def turned(arrays):
    msg, gru, square, kv, out = arrays
    return (msg.T, gru.transpose(1, 0, 2), square.transpose(1, 0, 2), kv, out.T)


def local(
    memory, last_update, src_local, edge_feat, event_time, nbr_owner, nbr_ids, nbr_mask, event_mask,
    dest_local, target, w_msg, w_gru, w_square, w_key_value, w_output,
    mom_msg, mom_gru, mom_square, mom_key_value, mom_output,
    avg_msg, avg_gru, avg_square, avg_key_value, avg_output,
):
    own = lax.axis_size("own")
    batch = lax.axis_size("batch")
    events, edge = edge_feat.shape
    nodes, width = memory.shape
    head_dim = width // HEADS
    time_width = w_key_value.shape[0] - width
    columns = time_columns(time_width, 128)
    layout = Layout(
        width, w_msg.shape[0], w_output.shape[0], w_gru.shape[2], *w_key_value.shape, 8 * own * batch
    )
    weights = turned((w_msg, w_gru, w_square, w_key_value, w_output))
    time_row, mask_row, src_row, target_row = (x[None, :] for x in (event_time, event_mask, src_local, target))
    table, cand_ids, flat_ids, positives, newest, *handed = exchange(
        own, batch,
        (memory.T, last_update[None, :], dest_local[None, :], time_row, mask_row, src_row,
         nbr_owner.T, nbr_ids.transpose(2, 1, 0), jnp.asarray(columns)) + weights + (edge_feat.T,),
    )
    packed = main(
        layout, own * nodes <= 16384, width, head_dim, dest_local.shape[0],
        (flat_ids.reshape(-1), cand_ids.reshape(-1), positives, table, time_row, mask_row, target_row,
         nbr_mask.transpose(2, 1, 0), *handed[:5], jnp.asarray(columns.T[:8]), *handed[5:]),
    )
    summed = reduce_all(own, batch, packed)
    step_rate = rate_coef * math.sqrt(events * own * batch)
    *states, loss, count = update_all(
        layout, step_rate, summed, positives,
        weights
        + turned((mom_msg, mom_gru, mom_square, mom_key_value, mom_output))
        + turned((avg_msg, avg_gru, avg_square, avg_key_value, avg_output)),
    )
    states = [x for i in range(3) for x in turned(states[5 * i : 5 * i + 5])]
    return (loss.reshape(()), count.reshape(()), newest.reshape(-1), *states)


def solution(mesh):
    row = P(("batch", "own"))
    placed = (
        (P("own", None), P("own"), row, P(("batch", "own"), None), row, P(("batch", "own"), None))
        + (P(("batch", "own"), None, None),) * 2
        + (row,) * 3
        + (P(),) * 15
    )
    return jax.shard_map(
        local,
        mesh=mesh,
        in_specs=placed,
        out_specs=(P(), P(), P("own")) + (P(),) * 15,
        check_vma=False,
    )
```

```python
from functools import partial
import math

import jax
import jax.numpy as jnp
import numpy as np
from jax import lax
from jax.experimental import pallas as pl
from jax.experimental.pallas import tpu as pltpu
from jax.sharding import PartitionSpec as P

HEADS = 2
LANES = 256
MESH = pl.DeviceIdType.MESH
f32 = jnp.float32
bf16 = jnp.bfloat16

mu_coef = 0.9
avg_coef = 0.1
rate_coef = 0.008
mask_fill = -1e30

COS_TERMS = (
    1.0,
    -19.73920440673828,
    64.93911743164062,
    -85.45011901855469,
    60.16745376586914,
    -25.966907501220703,
    6.527653217315674,
)


def pad_to(size, step):
    return -(-size // step) * step


def nn(a, b):
    return lax.dot_general(a, b, (((1,), (0,)), ((), ())), preferred_element_type=f32)


def nt(a, b):
    return lax.dot_general(a, b, (((1,), (1,)), ((), ())), preferred_element_type=f32)


def flip_bit(index, bit):
    size = 1 << bit
    return index + size * (1 - 2 * (lax.div(index, size) % 2))


def time_columns(time_width, rows):
    turns = 10.0 ** (-np.linspace(0.0, 9.0, time_width)) / (2.0 * np.pi)
    mant, expo = np.frexp(turns)
    high = np.ldexp(np.round(mant * 4096.0) / 4096.0, expo)
    out = np.zeros((rows, 128), np.float32)
    out[:time_width, 0] = high
    out[:time_width, 1] = turns - high
    return out


def cos_rows(delta, high, low):
    turns = delta * high
    rest = turns - jnp.floor(turns + 0.5) + delta * low
    square = rest * rest
    value = square * COS_TERMS[-1] + COS_TERMS[-2]
    for term in COS_TERMS[-3::-1]:
        value = value * square + term
    return value


class Heads:
    def __init__(self, head_dim, rows):
        self.low = head_dim // 8 * 8
        self.high = pad_to(head_dim, 8)
        self.cut = head_dim - self.low
        self.rows = rows

    def split(self, lanes):
        return lax.broadcasted_iota(jnp.int32, (8, lanes), 0) < self.cut

    def sums(self, x):
        lanes = x.shape[1]
        mid = x[self.low : self.high]
        first = self.split(lanes)
        a = jnp.sum(x[: self.low].reshape(self.low // 8, 8, lanes), 0)
        b = jnp.sum(x[self.high :].reshape((self.rows - self.high) // 8, 8, lanes), 0)
        a = a + jnp.where(first, mid, 0.0)
        b = b + jnp.where(first, 0.0, mid)
        return jnp.sum(a, 0, keepdims=True), jnp.sum(b, 0, keepdims=True)

    def scale(self, x, p0, p1):
        lanes = x.shape[1]
        mid = jnp.where(self.split(lanes), p0, p1)
        return jnp.concatenate(
            [x[: self.low] * p0, x[self.low : self.high] * mid, x[self.high :] * p1], 0
        )


GATES = ("g0r", "g0z", "g0n", "g1r", "g1z", "g1n", "s0t")
SQUARES = ("s1t", "s2t", "g0r_back", "g0z_back", "g0n_back", "s0", "s1", "s2", "oa", "ob")
LOW_STATE = ("queries", "fresh_low", "x_msg", "mem_low", "hidden")
STATE = ("mem_src", "pre_msg", "reset_gate", "update", "cand_act", "gate_n")


def exchange_kernel(
    own, batch,
    mem_ref, last_ref, cand_ref, time_ref, mask_ref, src_ref, owner_ref, nbr_ref, freq_ref,
    msg_hbm, gru_hbm, square_hbm, kv_hbm, outw_hbm, edge_hbm,
    table_ref, ids_ref, flat_ref, pos_ref, newest_ref, *rest,
):
    handed = rest[: 5 + len(LOW_STATE) + len(STATE)]
    rest = rest[len(handed) :]
    staged = rest[: len(handed)]
    wsq_ref, wout_ref, wkv_ref, wd_ref, wdt_ref = staged[:5]
    state = dict(zip(LOW_STATE + STATE, staged[5:]))
    (msg_ref, gru_ref, square_ref, kv_ref, outw_ref, edge_ref, gates_ref, wmsg_ref, mem3_ref, stage,
     shard, ext, pairs, square_pad, wide_pad, kv_pad, batch_buf, own_buf,
     local_sem, load_sem, hand_sem,
     table_send, table_recv, batch_send, batch_recv, own_send, own_recv) = rest[len(handed) :]
    loads = [
        pltpu.make_async_copy(source, target, load_sem.at[i])
        for i, (source, target) in enumerate((
            (gru_hbm, gru_ref), (square_hbm, square_ref), (outw_hbm, outw_ref),
            (msg_hbm, msg_ref), (kv_hbm, kv_ref), (edge_hbm, edge_ref),
        ))
    ]
    for copy in loads:
        copy.start()
    hands = [pltpu.make_async_copy(staged[i], handed[i], hand_sem.at[i]) for i in range(len(handed))]
    me = lax.axis_index("own")
    group = lax.axis_index("batch")
    barrier = pltpu.get_barrier_semaphore()
    for step in range(1, own):
        pl.semaphore_signal(barrier, inc=1, device_id=(group, lax.rem(me + step, own)), device_id_type=MESH)
    for step in range(1, batch):
        pl.semaphore_signal(barrier, inc=1, device_id=(lax.rem(group + step, batch), me), device_id_type=MESH)

    width, nodes = mem_ref.shape
    rows = pad_to(width, 16)
    ext[...] = jnp.zeros_like(ext)
    ext[0:width, :] = mem_ref[...]
    last = last_ref[...]
    ext[width : width + 1, :] = lax.div(last, 8).astype(f32)
    ext[width + 1 : width + 2, :] = lax.rem(last, 8).astype(f32)

    def turn(i, unused):
        block = ext[:, pl.ds(pl.multiple_of(i * 128, 128), 128)].T
        base = pl.multiple_of(i * 256, 256)
        pairs[pl.ds(base, 128, stride=2), :] = block[:, :128]
        pairs[pl.ds(base + 1, 128, stride=2), :] = block[:, 128:]
        return unused

    lax.fori_loop(0, nodes // 128, turn, 0)

    def pack(i, unused):
        got = [pairs[pl.ds(pl.multiple_of(i * 128, 128) + 2 * k, 2), :] for k in range(64)]
        for k in range(64):
            shard[i * 64 + k] = got[k].astype(bf16)
        return unused

    lax.fori_loop(0, nodes // 64, pack, 0)
    pl.semaphore_wait(barrier, own + batch - 2)

    half = nodes // 2
    bits = own.bit_length() - 1
    others = list(range(1, bits))
    cut = len(others) // 2
    orders = (others + [0], others[cut:] + others[:cut] + [0])

    def shard_copy(stream, pattern, bit):
        peer = flip_bit(me, bit)
        source = me
        for b in range(bits):
            if pattern >> b & 1:
                source = flip_bit(source, b)
        part = pl.ds(pl.multiple_of(source * nodes + stream * half, half), half)
        slot = pattern | 1 << bit
        src = shard.at[pl.ds(stream * half, half)] if pattern == 0 else table_ref.at[part]
        return pltpu.make_async_remote_copy(
            src_ref=src, dst_ref=table_ref.at[part],
            send_sem=table_send.at[stream, slot], recv_sem=table_recv.at[stream, slot],
            device_id=(group, peer), device_id_type=MESH,
        )

    copies = [{}, {}]
    for step in range(bits):
        for stream in range(2):
            bit = orders[stream][step]
            copy = shard_copy(stream, 0, bit)
            copy.start()
            copies[stream][1 << bit] = copy
    mine = pltpu.make_async_copy(
        shard, table_ref.at[pl.ds(pl.multiple_of(me * nodes, nodes), nodes)], local_sem
    )
    mine.start()

    events = src_ref.shape[1]
    time_row = time_ref[...].astype(f32)
    src_row = src_ref[...]
    best = []
    tile = 256
    for start in range(0, nodes, tile):
        node = lax.broadcasted_iota(jnp.int32, (tile, 128), 0) + start
        top = jnp.full((tile, 128), -1.0, f32)
        for lane in range(0, events, 128):
            hit = src_row[:, lane : lane + 128] == node
            top = jnp.maximum(top, jnp.where(hit, time_row[:, lane : lane + 128], -1.0))
        best.append(jnp.max(top.T, 0, keepdims=True))
    newest = jnp.concatenate(best, 1).astype(jnp.int32)
    newest = jnp.maximum(newest, last)
    count = jnp.sum(mask_ref[...].astype(f32), 1, keepdims=True).astype(jnp.int32)
    batch_buf[0, 0:1, :] = newest
    batch_buf[0, 1:2, :] = jnp.broadcast_to(count, (1, nodes))

    def peer_copy(step):
        return pltpu.make_async_remote_copy(
            src_ref=batch_buf.at[0], dst_ref=batch_buf.at[step],
            send_sem=batch_send.at[step], recv_sem=batch_recv.at[step],
            device_id=(lax.rem(group + step, batch), me), device_id_type=MESH,
        )

    peers = [peer_copy(step) for step in range(1, batch)]
    for copy in peers:
        copy.start()

    picks = owner_ref.shape[0]
    per_pick = nbr_ref.shape[0]
    for s in range(per_pick):
        flat = owner_ref[...] * nodes + nbr_ref[s]
        for block in range(events // 128):
            at = (s * (events // 128) + block) * picks
            flat_ref[at : at + picks, :] = flat[:, block * 128 : block * 128 + 128]
    whole = ext[0:rows, :]
    part0 = whole.astype(bf16)
    whole = whole - part0.astype(f32)
    part1 = whole.astype(bf16)
    mem3_ref[0:rows, :] = part0
    mem3_ref[rows : 2 * rows, :] = part1
    mem3_ref[2 * rows :, :] = (whole - part1.astype(f32)).astype(bf16)

    square_pad[...] = jnp.zeros_like(square_pad)
    for copy in loads:
        copy.wait()

    def put(name, value):
        square_pad[0:width, 0:width] = value
        if name in GATES:
            gates_ref[GATES.index(name)] = square_pad[...].astype(bf16)
        else:
            wsq_ref[SQUARES.index(name)] = square_pad[...].astype(bf16)

    for index in range(2):
        for gate, letter in enumerate("rzn"):
            value = gru_ref[:, index, gate * width : gate * width + width]
            put(f"g{index}{letter}", value.T)
            if index == 0:
                put(f"g0{letter}_back", value)
    for index in range(3):
        value = square_ref[:, index, :]
        put(f"s{index}", value)
        put(f"s{index}t", value.T)
    put("oa", outw_ref[:, 0:width].T)
    put("ob", outw_ref[:, width : 2 * width].T)
    wide_pad[...] = jnp.zeros_like(wide_pad)
    wide_pad[0:width, 0 : 2 * width] = outw_ref[...]
    wout_ref[...] = wide_pad[:, 0 : wout_ref.shape[1]].astype(bf16)
    wide_pad[0:width, 0 : msg_ref.shape[1]] = msg_ref[...]
    wmsg_ref[...] = wide_pad[...].astype(bf16)
    last_square = square_ref[:, 3, :]
    kv_pad[...] = jnp.zeros_like(kv_pad)
    kv_pad[0:width, 0:width] = last_square
    wd_ref[...] = kv_pad[0 : wd_ref.shape[0], 0 : wd_ref.shape[1]].astype(bf16)
    kv_pad[0:width, 0:width] = last_square.T
    wdt_ref[...] = kv_pad[0 : wdt_ref.shape[0], 0 : wdt_ref.shape[1]].astype(bf16)
    time_width = kv_ref.shape[0] - width
    kv_pad[...] = jnp.zeros_like(kv_pad)
    for index in range(2):
        part = kv_ref[:, index * width : index * width + width]
        kv_pad[index * rows : index * rows + width, 0:width] = part[0:width].T
        kv_pad[index * rows : index * rows + width, 256 : 256 + time_width] = part[width:].T
    wkv_ref[...] = kv_pad[...].astype(bf16)
    for copy in hands[:5]:
        copy.start()

    def forward(step):
        for stream in range(2):
            order = orders[stream]
            held = [0]
            for bit in order[:step]:
                held = held + [p | 1 << bit for p in held]
            for pattern in held:
                slot = pattern | 1 << order[step]
                copies[stream][slot].wait_recv()
                for bit in order[step + 1 :]:
                    copy = shard_copy(stream, slot, bit)
                    copy.start()
                    copies[stream][slot | 1 << bit] = copy

    forward(0)
    total = count
    for step, copy in enumerate(peers, 1):
        copy.wait_recv()
        newest = jnp.maximum(newest, batch_buf[step, 0:1, :])
        total = total + batch_buf[step, 1:2, 0:1]
    newest_ref[...] = newest

    cands = cand_ref.shape[1]
    own_buf[0, 0:1, :] = cand_ref[...] + me * nodes
    own_buf[0, 1:2, :] = jnp.broadcast_to(total, (1, cands))

    def owner_copy(step):
        return pltpu.make_async_remote_copy(
            src_ref=own_buf.at[0], dst_ref=own_buf.at[step],
            send_sem=own_send.at[step], recv_sem=own_recv.at[step],
            device_id=(group, lax.rem(me + step, own)), device_id_type=MESH,
        )

    owners = [owner_copy(step) for step in range(1, own)]
    for copy in owners:
        copy.start()

    edge = edge_ref.shape[0]
    high, low = freq_ref[:, 0:1], freq_ref[:, 1:2]
    stage[...] = jnp.zeros_like(stage)

    def w(name):
        return gates_ref[GATES.index(name)]

    def gru_body(c, unused):
        cs = pl.ds(pl.multiple_of(c * LANES, LANES), LANES)
        node = lax.broadcasted_iota(jnp.int32, (nodes, LANES), 0)
        onehot = (node == src_ref[:, cs]).astype(f32).astype(bf16)
        parts = nn(mem3_ref[...], onehot)
        mem = parts[:rows] + parts[rows : 2 * rows] + parts[2 * rows :]
        state["mem_src"][:, cs] = mem
        delta = time_ref[:, cs].astype(f32) - 8.0 * mem[width : width + 1] - mem[width + 1 : width + 2]
        stage[0:width, :] = mem[0:width]
        stage[width : width + edge, :] = edge_ref[:, cs].astype(f32)
        stage[width + edge : width + edge + time_width, :] = cos_rows(delta, high, low)[0:time_width]
        x = stage[...].astype(bf16)
        state["x_msg"][:, cs] = x
        m_low = mem.astype(bf16)
        state["mem_low"][:, cs] = m_low
        pre = nn(wmsg_ref[...], x)
        state["pre_msg"][:, cs] = pre
        hid = (pre * jax.nn.sigmoid(pre)).astype(bf16)
        state["hidden"][:, cs] = hid
        r = jax.nn.sigmoid(nn(w("g0r"), hid) + nn(w("g1r"), m_low))
        state["reset_gate"][:, cs] = r
        u = jax.nn.sigmoid(nn(w("g0z"), hid) + nn(w("g1z"), m_low))
        state["update"][:, cs] = u
        gn = nn(w("g1n"), m_low)
        state["gate_n"][:, cs] = gn
        cand = jnp.tanh(nn(w("g0n"), hid) + r * gn)
        state["cand_act"][:, cs] = cand
        fresh = ((1.0 - u) * cand + u * mem).astype(bf16)
        state["fresh_low"][:, cs] = fresh
        state["queries"][:, cs] = nn(w("s0t"), fresh).astype(bf16)
        return unused

    lax.fori_loop(0, events // LANES, gru_body, 0)
    for copy in hands[5:]:
        copy.start()
    for step in range(1, bits):
        forward(step)

    for step in range(own):
        if step:
            owners[step - 1].wait_recv()
            total = total + own_buf[step, 1:2, 0:1]
        source = lax.rem(me - step + own, own)
        for block in range(cands // 128):
            ids_ref[pl.ds(source * (cands // 128) + block, 1), :] = own_buf[
                step, 0:1, block * 128 : block * 128 + 128
            ]
    pos_ref[...] = jnp.broadcast_to(jnp.maximum(total.astype(f32), 1.0), pos_ref.shape)
    mine.wait()
    for copy in hands:
        copy.wait()
    for copy in peers + owners:
        copy.wait_send()
    for stream in range(2):
        for slot in copies[stream]:
            copies[stream][slot].wait_send()


def exchange(own, batch, args):
    mem, last, cand, time, mask, src, owner, nbr, freq, msg, gru, square, kv, outw, edge = args
    width, nodes = mem.shape
    events = src.shape[1]
    cands = cand.shape[1]
    rows = pad_to(width, 16)
    wide = pad_to(msg.shape[1], 16)
    vmem = pl.BlockSpec(memory_space=pltpu.VMEM)
    hbm = pl.BlockSpec(memory_space=pl.ANY)
    whole = lambda *shape: jax.ShapeDtypeStruct(shape, jnp.int32)
    handed = [
        ((len(SQUARES), rows, rows), bf16),
        ((rows, 2 * rows), bf16),
        ((2 * rows, 384), bf16),
        ((256, rows), bf16),
        ((rows, 256), bf16),
    ]
    handed += [((wide if name == "x_msg" else rows, events), bf16) for name in LOW_STATE]
    handed += [((rows, events), f32) for name in STATE]
    return pl.pallas_call(
        partial(exchange_kernel, own, batch),
        out_shape=(
            jax.ShapeDtypeStruct((own * nodes, 2, 128), bf16),
            whole(own * cands // 128, 128),
            whole(nbr.shape[0] * nbr.shape[1] * events // 128, 128),
            jax.ShapeDtypeStruct((8, 128), f32),
            whole(1, nodes),
        )
        + tuple(jax.ShapeDtypeStruct(*h) for h in handed),
        in_specs=[vmem] * 9 + [hbm] * 6,
        out_specs=(hbm,) + (vmem,) * 4 + (hbm,) * len(handed),
        scratch_shapes=[pltpu.VMEM(*h) for h in handed]
        + [pltpu.VMEM(x.shape, x.dtype) for x in (msg, gru, square, kv, outw, edge)]
        + [
            pltpu.VMEM((len(GATES), rows, rows), bf16),
            pltpu.VMEM((rows, wide), bf16),
            pltpu.VMEM((3 * rows, nodes), bf16),
            pltpu.VMEM((wide, LANES), f32),
            pltpu.VMEM((nodes, 2, 128), bf16),
            pltpu.VMEM((256, nodes), f32),
            pltpu.VMEM((2 * nodes + 64, 128), f32),
            pltpu.VMEM((rows, rows), f32),
            pltpu.VMEM((rows, wide), f32),
            pltpu.VMEM((2 * rows, 384), f32),
            pltpu.VMEM((batch, 8, nodes), jnp.int32),
            pltpu.VMEM((own, 8, cands), jnp.int32),
            pltpu.SemaphoreType.DMA,
            pltpu.SemaphoreType.DMA((6,)),
            pltpu.SemaphoreType.DMA((len(handed),)),
            pltpu.SemaphoreType.DMA((2, own)),
            pltpu.SemaphoreType.DMA((2, own)),
            pltpu.SemaphoreType.DMA((batch,)),
            pltpu.SemaphoreType.DMA((batch,)),
            pltpu.SemaphoreType.DMA((own,)),
            pltpu.SemaphoreType.DMA((own,)),
        ],
        compiler_params=pltpu.CompilerParams(
            collective_id=1, has_side_effects=True, vmem_limit_bytes=63 * 2**20
        ),
        name="exchange",
    )(*args)


class Layout:
    def __init__(self, width, wide, deep, gates, kv_rows, kv_cols, fold):
        rows = pad_to(width, 8)
        self.width = width
        self.pieces = {}
        row = 0
        for name, depth, columns in (
            ("msg", width, wide),
            ("out", width, deep),
            ("kv", kv_rows, kv_cols),
            ("gru0", width, gates),
            ("gru1", width, gates),
            ("square0", width, width),
            ("square1", width, width),
            ("square2", width, width),
            ("square3", width, width),
        ):
            tiles = []
            for column in range(0, columns, 128):
                size = min(128, columns - column)
                if size < 128 and name[:3] in ("gru", "squ"):
                    tiles.append([column, size, None, None])
                else:
                    tiles.append([column, size, row, 0])
                    row += pad_to(depth, 8)
            self.pieces[name] = (depth, tiles)
        host = self.pieces["msg"][1][-1]
        lane = pad_to(host[1], 8)
        for name in ("gru0", "gru1"):
            tile = self.pieces[name][1][-1]
            if tile[2] is None:
                assert lane + tile[1] <= 128
                tile[2:] = [host[2], lane]
                lane += tile[1]
        for pair in range(2):
            for side in range(2):
                tile = self.pieces[f"square{2 * pair + side}"][1][-1]
                assert tile[1] <= 64
                tile[2:] = [row, 64 * side]
            row += rows
        self.loss = row
        row += 8
        self.total = pad_to(row, fold)

    def put(self, ref, name, value):
        depth, tiles = self.pieces[name]
        for column, size, row, lane in tiles:
            ref[row : row + depth, lane : lane + size] = value[:depth, column : column + size]

    def tiles(self, ref, name):
        depth, tiles = self.pieces[name]
        for column, size, row, lane in tiles:
            yield slice(column, column + size), ref[row : row + depth, lane : lane + size]


def main_kernel(
    dims,
    ids_ref, cand_ref, pos_ref, table_ref, time_ref, mask_ref, target_ref, valid_ref,
    wsq_ref, wout_ref, wkv_ref, wd_ref, wdt_ref, freq_row_ref, queries, fresh_low, *rest,
):
    late = rest[: len(LOW_STATE) + len(STATE) - 2]
    grad_ref, load_sem = rest[len(late)], rest[-1]
    held = rest[len(late) + 1 : 2 * len(late) + 1]
    x_msg, mem_low, hidden, mem_src, pre_msg, reset_gate, update, cand_act, gate_n = held
    (
        xs, xs2, x_all, time_all, kv_all, score, dest_rows, slab, eye_ref, gslab, stage,
        att_low, x_out, hid_out, emb, emb_rows, attended, pre_out,
        acc_a, grad_att, gkv_m, pick_last, rows_ref,
    ) = rest[2 * len(late) + 1 : -1]
    loads = [pltpu.make_async_copy(late[i], held[i], load_sem.at[i]) for i in range(len(late))]
    for copy in loads:
        copy.start()
    width, head_dim, keep_kv, cand_width, layout = dims
    events = time_ref.shape[1]
    per_pick, picks = valid_ref.shape[:2]
    slots = per_pick * picks
    rows = pad_to(width, 16)
    time_width = layout.pieces["kv"][0] - width
    heads = Heads(head_dim, rows)
    scale = head_dim ** (-0.5)
    high_row, low_row = freq_row_ref[0:1, :], freq_row_ref[1:2, :]
    chunks = events // LANES
    owners = cand_ref.shape[0] // cand_width

    def w(name):
        return wsq_ref[SQUARES.index(name)]

    def gather(buf, read_id, at):
        got = [table_ref[read_id(k)] for k in range(128)]
        for k in range(0, 128, 2):
            pair = jnp.concatenate([got[k].astype(f32), got[k + 1].astype(f32)], 0)
            buf[pl.ds(pl.multiple_of(2 * at, 256) + 2 * k, 4), :] = pair

    def gathered(buf, start, count):
        base = pl.multiple_of(2 * start, 2 * count)
        return jnp.concatenate(
            [buf[pl.ds(base, count, stride=2), :], buf[pl.ds(base + 1, count, stride=2), :]], 1
        ).astype(bf16)

    grad_ref[layout.loss :, :] = jnp.zeros_like(grad_ref[layout.loss :, :])
    host = layout.pieces["msg"][1][-1][2]
    grad_ref[host : host + rows, :] = jnp.zeros((rows, 128), f32)
    eye = lax.broadcasted_iota(jnp.int32, (256, 256), 0) == lax.broadcasted_iota(jnp.int32, (256, 256), 1)
    eye_ref[...] = eye.astype(f32).astype(bf16)
    stage[...] = jnp.zeros_like(stage)
    lane = lax.broadcasted_iota(jnp.int32, (256, 128), 0)
    pick_last[...] = jnp.where(lane == width, 8.0, jnp.where(lane == width + 1, 1.0, 0.0)).astype(bf16)
    for start in range(0, events, 128):
        time_all[start : start + 128, :] = jnp.broadcast_to(
            time_ref[:, start : start + 128].astype(f32), (128, 128)
        ).T

    def cand_body(o, unused):
        def fill(i, unused):
            gather(xs, lambda k: cand_ref[o * cand_width + i * 128 + k], i * 128)
            return unused

        lax.fori_loop(0, cand_width // 128, fill, 0)
        at = pl.multiple_of(o * cand_width, cand_width)
        dest_rows[pl.ds(at, cand_width), :] = gathered(xs, 0, cand_width)
        return unused

    lax.fori_loop(0, owners, cand_body, 0)

    def lanes(c, size=LANES):
        return pl.ds(pl.multiple_of(c * size, size), size)

    def fetch(buf, j, i):
        base = ((lax.div(j, picks) * (events // 128) + i) * picks + lax.rem(j, picks)) * 128
        gather(buf, lambda k: ids_ref[base + k], i * 128)

    def slot_chunk(buf, j, c):
        cs = lanes(c)
        x = gathered(buf, c * LANES, LANES)
        delta = time_all[cs, :] - nn(x, pick_last[...])
        x = jnp.concatenate([x, cos_rows(delta, high_row, low_row).astype(bf16)], 1)
        x_all[j, cs, :] = x
        kv = nt(wkv_ref[...], x).astype(bf16)
        if keep_kv:
            kv_all[j, :, cs] = kv
        s0, s1 = heads.sums(kv[:rows].astype(f32) * queries[:, cs].astype(f32))
        live = valid_ref[lax.div(j, picks), pl.ds(lax.rem(j, picks), 1), cs] > 0
        score[j, 0:1, cs] = jnp.where(live, s0 * scale, mask_fill)
        score[j, 1:2, cs] = jnp.where(live, s1 * scale, mask_fill)

    def first_slot(i, unused):
        fetch(xs, 0, i)
        return unused

    lax.fori_loop(0, events // 128, first_slot, 0)

    def slot_pair(i, unused):
        for side, (now, later) in enumerate(((xs, xs2), (xs2, xs))):
            j = 2 * i + side
            ahead = jnp.minimum(j + 1, slots - 1)
            for c in range(chunks):
                for block in range(LANES // 128):
                    fetch(later, ahead, c * (LANES // 128) + block)
                slot_chunk(now, j, c)
        return unused

    lax.fori_loop(0, slots // 2, slot_pair, 0)

    def soft_body(c, unused):
        cs = lanes(c, 128)
        s = score[:, 0:2, cs]
        top = jnp.max(s, 0, keepdims=True)
        p = jnp.where(s > 0.5 * mask_fill, jnp.exp(s - top), 0.0)
        score[:, 0:2, cs] = p / jnp.sum(p, 0, keepdims=True)
        return unused

    lax.fori_loop(0, events // 128, soft_body, 0)

    def kv_of(j, cs, part):
        if keep_kv:
            return kv_all[j, part, cs]
        return nt(wkv_ref[part, :], x_all[j, cs, :]).astype(bf16)

    def att_body(c, unused):
        cs = lanes(c, 128)
        total = jnp.zeros((rows, 128), f32)
        for j in range(slots):
            v = kv_of(j, cs, slice(rows, 2 * rows)).astype(f32)
            total = total + heads.scale(v, score[j, 0:1, cs], score[j, 1:2, cs])
        attended[:, cs] = total
        att_low[:, cs] = total.astype(bf16)
        return unused

    lax.fori_loop(0, events // 128, att_body, 0)

    def out_body(c, unused):
        cs = lanes(c)
        stage[0:width, :] = nn(w("s1t"), att_low[:, cs])[0:width]
        stage[width : 2 * width, :] = fresh_low[:, cs].astype(f32)[0:width]
        x = stage[0 : 2 * rows, :].astype(bf16)
        x_out[:, cs] = x
        pre = nn(wout_ref[...], x)
        pre_out[:, cs] = pre
        hid = (pre * jax.nn.sigmoid(pre)).astype(bf16)
        hid_out[:, cs] = hid
        e = nn(w("s2t"), hid).astype(bf16)
        emb[:, cs] = e
        emb_rows[cs, :] = nt(eye_ref[...], e).astype(bf16)
        return unused

    lax.fori_loop(0, chunks, out_body, 0, unroll=4)

    def row_init(c, unused):
        cs = lanes(c)
        rows_ref[0:1, cs] = jnp.full((1, LANES), mask_fill, f32)
        rows_ref[1:3, cs] = jnp.zeros((2, LANES), f32)
        acc_a[:, cs] = jnp.zeros((rows, LANES), f32)
        return unused

    lax.fori_loop(0, chunks, row_init, 0)

    def dest_of(o):
        at = pl.multiple_of(o * cand_width, cand_width)
        return dest_rows[pl.ds(at, cand_width), :]

    def lse_block(i, unused):
        for side in range(2):
            o = 2 * i + side
            dest = nn(dest_of(o), wd_ref[...]).astype(bf16)
            for c in range(chunks):
                cs = lanes(c)
                logits = nn(dest, emb[:, cs])
                old = rows_ref[0:1, cs]
                top = jnp.maximum(old, jnp.max(logits, 0, keepdims=True))
                rows_ref[0:1, cs] = top
                rows_ref[1:2, cs] = rows_ref[1:2, cs] * jnp.exp(old - top) + jnp.sum(
                    jnp.exp(logits - top), 0, keepdims=True
                )
                hit = lax.broadcasted_iota(jnp.int32, logits.shape, 0) == target_ref[:, cs] - o * cand_width
                rows_ref[2:3, cs] = rows_ref[2:3, cs] + jnp.sum(jnp.where(hit, logits, 0.0), 0, keepdims=True)
        return unused

    lax.fori_loop(0, owners // 2, lse_block, 0)

    mask_row = mask_ref[...].astype(f32)
    log_sum = rows_ref[0:1, :] + jnp.log(rows_ref[1:2, :])
    rows_ref[3:4, :] = log_sum
    rows_ref[4:5, :] = mask_row / jnp.broadcast_to(pos_ref[0:1, 0:1], mask_row.shape)
    loss = jnp.sum(mask_row * (log_sum - rows_ref[2:3, :]), 1, keepdims=True)
    grad_ref[layout.loss : layout.loss + 8, :] = jnp.broadcast_to(loss, (8, 128))

    def back_block(o, grad_dest_w):
        block = dest_of(o)
        dest = nn(block, wd_ref[...]).astype(bf16)
        dest_t = nt(wdt_ref[...], block).astype(bf16)
        block_t = nt(eye_ref[...], block).astype(bf16)

        def chunk(c, unused):
            cs = lanes(c)
            logits = nn(dest, emb[:, cs])
            coeff = rows_ref[4:5, cs]
            hit = lax.broadcasted_iota(jnp.int32, logits.shape, 0) == target_ref[:, cs] - o * cand_width
            grad = jnp.exp(logits - rows_ref[3:4, cs]) - jnp.where(hit, 1.0, 0.0)
            grad = (grad * coeff).astype(bf16)
            slab[0:cand_width, cs] = grad
            return unused

        lax.fori_loop(0, chunks, chunk, 0, unroll=True)
        acc_a[...] += nn(dest_t, slab[0:cand_width, :])
        grad_dest = nn(slab[0:cand_width, :], emb_rows[...]).astype(bf16)
        return grad_dest_w + nn(block_t, grad_dest)[:rows]

    grad_dest_w = lax.fori_loop(0, owners, back_block, jnp.zeros((rows, rows), f32))
    layout.put(grad_ref, "square3", grad_dest_w)

    r0, r1, r2 = slice(0, rows), slice(rows, 2 * rows), slice(2 * rows, 3 * rows)

    def out_back(c, unused):
        cs = lanes(c)
        ge = acc_a[:, cs].astype(bf16)
        slab[r0, cs] = ge
        pre = pre_out[:, cs]
        sig = jax.nn.sigmoid(pre)
        gp = (nn(w("s2"), ge) * (sig * (1.0 + pre * (1.0 - sig)))).astype(bf16)
        slab[r1, cs] = gp
        gm = nn(w("oa"), gp).astype(bf16)
        slab[r2, cs] = gm
        acc_a[:, cs] = nn(w("ob"), gp)
        ga = nn(w("s1"), gm).astype(bf16)
        grad_att[:, cs] = ga
        d0, d1 = heads.sums(ga.astype(f32) * attended[:, cs])
        rows_ref[5:6, cs] = d0
        rows_ref[6:7, cs] = d1
        return unused

    lax.fori_loop(0, chunks, out_back, 0, unroll=4)
    layout.put(grad_ref, "square2", nt(hid_out[...], slab[r0, :]))
    layout.put(grad_ref, "out", nt(slab[r1, :], x_out[...]))
    layout.put(grad_ref, "square1", nt(att_low[...], slab[r2, :]))

    attended[...] = jnp.zeros_like(attended)
    gkv_m[...] = jnp.zeros_like(gkv_m)

    def slot_back(i, unused):
        for side in range(2):
            j = 2 * i + side
            for c in range(events // 256):
                cs = lanes(c, 256)
                kv = kv_of(j, cs, slice(0, 2 * rows)).astype(f32)
                ga = grad_att[:, cs].astype(f32)
                p0, p1 = score[j, 0:1, cs], score[j, 1:2, cs]
                g0, g1 = heads.sums(ga * kv[rows:])
                g0 = p0 * (g0 - rows_ref[5:6, cs]) * scale
                g1 = p1 * (g1 - rows_ref[6:7, cs]) * scale
                attended[:, cs] += heads.scale(kv[:rows], g0, g1)
                gslab[side, 0:rows, cs] = heads.scale(queries[:, cs].astype(f32), g0, g1).astype(bf16)
                gslab[side, rows:2*rows, cs] = heads.scale(ga, p0, p1).astype(bf16)
            both = gslab[side, 0 : 2 * rows, :]
            gkv_m[...] += nn(both, x_all[j])
        return unused

    lax.fori_loop(0, slots // 2, slot_back, 0)
    gkv = gkv_m[...].T
    both = [jnp.concatenate([g[:, :width], g[:, rows : rows + width]], 1)
            for g in (gkv[:width], gkv[256 : 256 + time_width])]
    layout.put(grad_ref, "kv", jnp.concatenate(both, 0))

    for copy in loads:
        copy.wait()
    def gru_back(c, unused):
        cs = lanes(c)
        gq = attended[:, cs].astype(bf16)
        slab[r0, cs] = gq
        gf = acc_a[:, cs] + nn(w("s0"), gq)
        u, cand, r = update[:, cs], cand_act[:, cs], reset_gate[:, cs]
        act = gf * (1.0 - u) * (1.0 - cand * cand)
        gr = (act * gate_n[:, cs] * r * (1.0 - r)).astype(bf16)
        gu = (gf * (mem_src[:, cs] - cand) * u * (1.0 - u)).astype(bf16)
        gn = act.astype(bf16)
        gh = (act * r).astype(bf16)
        slab[r1, cs] = gr
        slab[r2, cs] = gu
        x_out[0:rows, cs] = gn
        hid_out[:, cs] = gh
        pre = pre_msg[:, cs]
        sig = jax.nn.sigmoid(pre)
        back = nn(w("g0r_back"), gr) + nn(w("g0z_back"), gu) + nn(w("g0n_back"), gn)
        att_low[:, cs] = (back * (sig * (1.0 + pre * (1.0 - sig)))).astype(bf16)
        return unused

    lax.fori_loop(0, chunks, gru_back, 0, unroll=4)
    layout.put(grad_ref, "square0", nt(fresh_low[...], slab[r0, :]))
    for index, (left, last) in enumerate(((hidden, x_out[0:rows, :]), (mem_low, hid_out[...]))):
        left = left[...]
        parts = [nt(left, slab[r1, :]), nt(left, slab[r2, :]), nt(left, last)]
        layout.put(grad_ref, f"gru{index}", jnp.concatenate([p[:, :width] for p in parts], 1))
    layout.put(grad_ref, "msg", nt(att_low[...], x_msg[...]))


def main(layout, keep_kv, width, head_dim, cand_width, args):
    events = args[4].shape[1]
    slots = args[7].shape[0] * args[7].shape[1]
    late = args[16:]
    rows = pad_to(width, 16)
    cands = args[1].shape[0]
    smem = pl.BlockSpec(memory_space=pltpu.SMEM)
    vmem = pl.BlockSpec(memory_space=pltpu.VMEM)
    hbm = pl.BlockSpec(memory_space=pl.ANY)
    low = lambda *shape: pltpu.VMEM(shape, bf16)
    full = lambda *shape: pltpu.VMEM(shape, f32)
    return pl.pallas_call(
        partial(main_kernel, (width, head_dim, keep_kv, cand_width, layout)),
        out_shape=jax.ShapeDtypeStruct((layout.total, 128), f32),
        in_specs=[smem, smem] + [vmem] * 14 + [hbm] * len(late),
        out_specs=vmem,
        scratch_shapes=[pltpu.VMEM(x.shape, x.dtype) for x in late]
        + [
            full(2 * events + 64, 128),
            full(2 * events + 64, 128),
            low(slots, events, 384),
            full(events, 128),
            low(slots if keep_kv else 1, 2 * rows if keep_kv else 16, events),
            full(slots, 8, events),
            low(cands, 256),
            low(max(3 * rows, cand_width), events),
            low(256, 256),
            low(2, max(2 * rows, cand_width), events),
            full(2 * rows, LANES),
            low(rows, events),
            low(2 * rows, events),
            low(rows, events),
            low(rows, events),
            low(events, rows),
            full(rows, events),
            full(rows, events),
            full(rows, events),
            low(rows, events),
            full(2 * rows, 384),
            low(256, 128),
            full(8, events),
            pltpu.SemaphoreType.DMA((len(late),)),
        ],
        compiler_params=pltpu.CompilerParams(vmem_limit_bytes=63 * 2**20),
        name="train",
    )(*args)


def reduce_kernel(own, batch, streams, grad_ref, out_ref, acc, recv, local_sem, send_sem, recv_sem):
    place = {"own": lax.axis_index("own"), "batch": lax.axis_index("batch")}

    digits = [lax.div(place["own"], 1 << b) % 2 for b in range(own.bit_length() - 1)]

    def parts(bits):
        if not bits:
            return batch, place["batch"]
        return 1 << len(bits), sum(digits[b] * (1 << i) for i, b in enumerate(bits))

    def peers(bits):
        if not bits:
            for d in range(1, batch):
                there = lax.rem(place["batch"] + d, batch)
                yield (there, place["own"]), there
            return
        for pattern in range(1, 1 << len(bits)):
            there, at = place["own"], 0
            for i, b in enumerate(bits):
                digit = digits[b]
                if pattern >> i & 1:
                    there, digit = there + (1 << b) * (1 - 2 * digit), 1 - digit
                at = at + digit * (1 << i)
            yield (place["batch"], there), at

    load = pltpu.make_async_copy(grad_ref, acc, local_sem)
    load.start()
    barrier = pltpu.get_barrier_semaphore()
    devices = {}
    for order in [order for start, size, order in streams]:
        for bits in order:
            devices.setdefault(tuple(sorted(bits)), [device for device, there in peers(sorted(bits))])
    greeted = [device for bits in devices if all(set(bits) >= set(other) or not set(bits) & set(other) for other in devices)
               for device in devices[bits]]
    for device in greeted:
        pl.semaphore_signal(barrier, inc=1, device_id=device, device_id_type=MESH)
    pl.semaphore_wait(barrier, len(greeted))
    load.wait()

    sent = []
    longest = max(len(order) for start, size, order in streams)

    class Stream:
        def __init__(self, index, start, size, order):
            self.index, self.base, self.size, self.inner, self.order = index, start, size, start, order
            self.copies = []
            self.slots = [0]
            for bits in order:
                self.slots.append(self.slots[-1] + parts(bits)[0] - 1)

        def copy(self, source, target, peer, slot):
            copy = pltpu.make_async_remote_copy(
                src_ref=source, dst_ref=target,
                send_sem=send_sem.at[self.index, slot], recv_sem=recv_sem.at[self.index, slot],
                device_id=peer, device_id_type=MESH,
            )
            copy.start()
            self.copies.append(copy)
            sent.append(copy)

        def scatter(self, step):
            count, mine = parts(self.order[step])
            piece = self.size // count
            for d, (peer, theirs) in enumerate(peers(self.order[step]), 1):
                away = pl.multiple_of(self.base + theirs * piece, 8)
                self.copy(
                    acc.at[pl.ds(away, piece), :], recv.at[pl.ds(self.inner + (d - 1) * piece, piece), :],
                    peer, self.slots[step] + d - 1,
                )
            self.base = pl.multiple_of(self.base + mine * piece, 8)
            self.size = piece

        def add(self, step):
            target = out_ref if step == len(self.order) - 1 else acc
            part = pl.ds(self.base, self.size)
            total = acc[part, :]
            for copy in self.copies:
                copy.wait_recv()
                total = total + recv[pl.ds(self.inner, self.size), :]
                self.inner += self.size
            target[part, :] = total
            self.copies = []

        def gather(self, step):
            count, mine = parts(self.order[step])
            part = pl.ds(self.base, self.size)
            for d, (peer, theirs) in enumerate(peers(self.order[step]), 1):
                self.copy(out_ref.at[part, :], out_ref.at[part, :], peer, self.slots[-1] + self.slots[step] + d - 1)
            self.base = pl.multiple_of(self.base - mine * self.size, 8)
            self.size *= count

        def gathered(self):
            for copy in self.copies:
                copy.wait_recv()
            self.copies = []

    flows = [Stream(index, *stream) for index, stream in enumerate(streams)]
    for step in range(2 * longest + 1):
        for flow in flows:
            rounds = len(flow.order)
            if 0 < step <= rounds:
                flow.add(step - 1)
            elif rounds < step <= 2 * rounds:
                flow.gathered()
            if step < rounds:
                flow.scatter(step)
            elif step < 2 * rounds:
                flow.gather(2 * rounds - 1 - step)
    for copy in sent:
        copy.wait_send()


def reduce_all(own, batch, packed):
    total = packed.shape[0]
    own_bits = own.bit_length() - 1
    fold = 8 * own * batch
    core, xs, ys, zs = (0,), tuple(range(1, (own_bits + 1) // 2)), tuple(range((own_bits + 1) // 2, own_bits)), ()
    plan = ((6, (core, xs + ys, zs)), (3, (core, zs, xs + ys)), (6, (core, ys + xs, zs)), (3, (core, zs, ys + xs)))
    streams = []
    start = 0
    blocks = total // fold
    shares = sum(share for share, order in plan)
    for index, (share, order) in enumerate(plan):
        size = total - start if index == len(plan) - 1 else blocks * share // shares * fold
        if size:
            streams.append((start, size, order))
        start += size
    count = 2 * (own * batch)
    return pl.pallas_call(
        partial(reduce_kernel, own, batch, streams),
        out_shape=jax.ShapeDtypeStruct(packed.shape, f32),
        in_specs=[pl.BlockSpec(memory_space=pl.ANY)],
        out_specs=pl.BlockSpec(memory_space=pltpu.VMEM),
        scratch_shapes=[
            pltpu.VMEM(packed.shape, f32),
            pltpu.VMEM(packed.shape, f32),
            pltpu.SemaphoreType.DMA,
            pltpu.SemaphoreType.DMA((len(streams), count)),
            pltpu.SemaphoreType.DMA((len(streams), count)),
        ],
        compiler_params=pltpu.CompilerParams(
            collective_id=2, has_side_effects=True, vmem_limit_bytes=63 * 2**20
        ),
        name="reduce",
    )(packed)


def update_kernel(layout, step_rate, grad_ref, pos_ref, *refs):
    sources, targets, loss_ref, count_ref = refs[:15], refs[15:30], refs[30], refs[31]
    held, laid = refs[32:47], refs[47:49]
    in_sem, out_sem = refs[49:]
    loss_ref[...] = grad_ref[layout.loss : layout.loss + 1, 0:1]
    count_ref[...] = pos_ref[0:1, 0:1]
    arrive = [pltpu.make_async_copy(sources[i], held[i], in_sem.at[i]) for i in range(15)]
    leave = [pltpu.make_async_copy(held[i], targets[(i + 5) % 10 if i < 10 else i], out_sem.at[i]) for i in range(15)]
    order = (1, 2, 0, 3, 4)
    for index in order:
        for kind in range(3):
            arrive[5 * kind + index].start()

    for ref, name, parts in ((laid[0], "gru", 2), (laid[1], "square", 4)):
        for part in range(parts):
            for columns, gradient in layout.tiles(grad_ref, f"{name}{part}"):
                ref[:, part, columns] = gradient

    def step(index, at, gradient):
        weights, moments, averages = (held[5 * kind + index] for kind in range(3))
        moment = mu_coef * moments[at] + gradient
        weight = weights[at] - step_rate * (gradient + mu_coef * moment)
        moments[at] = moment
        weights[at] = weight
        averages[at] = (1.0 - avg_coef) * averages[at] + avg_coef * weight

    for index in order:
        for kind in range(3):
            arrive[5 * kind + index].wait()
        if index in (1, 2):
            step(index, slice(None), laid[index - 1][...])
        else:
            for columns, gradient in layout.tiles(grad_ref, ("msg", "", "", "kv", "out")[index]):
                step(index, (slice(None), columns), gradient)
        for kind in range(3):
            leave[5 * kind + index].start()
    for copy in leave:
        copy.wait()


def update_all(layout, step_rate, packed, positives, params):
    vmem = pl.BlockSpec(memory_space=pltpu.VMEM)
    hbm = pl.BlockSpec(memory_space=pl.ANY)
    buffers = [pltpu.VMEM(p.shape, f32) for p in params]
    return pl.pallas_call(
        partial(update_kernel, layout, step_rate),
        out_shape=tuple(jax.ShapeDtypeStruct(p.shape, f32) for p in params[5:10] + params[:5] + params[10:])
        + (jax.ShapeDtypeStruct((1, 1), f32),) * 2,
        in_specs=[vmem] * 2 + [hbm] * 15,
        out_specs=(hbm,) * 15 + (vmem,) * 2,
        scratch_shapes=buffers + buffers[1:3] + [pltpu.SemaphoreType.DMA((15,))] * 2,
        compiler_params=pltpu.CompilerParams(vmem_limit_bytes=63 * 2**20),
        name="update",
    )(packed, positives, *params)


def turned(arrays):
    msg, gru, square, kv, out = arrays
    return (msg.T, gru.transpose(1, 0, 2), square.transpose(1, 0, 2), kv, out.T)


def local(
    memory, last_update, src_local, edge_feat, event_time, nbr_owner, nbr_ids, nbr_mask, event_mask,
    dest_local, target, w_msg, w_gru, w_square, w_key_value, w_output,
    mom_msg, mom_gru, mom_square, mom_key_value, mom_output,
    avg_msg, avg_gru, avg_square, avg_key_value, avg_output,
):
    own = lax.axis_size("own")
    batch = lax.axis_size("batch")
    events, edge = edge_feat.shape
    nodes, width = memory.shape
    head_dim = width // HEADS
    time_width = w_key_value.shape[0] - width
    columns = time_columns(time_width, 128)
    layout = Layout(
        width, w_msg.shape[0], w_output.shape[0], w_gru.shape[2], *w_key_value.shape, 8 * own * batch
    )
    weights = turned((w_msg, w_gru, w_square, w_key_value, w_output))
    time_row, mask_row, src_row, target_row = (x[None, :] for x in (event_time, event_mask, src_local, target))
    table, cand_ids, flat_ids, positives, newest, *handed = exchange(
        own, batch,
        (memory.T, last_update[None, :], dest_local[None, :], time_row, mask_row, src_row,
         nbr_owner.T, nbr_ids.transpose(2, 1, 0), jnp.asarray(columns)) + weights + (edge_feat.T,),
    )
    packed = main(
        layout, own * nodes <= 16384, width, head_dim, dest_local.shape[0],
        (flat_ids.reshape(-1), cand_ids.reshape(-1), positives, table, time_row, mask_row, target_row,
         nbr_mask.transpose(2, 1, 0), *handed[:5], jnp.asarray(columns.T[:8]), *handed[5:]),
    )
    summed = reduce_all(own, batch, packed)
    step_rate = rate_coef * math.sqrt(events * own * batch)
    *states, loss, count = update_all(
        layout, step_rate, summed, positives,
        weights
        + turned((mom_msg, mom_gru, mom_square, mom_key_value, mom_output))
        + turned((avg_msg, avg_gru, avg_square, avg_key_value, avg_output)),
    )
    states = [x for i in range(3) for x in turned(states[5 * i : 5 * i + 5])]
    return (loss.reshape(()), count.reshape(()), newest.reshape(-1), *states)


def solution(mesh):
    row = P(("batch", "own"))
    placed = (
        (P("own", None), P("own"), row, P(("batch", "own"), None), row, P(("batch", "own"), None))
        + (P(("batch", "own"), None, None),) * 2
        + (row,) * 3
        + (P(),) * 15
    )
    return jax.shard_map(
        local,
        mesh=mesh,
        in_specs=placed,
        out_specs=(P(), P(), P("own")) + (P(),) * 15,
        check_vma=False,
    )
```

```python
from functools import partial
import math

import jax
import jax.numpy as jnp
import numpy as np
from jax import lax
from jax.experimental import pallas as pl
from jax.experimental.pallas import tpu as pltpu
from jax.sharding import PartitionSpec as P

HEADS = 2
LANES = 256
MESH = pl.DeviceIdType.MESH
f32 = jnp.float32
bf16 = jnp.bfloat16

mu_coef = 0.9
avg_coef = 0.1
rate_coef = 0.008
mask_fill = -1e30

COS_TERMS = (
    1.0,
    -19.73920440673828,
    64.93911743164062,
    -85.45011901855469,
    60.16745376586914,
    -25.966907501220703,
    6.527653217315674,
)


def pad_to(size, step):
    return -(-size // step) * step


def nn(a, b):
    return lax.dot_general(a, b, (((1,), (0,)), ((), ())), preferred_element_type=f32)


def nt(a, b):
    return lax.dot_general(a, b, (((1,), (1,)), ((), ())), preferred_element_type=f32)


def flip_bit(index, bit):
    size = 1 << bit
    return index + size * (1 - 2 * (lax.div(index, size) % 2))


def time_columns(time_width, rows):
    turns = 10.0 ** (-np.linspace(0.0, 9.0, time_width)) / (2.0 * np.pi)
    mant, expo = np.frexp(turns)
    high = np.ldexp(np.round(mant * 4096.0) / 4096.0, expo)
    out = np.zeros((rows, 128), np.float32)
    out[:time_width, 0] = high
    out[:time_width, 1] = turns - high
    return out


def cos_rows(delta, high, low):
    turns = delta * high
    rest = turns - jnp.floor(turns + 0.5) + delta * low
    square = rest * rest
    value = square * COS_TERMS[-1] + COS_TERMS[-2]
    for term in COS_TERMS[-3::-1]:
        value = value * square + term
    return value


class Heads:
    def __init__(self, head_dim, rows):
        self.low = head_dim // 8 * 8
        self.high = pad_to(head_dim, 8)
        self.cut = head_dim - self.low
        self.rows = rows

    def split(self, lanes):
        return lax.broadcasted_iota(jnp.int32, (8, lanes), 0) < self.cut

    def sums(self, x):
        lanes = x.shape[1]
        mid = x[self.low : self.high]
        first = self.split(lanes)
        a = jnp.sum(x[: self.low].reshape(self.low // 8, 8, lanes), 0)
        b = jnp.sum(x[self.high :].reshape((self.rows - self.high) // 8, 8, lanes), 0)
        a = a + jnp.where(first, mid, 0.0)
        b = b + jnp.where(first, 0.0, mid)
        return jnp.sum(a, 0, keepdims=True), jnp.sum(b, 0, keepdims=True)

    def scale(self, x, p0, p1):
        lanes = x.shape[1]
        mid = jnp.where(self.split(lanes), p0, p1)
        return jnp.concatenate(
            [x[: self.low] * p0, x[self.low : self.high] * mid, x[self.high :] * p1], 0
        )


GATES = ("g0r", "g0z", "g0n", "g1r", "g1z", "g1n", "s0t")
SQUARES = ("s1t", "s2t", "g0r_back", "g0z_back", "g0n_back", "s0", "s1", "s2", "oa", "ob")
LOW_STATE = ("queries", "fresh_low", "x_msg", "mem_low", "hidden")
STATE = ("mem_src", "pre_msg", "reset_gate", "update", "cand_act", "gate_n")


def exchange_kernel(
    own, batch,
    mem_ref, last_ref, cand_ref, time_ref, mask_ref, src_ref, owner_ref, nbr_ref, freq_ref,
    msg_hbm, gru_hbm, square_hbm, kv_hbm, outw_hbm, edge_hbm,
    table_ref, ids_ref, flat_ref, pos_ref, newest_ref, *rest,
):
    handed = rest[: 5 + len(LOW_STATE) + len(STATE)]
    rest = rest[len(handed) :]
    staged = rest[: len(handed)]
    wsq_ref, wout_ref, wkv_ref, wd_ref, wdt_ref = staged[:5]
    state = dict(zip(LOW_STATE + STATE, staged[5:]))
    (msg_ref, gru_ref, square_ref, kv_ref, outw_ref, edge_ref, gates_ref, wmsg_ref, mem3_ref, stage,
     shard, ext, pairs, square_pad, wide_pad, kv_pad, batch_buf, own_buf,
     local_sem, load_sem, hand_sem,
     table_send, table_recv, batch_send, batch_recv, own_send, own_recv) = rest[len(handed) :]
    loads = [
        pltpu.make_async_copy(source, target, load_sem.at[i])
        for i, (source, target) in enumerate((
            (gru_hbm, gru_ref), (square_hbm, square_ref), (outw_hbm, outw_ref),
            (msg_hbm, msg_ref), (kv_hbm, kv_ref), (edge_hbm, edge_ref),
        ))
    ]
    for copy in loads:
        copy.start()
    hands = [pltpu.make_async_copy(staged[i], handed[i], hand_sem.at[i]) for i in range(len(handed))]
    me = lax.axis_index("own")
    group = lax.axis_index("batch")
    barrier = pltpu.get_barrier_semaphore()
    for step in range(1, own):
        pl.semaphore_signal(barrier, inc=1, device_id=(group, lax.rem(me + step, own)), device_id_type=MESH)
    for step in range(1, batch):
        pl.semaphore_signal(barrier, inc=1, device_id=(lax.rem(group + step, batch), me), device_id_type=MESH)

    width, nodes = mem_ref.shape
    rows = pad_to(width, 16)
    ext[...] = jnp.zeros_like(ext)
    ext[0:width, :] = mem_ref[...]
    last = last_ref[...]
    ext[width : width + 1, :] = lax.div(last, 8).astype(f32)
    ext[width + 1 : width + 2, :] = lax.rem(last, 8).astype(f32)

    def turn(i, unused):
        block = ext[:, pl.ds(pl.multiple_of(i * 128, 128), 128)].T
        base = pl.multiple_of(i * 256, 256)
        pairs[pl.ds(base, 128, stride=2), :] = block[:, :128]
        pairs[pl.ds(base + 1, 128, stride=2), :] = block[:, 128:]
        return unused

    lax.fori_loop(0, nodes // 128, turn, 0)

    def pack(i, unused):
        got = [pairs[pl.ds(pl.multiple_of(i * 128, 128) + 2 * k, 2), :] for k in range(64)]
        for k in range(64):
            shard[i * 64 + k] = got[k].astype(bf16)
        return unused

    lax.fori_loop(0, nodes // 64, pack, 0)
    pl.semaphore_wait(barrier, own + batch - 2)

    half = nodes // 2
    bits = own.bit_length() - 1
    others = list(range(1, bits))
    cut = len(others) // 2
    orders = (others + [0], others[cut:] + others[:cut] + [0])

    def shard_copy(stream, pattern, bit):
        peer = flip_bit(me, bit)
        source = me
        for b in range(bits):
            if pattern >> b & 1:
                source = flip_bit(source, b)
        part = pl.ds(pl.multiple_of(source * nodes + stream * half, half), half)
        slot = pattern | 1 << bit
        src = shard.at[pl.ds(stream * half, half)] if pattern == 0 else table_ref.at[part]
        return pltpu.make_async_remote_copy(
            src_ref=src, dst_ref=table_ref.at[part],
            send_sem=table_send.at[stream, slot], recv_sem=table_recv.at[stream, slot],
            device_id=(group, peer), device_id_type=MESH,
        )

    copies = [{}, {}]
    for step in range(bits):
        for stream in range(2):
            bit = orders[stream][step]
            copy = shard_copy(stream, 0, bit)
            copy.start()
            copies[stream][1 << bit] = copy
    mine = pltpu.make_async_copy(
        shard, table_ref.at[pl.ds(pl.multiple_of(me * nodes, nodes), nodes)], local_sem
    )
    mine.start()

    events = src_ref.shape[1]
    time_row = time_ref[...].astype(f32)
    src_row = src_ref[...]
    best = []
    tile = 256
    for start in range(0, nodes, tile):
        node = lax.broadcasted_iota(jnp.int32, (tile, 128), 0) + start
        top = jnp.full((tile, 128), -1.0, f32)
        for lane in range(0, events, 128):
            hit = src_row[:, lane : lane + 128] == node
            top = jnp.maximum(top, jnp.where(hit, time_row[:, lane : lane + 128], -1.0))
        best.append(jnp.max(top.T, 0, keepdims=True))
    newest = jnp.concatenate(best, 1).astype(jnp.int32)
    newest = jnp.maximum(newest, last)
    count = jnp.sum(mask_ref[...].astype(f32), 1, keepdims=True).astype(jnp.int32)
    batch_buf[0, 0:1, :] = newest
    batch_buf[0, 1:2, :] = jnp.broadcast_to(count, (1, nodes))

    def peer_copy(step):
        return pltpu.make_async_remote_copy(
            src_ref=batch_buf.at[0], dst_ref=batch_buf.at[step],
            send_sem=batch_send.at[step], recv_sem=batch_recv.at[step],
            device_id=(lax.rem(group + step, batch), me), device_id_type=MESH,
        )

    peers = [peer_copy(step) for step in range(1, batch)]
    for copy in peers:
        copy.start()

    picks = owner_ref.shape[0]
    per_pick = nbr_ref.shape[0]
    for s in range(per_pick):
        flat = owner_ref[...] * nodes + nbr_ref[s]
        for block in range(events // 128):
            at = (s * (events // 128) + block) * picks
            flat_ref[at : at + picks, :] = flat[:, block * 128 : block * 128 + 128]
    whole = ext[0:rows, :]
    part0 = whole.astype(bf16)
    whole = whole - part0.astype(f32)
    part1 = whole.astype(bf16)
    mem3_ref[0:rows, :] = part0
    mem3_ref[rows : 2 * rows, :] = part1
    mem3_ref[2 * rows :, :] = (whole - part1.astype(f32)).astype(bf16)

    square_pad[...] = jnp.zeros_like(square_pad)
    for copy in loads:
        copy.wait()

    def put(name, value):
        square_pad[0:width, 0:width] = value
        if name in GATES:
            gates_ref[GATES.index(name)] = square_pad[...].astype(bf16)
        else:
            wsq_ref[SQUARES.index(name)] = square_pad[...].astype(bf16)

    for index in range(2):
        for gate, letter in enumerate("rzn"):
            value = gru_ref[:, index, gate * width : gate * width + width]
            put(f"g{index}{letter}", value.T)
            if index == 0:
                put(f"g0{letter}_back", value)
    for index in range(3):
        value = square_ref[:, index, :]
        put(f"s{index}", value)
        put(f"s{index}t", value.T)
    put("oa", outw_ref[:, 0:width].T)
    put("ob", outw_ref[:, width : 2 * width].T)
    wide_pad[...] = jnp.zeros_like(wide_pad)
    wide_pad[0:width, 0 : 2 * width] = outw_ref[...]
    wout_ref[...] = wide_pad[:, 0 : wout_ref.shape[1]].astype(bf16)
    wide_pad[0:width, 0 : msg_ref.shape[1]] = msg_ref[...]
    wmsg_ref[...] = wide_pad[...].astype(bf16)
    last_square = square_ref[:, 3, :]
    kv_pad[...] = jnp.zeros_like(kv_pad)
    kv_pad[0:width, 0:width] = last_square
    wd_ref[...] = kv_pad[0 : wd_ref.shape[0], 0 : wd_ref.shape[1]].astype(bf16)
    kv_pad[0:width, 0:width] = last_square.T
    wdt_ref[...] = kv_pad[0 : wdt_ref.shape[0], 0 : wdt_ref.shape[1]].astype(bf16)
    time_width = kv_ref.shape[0] - width
    kv_pad[...] = jnp.zeros_like(kv_pad)
    for index in range(2):
        part = kv_ref[:, index * width : index * width + width]
        kv_pad[index * rows : index * rows + width, 0:width] = part[0:width].T
        kv_pad[index * rows : index * rows + width, 256 : 256 + time_width] = part[width:].T
    wkv_ref[...] = kv_pad[...].astype(bf16)
    for copy in hands[:5]:
        copy.start()

    def forward(step):
        for stream in range(2):
            order = orders[stream]
            held = [0]
            for bit in order[:step]:
                held = held + [p | 1 << bit for p in held]
            for pattern in held:
                slot = pattern | 1 << order[step]
                copies[stream][slot].wait_recv()
                for bit in order[step + 1 :]:
                    copy = shard_copy(stream, slot, bit)
                    copy.start()
                    copies[stream][slot | 1 << bit] = copy

    forward(0)
    total = count
    for step, copy in enumerate(peers, 1):
        copy.wait_recv()
        newest = jnp.maximum(newest, batch_buf[step, 0:1, :])
        total = total + batch_buf[step, 1:2, 0:1]
    newest_ref[...] = newest

    cands = cand_ref.shape[1]
    own_buf[0, 0:1, :] = cand_ref[...] + me * nodes
    own_buf[0, 1:2, :] = jnp.broadcast_to(total, (1, cands))

    def owner_copy(step):
        return pltpu.make_async_remote_copy(
            src_ref=own_buf.at[0], dst_ref=own_buf.at[step],
            send_sem=own_send.at[step], recv_sem=own_recv.at[step],
            device_id=(group, lax.rem(me + step, own)), device_id_type=MESH,
        )

    owners = [owner_copy(step) for step in range(1, own)]
    for copy in owners:
        copy.start()

    edge = edge_ref.shape[0]
    high, low = freq_ref[:, 0:1], freq_ref[:, 1:2]
    stage[...] = jnp.zeros_like(stage)

    def w(name):
        return gates_ref[GATES.index(name)]

    def gru_body(c, unused):
        cs = pl.ds(pl.multiple_of(c * LANES, LANES), LANES)
        node = lax.broadcasted_iota(jnp.int32, (nodes, LANES), 0)
        onehot = (node == src_ref[:, cs]).astype(f32).astype(bf16)
        parts = nn(mem3_ref[...], onehot)
        mem = parts[:rows] + parts[rows : 2 * rows] + parts[2 * rows :]
        state["mem_src"][:, cs] = mem
        delta = time_ref[:, cs].astype(f32) - 8.0 * mem[width : width + 1] - mem[width + 1 : width + 2]
        stage[0:width, :] = mem[0:width]
        stage[width : width + edge, :] = edge_ref[:, cs].astype(f32)
        stage[width + edge : width + edge + time_width, :] = cos_rows(delta, high, low)[0:time_width]
        x = stage[...].astype(bf16)
        state["x_msg"][:, cs] = x
        m_low = mem.astype(bf16)
        state["mem_low"][:, cs] = m_low
        pre = nn(wmsg_ref[...], x)
        state["pre_msg"][:, cs] = pre
        hid = (pre * jax.nn.sigmoid(pre)).astype(bf16)
        state["hidden"][:, cs] = hid
        r = jax.nn.sigmoid(nn(w("g0r"), hid) + nn(w("g1r"), m_low))
        state["reset_gate"][:, cs] = r
        u = jax.nn.sigmoid(nn(w("g0z"), hid) + nn(w("g1z"), m_low))
        state["update"][:, cs] = u
        gn = nn(w("g1n"), m_low)
        state["gate_n"][:, cs] = gn
        cand = jnp.tanh(nn(w("g0n"), hid) + r * gn)
        state["cand_act"][:, cs] = cand
        fresh = ((1.0 - u) * cand + u * mem).astype(bf16)
        state["fresh_low"][:, cs] = fresh
        state["queries"][:, cs] = nn(w("s0t"), fresh).astype(bf16)
        return unused

    lax.fori_loop(0, events // LANES, gru_body, 0)
    for copy in hands[5:]:
        copy.start()
    for step in range(1, bits):
        forward(step)

    for step in range(own):
        if step:
            owners[step - 1].wait_recv()
            total = total + own_buf[step, 1:2, 0:1]
        source = lax.rem(me - step + own, own)
        for block in range(cands // 128):
            ids_ref[pl.ds(source * (cands // 128) + block, 1), :] = own_buf[
                step, 0:1, block * 128 : block * 128 + 128
            ]
    pos_ref[...] = jnp.broadcast_to(jnp.maximum(total.astype(f32), 1.0), pos_ref.shape)
    mine.wait()
    for copy in hands:
        copy.wait()
    for copy in peers + owners:
        copy.wait_send()
    for stream in range(2):
        for slot in copies[stream]:
            copies[stream][slot].wait_send()


def exchange(own, batch, args):
    mem, last, cand, time, mask, src, owner, nbr, freq, msg, gru, square, kv, outw, edge = args
    width, nodes = mem.shape
    events = src.shape[1]
    cands = cand.shape[1]
    rows = pad_to(width, 16)
    wide = pad_to(msg.shape[1], 16)
    vmem = pl.BlockSpec(memory_space=pltpu.VMEM)
    hbm = pl.BlockSpec(memory_space=pl.ANY)
    whole = lambda *shape: jax.ShapeDtypeStruct(shape, jnp.int32)
    handed = [
        ((len(SQUARES), rows, rows), bf16),
        ((rows, 2 * rows), bf16),
        ((2 * rows, 384), bf16),
        ((256, rows), bf16),
        ((rows, 256), bf16),
    ]
    handed += [((wide if name == "x_msg" else rows, events), bf16) for name in LOW_STATE]
    handed += [((rows, events), f32) for name in STATE]
    return pl.pallas_call(
        partial(exchange_kernel, own, batch),
        out_shape=(
            jax.ShapeDtypeStruct((own * nodes, 2, 128), bf16),
            whole(own * cands // 128, 128),
            whole(nbr.shape[0] * nbr.shape[1] * events // 128, 128),
            jax.ShapeDtypeStruct((8, 128), f32),
            whole(1, nodes),
        )
        + tuple(jax.ShapeDtypeStruct(*h) for h in handed),
        in_specs=[vmem] * 9 + [hbm] * 6,
        out_specs=(hbm,) + (vmem,) * 4 + (hbm,) * len(handed),
        scratch_shapes=[pltpu.VMEM(*h) for h in handed]
        + [pltpu.VMEM(x.shape, x.dtype) for x in (msg, gru, square, kv, outw, edge)]
        + [
            pltpu.VMEM((len(GATES), rows, rows), bf16),
            pltpu.VMEM((rows, wide), bf16),
            pltpu.VMEM((3 * rows, nodes), bf16),
            pltpu.VMEM((wide, LANES), f32),
            pltpu.VMEM((nodes, 2, 128), bf16),
            pltpu.VMEM((256, nodes), f32),
            pltpu.VMEM((2 * nodes + 64, 128), f32),
            pltpu.VMEM((rows, rows), f32),
            pltpu.VMEM((rows, wide), f32),
            pltpu.VMEM((2 * rows, 384), f32),
            pltpu.VMEM((batch, 8, nodes), jnp.int32),
            pltpu.VMEM((own, 8, cands), jnp.int32),
            pltpu.SemaphoreType.DMA,
            pltpu.SemaphoreType.DMA((6,)),
            pltpu.SemaphoreType.DMA((len(handed),)),
            pltpu.SemaphoreType.DMA((2, own)),
            pltpu.SemaphoreType.DMA((2, own)),
            pltpu.SemaphoreType.DMA((batch,)),
            pltpu.SemaphoreType.DMA((batch,)),
            pltpu.SemaphoreType.DMA((own,)),
            pltpu.SemaphoreType.DMA((own,)),
        ],
        compiler_params=pltpu.CompilerParams(
            collective_id=1, has_side_effects=True, vmem_limit_bytes=63 * 2**20
        ),
        name="exchange",
    )(*args)


class Layout:
    def __init__(self, width, wide, deep, gates, kv_rows, kv_cols, fold):
        rows = pad_to(width, 8)
        self.width = width
        self.pieces = {}
        row = 0
        for name, depth, columns in (
            ("msg", width, wide),
            ("out", width, deep),
            ("kv", kv_rows, kv_cols),
            ("gru0", width, gates),
            ("gru1", width, gates),
            ("square0", width, width),
            ("square1", width, width),
            ("square2", width, width),
            ("square3", width, width),
        ):
            tiles = []
            for column in range(0, columns, 128):
                size = min(128, columns - column)
                if size < 128 and name[:3] in ("gru", "squ"):
                    tiles.append([column, size, None, None])
                else:
                    tiles.append([column, size, row, 0])
                    row += pad_to(depth, 8)
            self.pieces[name] = (depth, tiles)
        host = self.pieces["msg"][1][-1]
        lane = pad_to(host[1], 8)
        for name in ("gru0", "gru1"):
            tile = self.pieces[name][1][-1]
            if tile[2] is None:
                assert lane + tile[1] <= 128
                tile[2:] = [host[2], lane]
                lane += tile[1]
        for pair in range(2):
            for side in range(2):
                tile = self.pieces[f"square{2 * pair + side}"][1][-1]
                assert tile[1] <= 64
                tile[2:] = [row, 64 * side]
            row += rows
        self.loss = row
        row += 8
        self.total = pad_to(row, fold)

    def put(self, ref, name, value):
        depth, tiles = self.pieces[name]
        for column, size, row, lane in tiles:
            ref[row : row + depth, lane : lane + size] = value[:depth, column : column + size]

    def tiles(self, ref, name):
        depth, tiles = self.pieces[name]
        for column, size, row, lane in tiles:
            yield slice(column, column + size), ref[row : row + depth, lane : lane + size]


def main_kernel(
    dims,
    ids_ref, cand_ref, pos_ref, table_ref, time_ref, mask_ref, target_ref, valid_ref,
    wsq_ref, wout_ref, wkv_ref, wd_ref, wdt_ref, freq_row_ref, queries, fresh_low, *rest,
):
    late = rest[: len(LOW_STATE) + len(STATE) - 2]
    grad_ref, load_sem = rest[len(late)], rest[-1]
    held = rest[len(late) + 1 : 2 * len(late) + 1]
    x_msg, mem_low, hidden, mem_src, pre_msg, reset_gate, update, cand_act, gate_n = held
    (
        xs, xs2, x_all, time_all, kv_all, score, dest_rows, slab, eye_ref, gslab, stage,
        att_low, x_out, hid_out, emb, emb_rows, attended, pre_out,
        acc_a, grad_att, gkv_m, pick_last, rows_ref,
    ) = rest[2 * len(late) + 1 : -1]
    loads = [pltpu.make_async_copy(late[i], held[i], load_sem.at[i]) for i in range(len(late))]
    for copy in loads:
        copy.start()
    width, head_dim, keep_kv, cand_width, layout = dims
    events = time_ref.shape[1]
    per_pick, picks = valid_ref.shape[:2]
    slots = per_pick * picks
    rows = pad_to(width, 16)
    time_width = layout.pieces["kv"][0] - width
    heads = Heads(head_dim, rows)
    scale = head_dim ** (-0.5)
    high_row, low_row = freq_row_ref[0:1, :], freq_row_ref[1:2, :]
    chunks = events // LANES
    owners = cand_ref.shape[0] // cand_width

    def w(name):
        return wsq_ref[SQUARES.index(name)]

    def gather(buf, read_id, at):
        got = [table_ref[read_id(k)] for k in range(128)]
        for k in range(0, 128, 2):
            pair = jnp.concatenate([got[k].astype(f32), got[k + 1].astype(f32)], 0)
            buf[pl.ds(pl.multiple_of(2 * at, 256) + 2 * k, 4), :] = pair

    def gathered(buf, start, count):
        base = pl.multiple_of(2 * start, 2 * count)
        return jnp.concatenate(
            [buf[pl.ds(base, count, stride=2), :], buf[pl.ds(base + 1, count, stride=2), :]], 1
        ).astype(bf16)

    grad_ref[layout.loss :, :] = jnp.zeros_like(grad_ref[layout.loss :, :])
    host = layout.pieces["msg"][1][-1][2]
    grad_ref[host : host + rows, :] = jnp.zeros((rows, 128), f32)
    eye = lax.broadcasted_iota(jnp.int32, (256, 256), 0) == lax.broadcasted_iota(jnp.int32, (256, 256), 1)
    eye_ref[...] = eye.astype(f32).astype(bf16)
    stage[...] = jnp.zeros_like(stage)
    lane = lax.broadcasted_iota(jnp.int32, (256, 128), 0)
    pick_last[...] = jnp.where(lane == width, 8.0, jnp.where(lane == width + 1, 1.0, 0.0)).astype(bf16)
    for start in range(0, events, 128):
        time_all[start : start + 128, :] = jnp.broadcast_to(
            time_ref[:, start : start + 128].astype(f32), (128, 128)
        ).T

    def cand_body(o, unused):
        def fill(i, unused):
            gather(xs, lambda k: cand_ref[o * cand_width + i * 128 + k], i * 128)
            return unused

        lax.fori_loop(0, cand_width // 128, fill, 0)
        at = pl.multiple_of(o * cand_width, cand_width)
        dest_rows[pl.ds(at, cand_width), :] = gathered(xs, 0, cand_width)
        return unused

    lax.fori_loop(0, owners, cand_body, 0)

    def lanes(c, size=LANES):
        return pl.ds(pl.multiple_of(c * size, size), size)

    def fetch(buf, j, i):
        base = ((lax.div(j, picks) * (events // 128) + i) * picks + lax.rem(j, picks)) * 128
        gather(buf, lambda k: ids_ref[base + k], i * 128)

    def slot_chunk(buf, j, c):
        cs = lanes(c)
        x = gathered(buf, c * LANES, LANES)
        delta = time_all[cs, :] - nn(x, pick_last[...])
        x = jnp.concatenate([x, cos_rows(delta, high_row, low_row).astype(bf16)], 1)
        x_all[j, cs, :] = x
        kv = nt(wkv_ref[...], x).astype(bf16)
        if keep_kv:
            kv_all[j, :, cs] = kv
        s0, s1 = heads.sums(kv[:rows].astype(f32) * queries[:, cs].astype(f32))
        live = valid_ref[lax.div(j, picks), pl.ds(lax.rem(j, picks), 1), cs] > 0
        score[j, 0:1, cs] = jnp.where(live, s0 * scale, mask_fill)
        score[j, 1:2, cs] = jnp.where(live, s1 * scale, mask_fill)

    def first_slot(i, unused):
        fetch(xs, 0, i)
        return unused

    lax.fori_loop(0, events // 128, first_slot, 0)

    def slot_pair(i, unused):
        for side, (now, later) in enumerate(((xs, xs2), (xs2, xs))):
            j = 2 * i + side
            ahead = jnp.minimum(j + 1, slots - 1)
            for c in range(chunks):
                for block in range(LANES // 128):
                    fetch(later, ahead, c * (LANES // 128) + block)
                slot_chunk(now, j, c)
        return unused

    lax.fori_loop(0, slots // 2, slot_pair, 0)

    def soft_body(c, unused):
        cs = lanes(c, 128)
        s = score[:, 0:2, cs]
        top = jnp.max(s, 0, keepdims=True)
        p = jnp.where(s > 0.5 * mask_fill, jnp.exp(s - top), 0.0)
        score[:, 0:2, cs] = p / jnp.sum(p, 0, keepdims=True)
        return unused

    lax.fori_loop(0, events // 128, soft_body, 0)

    def kv_of(j, cs, part):
        if keep_kv:
            return kv_all[j, part, cs]
        return nt(wkv_ref[part, :], x_all[j, cs, :]).astype(bf16)

    def att_body(c, unused):
        cs = lanes(c, 256)
        total = jnp.zeros((rows, 256), f32)
        for j in range(slots):
            v = kv_of(j, cs, slice(rows, 2 * rows)).astype(f32)
            total = total + heads.scale(v, score[j, 0:1, cs], score[j, 1:2, cs])
        attended[:, cs] = total
        att_low[:, cs] = total.astype(bf16)
        return unused

    lax.fori_loop(0, events // 256, att_body, 0)

    def out_body(c, unused):
        cs = lanes(c)
        stage[0:width, :] = nn(w("s1t"), att_low[:, cs])[0:width]
        stage[width : 2 * width, :] = fresh_low[:, cs].astype(f32)[0:width]
        x = stage[0 : 2 * rows, :].astype(bf16)
        x_out[:, cs] = x
        pre = nn(wout_ref[...], x)
        pre_out[:, cs] = pre
        hid = (pre * jax.nn.sigmoid(pre)).astype(bf16)
        hid_out[:, cs] = hid
        e = nn(w("s2t"), hid).astype(bf16)
        emb[:, cs] = e
        emb_rows[cs, :] = nt(eye_ref[...], e).astype(bf16)
        return unused

    lax.fori_loop(0, chunks, out_body, 0, unroll=4)

    def row_init(c, unused):
        cs = lanes(c)
        rows_ref[0:1, cs] = jnp.full((1, LANES), mask_fill, f32)
        rows_ref[1:3, cs] = jnp.zeros((2, LANES), f32)
        acc_a[:, cs] = jnp.zeros((rows, LANES), f32)
        return unused

    lax.fori_loop(0, chunks, row_init, 0)

    def dest_of(o):
        at = pl.multiple_of(o * cand_width, cand_width)
        return dest_rows[pl.ds(at, cand_width), :]

    def lse_block(i, unused):
        for side in range(2):
            o = 2 * i + side
            dest = nn(dest_of(o), wd_ref[...]).astype(bf16)
            for c in range(events // 512):
                cs = lanes(c, 512)
                logits = nn(dest, emb[:, cs])
                old = rows_ref[0:1, cs]
                top = jnp.maximum(old, jnp.max(logits, 0, keepdims=True))
                rows_ref[0:1, cs] = top
                rows_ref[1:2, cs] = rows_ref[1:2, cs] * jnp.exp(old - top) + jnp.sum(
                    jnp.exp(logits - top), 0, keepdims=True
                )
                hit = lax.broadcasted_iota(jnp.int32, logits.shape, 0) == target_ref[:, cs] - o * cand_width
                rows_ref[2:3, cs] = rows_ref[2:3, cs] + jnp.sum(jnp.where(hit, logits, 0.0), 0, keepdims=True)
        return unused

    lax.fori_loop(0, owners // 2, lse_block, 0)

    mask_row = mask_ref[...].astype(f32)
    log_sum = rows_ref[0:1, :] + jnp.log(rows_ref[1:2, :])
    rows_ref[3:4, :] = log_sum
    rows_ref[4:5, :] = mask_row / jnp.broadcast_to(pos_ref[0:1, 0:1], mask_row.shape)
    loss = jnp.sum(mask_row * (log_sum - rows_ref[2:3, :]), 1, keepdims=True)
    grad_ref[layout.loss : layout.loss + 8, :] = jnp.broadcast_to(loss, (8, 128))

    def back_block(o, grad_dest_w):
        block = dest_of(o)
        dest = nn(block, wd_ref[...]).astype(bf16)
        dest_t = nt(wdt_ref[...], block).astype(bf16)
        block_t = nt(eye_ref[...], block).astype(bf16)

        def chunk(c, unused):
            cs = lanes(c)
            logits = nn(dest, emb[:, cs])
            coeff = rows_ref[4:5, cs]
            hit = lax.broadcasted_iota(jnp.int32, logits.shape, 0) == target_ref[:, cs] - o * cand_width
            grad = jnp.exp(logits - rows_ref[3:4, cs]) - jnp.where(hit, 1.0, 0.0)
            grad = (grad * coeff).astype(bf16)
            slab[0:cand_width, cs] = grad
            return unused

        lax.fori_loop(0, chunks, chunk, 0, unroll=True)
        acc_a[...] += nn(dest_t, slab[0:cand_width, :])
        grad_dest = nn(slab[0:cand_width, :], emb_rows[...]).astype(bf16)
        return grad_dest_w + nn(block_t, grad_dest)[:rows]

    grad_dest_w = lax.fori_loop(0, owners, back_block, jnp.zeros((rows, rows), f32))
    layout.put(grad_ref, "square3", grad_dest_w)

    r0, r1, r2 = slice(0, rows), slice(rows, 2 * rows), slice(2 * rows, 3 * rows)

    def out_back(c, unused):
        cs = lanes(c)
        ge = acc_a[:, cs].astype(bf16)
        slab[r0, cs] = ge
        pre = pre_out[:, cs]
        sig = jax.nn.sigmoid(pre)
        gp = (nn(w("s2"), ge) * (sig * (1.0 + pre * (1.0 - sig)))).astype(bf16)
        slab[r1, cs] = gp
        gm = nn(w("oa"), gp).astype(bf16)
        slab[r2, cs] = gm
        acc_a[:, cs] = nn(w("ob"), gp)
        ga = nn(w("s1"), gm).astype(bf16)
        grad_att[:, cs] = ga
        d0, d1 = heads.sums(ga.astype(f32) * attended[:, cs])
        rows_ref[5:6, cs] = d0
        rows_ref[6:7, cs] = d1
        return unused

    lax.fori_loop(0, chunks, out_back, 0, unroll=4)
    layout.put(grad_ref, "square2", nt(hid_out[...], slab[r0, :]))
    layout.put(grad_ref, "out", nt(slab[r1, :], x_out[...]))
    layout.put(grad_ref, "square1", nt(att_low[...], slab[r2, :]))

    attended[...] = jnp.zeros_like(attended)
    gkv_m[...] = jnp.zeros_like(gkv_m)

    def slot_back(i, unused):
        for side in range(2):
            j = 2 * i + side
            for c in range(events // 256):
                cs = lanes(c, 256)
                kv = kv_of(j, cs, slice(0, 2 * rows)).astype(f32)
                ga = grad_att[:, cs].astype(f32)
                p0, p1 = score[j, 0:1, cs], score[j, 1:2, cs]
                g0, g1 = heads.sums(ga * kv[rows:])
                g0 = p0 * (g0 - rows_ref[5:6, cs]) * scale
                g1 = p1 * (g1 - rows_ref[6:7, cs]) * scale
                attended[:, cs] += heads.scale(kv[:rows], g0, g1)
                gslab[side, 0:rows, cs] = heads.scale(queries[:, cs].astype(f32), g0, g1).astype(bf16)
                gslab[side, rows:2*rows, cs] = heads.scale(ga, p0, p1).astype(bf16)
            both = gslab[side, 0 : 2 * rows, :]
            gkv_m[...] += nn(both, x_all[j])
        return unused

    lax.fori_loop(0, slots // 2, slot_back, 0)
    gkv = gkv_m[...].T
    both = [jnp.concatenate([g[:, :width], g[:, rows : rows + width]], 1)
            for g in (gkv[:width], gkv[256 : 256 + time_width])]
    layout.put(grad_ref, "kv", jnp.concatenate(both, 0))

    for copy in loads:
        copy.wait()
    def gru_back(c, unused):
        cs = lanes(c)
        gq = attended[:, cs].astype(bf16)
        slab[r0, cs] = gq
        gf = acc_a[:, cs] + nn(w("s0"), gq)
        u, cand, r = update[:, cs], cand_act[:, cs], reset_gate[:, cs]
        act = gf * (1.0 - u) * (1.0 - cand * cand)
        gr = (act * gate_n[:, cs] * r * (1.0 - r)).astype(bf16)
        gu = (gf * (mem_src[:, cs] - cand) * u * (1.0 - u)).astype(bf16)
        gn = act.astype(bf16)
        gh = (act * r).astype(bf16)
        slab[r1, cs] = gr
        slab[r2, cs] = gu
        x_out[0:rows, cs] = gn
        hid_out[:, cs] = gh
        pre = pre_msg[:, cs]
        sig = jax.nn.sigmoid(pre)
        back = nn(w("g0r_back"), gr) + nn(w("g0z_back"), gu) + nn(w("g0n_back"), gn)
        att_low[:, cs] = (back * (sig * (1.0 + pre * (1.0 - sig)))).astype(bf16)
        return unused

    lax.fori_loop(0, chunks, gru_back, 0, unroll=4)
    layout.put(grad_ref, "square0", nt(fresh_low[...], slab[r0, :]))
    for index, (left, last) in enumerate(((hidden, x_out[0:rows, :]), (mem_low, hid_out[...]))):
        left = left[...]
        parts = [nt(left, slab[r1, :]), nt(left, slab[r2, :]), nt(left, last)]
        layout.put(grad_ref, f"gru{index}", jnp.concatenate([p[:, :width] for p in parts], 1))
    layout.put(grad_ref, "msg", nt(att_low[...], x_msg[...]))


def main(layout, keep_kv, width, head_dim, cand_width, args):
    events = args[4].shape[1]
    slots = args[7].shape[0] * args[7].shape[1]
    late = args[16:]
    rows = pad_to(width, 16)
    cands = args[1].shape[0]
    smem = pl.BlockSpec(memory_space=pltpu.SMEM)
    vmem = pl.BlockSpec(memory_space=pltpu.VMEM)
    hbm = pl.BlockSpec(memory_space=pl.ANY)
    low = lambda *shape: pltpu.VMEM(shape, bf16)
    full = lambda *shape: pltpu.VMEM(shape, f32)
    return pl.pallas_call(
        partial(main_kernel, (width, head_dim, keep_kv, cand_width, layout)),
        out_shape=jax.ShapeDtypeStruct((layout.total, 128), f32),
        in_specs=[smem, smem] + [vmem] * 14 + [hbm] * len(late),
        out_specs=vmem,
        scratch_shapes=[pltpu.VMEM(x.shape, x.dtype) for x in late]
        + [
            full(2 * events + 64, 128),
            full(2 * events + 64, 128),
            low(slots, events, 384),
            full(events, 128),
            low(slots if keep_kv else 1, 2 * rows if keep_kv else 16, events),
            full(slots, 8, events),
            low(cands, 256),
            low(max(3 * rows, cand_width), events),
            low(256, 256),
            low(2, max(2 * rows, cand_width), events),
            full(2 * rows, LANES),
            low(rows, events),
            low(2 * rows, events),
            low(rows, events),
            low(rows, events),
            low(events, rows),
            full(rows, events),
            full(rows, events),
            full(rows, events),
            low(rows, events),
            full(2 * rows, 384),
            low(256, 128),
            full(8, events),
            pltpu.SemaphoreType.DMA((len(late),)),
        ],
        compiler_params=pltpu.CompilerParams(vmem_limit_bytes=63 * 2**20),
        name="train",
    )(*args)


def reduce_kernel(own, batch, streams, grad_ref, out_ref, acc, recv, local_sem, send_sem, recv_sem):
    place = {"own": lax.axis_index("own"), "batch": lax.axis_index("batch")}

    digits = [lax.div(place["own"], 1 << b) % 2 for b in range(own.bit_length() - 1)]

    def parts(bits):
        if not bits:
            return batch, place["batch"]
        return 1 << len(bits), sum(digits[b] * (1 << i) for i, b in enumerate(bits))

    def peers(bits):
        if not bits:
            for d in range(1, batch):
                there = lax.rem(place["batch"] + d, batch)
                yield (there, place["own"]), there
            return
        for pattern in range(1, 1 << len(bits)):
            there, at = place["own"], 0
            for i, b in enumerate(bits):
                digit = digits[b]
                if pattern >> i & 1:
                    there, digit = there + (1 << b) * (1 - 2 * digit), 1 - digit
                at = at + digit * (1 << i)
            yield (place["batch"], there), at

    load = pltpu.make_async_copy(grad_ref, acc, local_sem)
    load.start()
    barrier = pltpu.get_barrier_semaphore()
    devices = {}
    for order in [order for start, size, order in streams]:
        for bits in order:
            devices.setdefault(tuple(sorted(bits)), [device for device, there in peers(sorted(bits))])
    greeted = [device for bits in devices if all(set(bits) >= set(other) or not set(bits) & set(other) for other in devices)
               for device in devices[bits]]
    for device in greeted:
        pl.semaphore_signal(barrier, inc=1, device_id=device, device_id_type=MESH)
    pl.semaphore_wait(barrier, len(greeted))
    load.wait()

    sent = []
    longest = max(len(order) for start, size, order in streams)

    class Stream:
        def __init__(self, index, start, size, order):
            self.index, self.base, self.size, self.inner, self.order = index, start, size, start, order
            self.copies = []
            self.slots = [0]
            for bits in order:
                self.slots.append(self.slots[-1] + parts(bits)[0] - 1)

        def copy(self, source, target, peer, slot):
            copy = pltpu.make_async_remote_copy(
                src_ref=source, dst_ref=target,
                send_sem=send_sem.at[self.index, slot], recv_sem=recv_sem.at[self.index, slot],
                device_id=peer, device_id_type=MESH,
            )
            copy.start()
            self.copies.append(copy)
            sent.append(copy)

        def scatter(self, step):
            count, mine = parts(self.order[step])
            piece = self.size // count
            for d, (peer, theirs) in enumerate(peers(self.order[step]), 1):
                away = pl.multiple_of(self.base + theirs * piece, 8)
                self.copy(
                    acc.at[pl.ds(away, piece), :], recv.at[pl.ds(self.inner + (d - 1) * piece, piece), :],
                    peer, self.slots[step] + d - 1,
                )
            self.base = pl.multiple_of(self.base + mine * piece, 8)
            self.size = piece

        def add(self, step):
            target = out_ref if step == len(self.order) - 1 else acc
            part = pl.ds(self.base, self.size)
            total = acc[part, :]
            for copy in self.copies:
                copy.wait_recv()
                total = total + recv[pl.ds(self.inner, self.size), :]
                self.inner += self.size
            target[part, :] = total
            self.copies = []

        def gather(self, step):
            count, mine = parts(self.order[step])
            part = pl.ds(self.base, self.size)
            for d, (peer, theirs) in enumerate(peers(self.order[step]), 1):
                self.copy(out_ref.at[part, :], out_ref.at[part, :], peer, self.slots[-1] + self.slots[step] + d - 1)
            self.base = pl.multiple_of(self.base - mine * self.size, 8)
            self.size *= count

        def gathered(self):
            for copy in self.copies:
                copy.wait_recv()
            self.copies = []

    flows = [Stream(index, *stream) for index, stream in enumerate(streams)]
    for step in range(2 * longest + 1):
        for flow in flows:
            rounds = len(flow.order)
            if 0 < step <= rounds:
                flow.add(step - 1)
            elif rounds < step <= 2 * rounds:
                flow.gathered()
            if step < rounds:
                flow.scatter(step)
            elif step < 2 * rounds:
                flow.gather(2 * rounds - 1 - step)
    for copy in sent:
        copy.wait_send()


def reduce_all(own, batch, packed):
    total = packed.shape[0]
    own_bits = own.bit_length() - 1
    fold = 8 * own * batch
    core, xs, ys, zs = (0,), tuple(range(1, (own_bits + 1) // 2)), tuple(range((own_bits + 1) // 2, own_bits)), ()
    plan = ((6, (core, xs + ys, zs)), (3, (core, zs, xs + ys)), (6, (core, ys + xs, zs)), (3, (core, zs, ys + xs)))
    streams = []
    start = 0
    blocks = total // fold
    shares = sum(share for share, order in plan)
    for index, (share, order) in enumerate(plan):
        size = total - start if index == len(plan) - 1 else blocks * share // shares * fold
        if size:
            streams.append((start, size, order))
        start += size
    count = 2 * (own * batch)
    return pl.pallas_call(
        partial(reduce_kernel, own, batch, streams),
        out_shape=jax.ShapeDtypeStruct(packed.shape, f32),
        in_specs=[pl.BlockSpec(memory_space=pl.ANY)],
        out_specs=pl.BlockSpec(memory_space=pltpu.VMEM),
        scratch_shapes=[
            pltpu.VMEM(packed.shape, f32),
            pltpu.VMEM(packed.shape, f32),
            pltpu.SemaphoreType.DMA,
            pltpu.SemaphoreType.DMA((len(streams), count)),
            pltpu.SemaphoreType.DMA((len(streams), count)),
        ],
        compiler_params=pltpu.CompilerParams(
            collective_id=2, has_side_effects=True, vmem_limit_bytes=63 * 2**20
        ),
        name="reduce",
    )(packed)


def update_kernel(layout, step_rate, grad_ref, pos_ref, *refs):
    sources, targets, loss_ref, count_ref = refs[:15], refs[15:30], refs[30], refs[31]
    held, laid = refs[32:47], refs[47:49]
    in_sem, out_sem = refs[49:]
    loss_ref[...] = grad_ref[layout.loss : layout.loss + 1, 0:1]
    count_ref[...] = pos_ref[0:1, 0:1]
    arrive = [pltpu.make_async_copy(sources[i], held[i], in_sem.at[i]) for i in range(15)]
    leave = [pltpu.make_async_copy(held[i], targets[(i + 5) % 10 if i < 10 else i], out_sem.at[i]) for i in range(15)]
    order = (1, 2, 0, 3, 4)
    for index in order:
        for kind in range(3):
            arrive[5 * kind + index].start()

    for ref, name, parts in ((laid[0], "gru", 2), (laid[1], "square", 4)):
        for part in range(parts):
            for columns, gradient in layout.tiles(grad_ref, f"{name}{part}"):
                ref[:, part, columns] = gradient

    def step(index, at, gradient):
        weights, moments, averages = (held[5 * kind + index] for kind in range(3))
        moment = mu_coef * moments[at] + gradient
        weight = weights[at] - step_rate * (gradient + mu_coef * moment)
        moments[at] = moment
        weights[at] = weight
        averages[at] = (1.0 - avg_coef) * averages[at] + avg_coef * weight

    for index in order:
        for kind in range(3):
            arrive[5 * kind + index].wait()
        if index in (1, 2):
            step(index, slice(None), laid[index - 1][...])
        else:
            for columns, gradient in layout.tiles(grad_ref, ("msg", "", "", "kv", "out")[index]):
                step(index, (slice(None), columns), gradient)
        for kind in range(3):
            leave[5 * kind + index].start()
    for copy in leave:
        copy.wait()


def update_all(layout, step_rate, packed, positives, params):
    vmem = pl.BlockSpec(memory_space=pltpu.VMEM)
    hbm = pl.BlockSpec(memory_space=pl.ANY)
    buffers = [pltpu.VMEM(p.shape, f32) for p in params]
    return pl.pallas_call(
        partial(update_kernel, layout, step_rate),
        out_shape=tuple(jax.ShapeDtypeStruct(p.shape, f32) for p in params[5:10] + params[:5] + params[10:])
        + (jax.ShapeDtypeStruct((1, 1), f32),) * 2,
        in_specs=[vmem] * 2 + [hbm] * 15,
        out_specs=(hbm,) * 15 + (vmem,) * 2,
        scratch_shapes=buffers + buffers[1:3] + [pltpu.SemaphoreType.DMA((15,))] * 2,
        compiler_params=pltpu.CompilerParams(vmem_limit_bytes=63 * 2**20),
        name="update",
    )(packed, positives, *params)


def turned(arrays):
    msg, gru, square, kv, out = arrays
    return (msg.T, gru.transpose(1, 0, 2), square.transpose(1, 0, 2), kv, out.T)


def local(
    memory, last_update, src_local, edge_feat, event_time, nbr_owner, nbr_ids, nbr_mask, event_mask,
    dest_local, target, w_msg, w_gru, w_square, w_key_value, w_output,
    mom_msg, mom_gru, mom_square, mom_key_value, mom_output,
    avg_msg, avg_gru, avg_square, avg_key_value, avg_output,
):
    own = lax.axis_size("own")
    batch = lax.axis_size("batch")
    events, edge = edge_feat.shape
    nodes, width = memory.shape
    head_dim = width // HEADS
    time_width = w_key_value.shape[0] - width
    columns = time_columns(time_width, 128)
    layout = Layout(
        width, w_msg.shape[0], w_output.shape[0], w_gru.shape[2], *w_key_value.shape, 8 * own * batch
    )
    weights = turned((w_msg, w_gru, w_square, w_key_value, w_output))
    time_row, mask_row, src_row, target_row = (x[None, :] for x in (event_time, event_mask, src_local, target))
    table, cand_ids, flat_ids, positives, newest, *handed = exchange(
        own, batch,
        (memory.T, last_update[None, :], dest_local[None, :], time_row, mask_row, src_row,
         nbr_owner.T, nbr_ids.transpose(2, 1, 0), jnp.asarray(columns)) + weights + (edge_feat.T,),
    )
    packed = main(
        layout, own * nodes <= 16384, width, head_dim, dest_local.shape[0],
        (flat_ids.reshape(-1), cand_ids.reshape(-1), positives, table, time_row, mask_row, target_row,
         nbr_mask.transpose(2, 1, 0), *handed[:5], jnp.asarray(columns.T[:8]), *handed[5:]),
    )
    summed = reduce_all(own, batch, packed)
    step_rate = rate_coef * math.sqrt(events * own * batch)
    *states, loss, count = update_all(
        layout, step_rate, summed, positives,
        weights
        + turned((mom_msg, mom_gru, mom_square, mom_key_value, mom_output))
        + turned((avg_msg, avg_gru, avg_square, avg_key_value, avg_output)),
    )
    states = [x for i in range(3) for x in turned(states[5 * i : 5 * i + 5])]
    return (loss.reshape(()), count.reshape(()), newest.reshape(-1), *states)


def solution(mesh):
    row = P(("batch", "own"))
    placed = (
        (P("own", None), P("own"), row, P(("batch", "own"), None), row, P(("batch", "own"), None))
        + (P(("batch", "own"), None, None),) * 2
        + (row,) * 3
        + (P(),) * 15
    )
    return jax.shard_map(
        local,
        mesh=mesh,
        in_specs=placed,
        out_specs=(P(), P(), P("own")) + (P(),) * 15,
        check_vma=False,
    )
```
